128 devices in a mesh: vol: 16 (over x, y), zone: 8 (over z, core).
Axes of the slice: x: 4, y: 4, z: 4, core: 2. Of those that a mesh axis runs over, the one named last changes fastest.
Arguments:
- load: float32 [3, 2048, 2048], P(None, 'vol', 'zone'), may hold values from -12 to 12
- support_stiffness: float32 [2048, 2048], P('vol', 'zone'), may hold values from 0.5 to 4
- plastic_flags: int32 [2048, 16], P('vol', 'zone'), may hold values 0 or 1
- owner_map: int32 [16, 8, 16], P('vol', 'zone'), may hold values from 0 to 7, as said below
- pattern: int32 [16, 8, 16, 3], P('vol', 'zone'), may hold values from 0 to 31, as said below
- active: int32 [16, 8, 16], P('vol', 'zone'), may hold values 0 or 1
- mortar: float32 [16, 8, 16, 3, 128, 128], P('vol', 'zone'), may hold values from -1 to 2
Outputs:
- displacement: float32 [3, 2048, 2048], P(None, 'vol', 'zone')
- residual: float32 [3, 2048, 2048], P(None, 'vol', 'zone')
The draws below stay inside these ranges and needn't reach their ends.
Inputs may be any that keep to these rules, and one draw needn't show every extreme that they name: owner_map[i, s, m] is the zone index of the owner, in vol group i, of surface block m of device (i, s). At most 4 blocks of one device go to one owner, and in each vol group some owner receives exactly 4 blocks from every device. pattern[i, z, r] names slots of owner z of vol group i, slot s * 4 + k being the k-th block (in increasing block index) that device s of the group sends to z. Every entry names a slot that holds a block, unless the owner receives none (then all are 0), and every slot that holds a block is named.
All inputs are finite; a program needn't handle non-finite values. No bound on the sum of `plastic_flags` or of `active` on one device may be relied on, other than what follows from the above.
Results may differ from the reference program's by a relative error of at most 0.005.
Values sent between devices are 32-bit elements; how exact they have to be, the bound alone decides.
A program may use at most 64 MiB of HBM per device.

```python
import math
import jax
import jax.numpy as jnp
from jax import lax

CX = 128
CY = 256
SROWS = 8
BLK = 128
NNZ = 3
KRY = 3
NEWTON = 2
NX = 2048
NY = 2048
SB = 16
CAP = 4
SLOTS = 32
MROWS = 16
N_VOL = 16
N_ZONE = 8


def shared_owners(key):
    key = jax.random.fold_in(key, 11)
    heavy_key, fill_key, order_key = jax.random.split(key, 3)
    heavy = jax.random.randint(heavy_key, (N_VOL,), 0, N_ZONE)
    listing = jnp.repeat(jnp.arange(N_ZONE - 1, dtype=jnp.int32), CAP)
    fill_keys = jax.random.split(fill_key, N_VOL * N_ZONE)
    mixed = jax.vmap(lambda single: jax.random.permutation(single, listing))(fill_keys)
    others = mixed.reshape(N_VOL, N_ZONE, -1)[:, :, :SB - CAP]
    others = others + (others >= heavy[:, None, None]).astype(jnp.int32)
    heavy_part = jnp.broadcast_to(heavy[:, None, None], (N_VOL, N_ZONE, CAP)).astype(jnp.int32)
    joined = jnp.concatenate([heavy_part, others.astype(jnp.int32)], axis=2).reshape(N_VOL * N_ZONE, SB)
    order_keys = jax.random.split(order_key, N_VOL * N_ZONE)
    shuffled = jax.vmap(lambda single, row_values: jax.random.permutation(single, row_values))(order_keys, joined)
    return shuffled.reshape(N_VOL, N_ZONE, SB).astype(jnp.int32)


def draw_owner_map(key, part):
    owners = shared_owners(key)
    return owners


def draw_pattern(key, part):
    owners = shared_owners(key)
    key = jax.random.fold_in(key, 7)
    dest_ids = jnp.arange(N_ZONE, dtype=jnp.int32)[None, :, None, None]
    counts = jnp.sum((owners[:, None, :, :] == dest_ids).astype(jnp.int32), axis=3)
    filled = (jnp.arange(CAP, dtype=jnp.int32)[None, None, None, :] < counts[..., None]).astype(jnp.int32)
    filled = filled.reshape(N_VOL, N_ZONE, SLOTS)
    order = jnp.argsort(1 - filled, axis=-1, stable=True).astype(jnp.int32)
    number = jnp.maximum(jnp.sum(filled, axis=-1), 1)[..., None]
    row_ids = jnp.arange(MROWS, dtype=jnp.int32)[None, None, :]
    first = jnp.take_along_axis(order, row_ids % number, axis=-1)
    second = jnp.take_along_axis(order, (row_ids + MROWS) % number, axis=-1)
    picks = jax.random.randint(key, (N_VOL, N_ZONE, MROWS * (NNZ - 2)), 0, number)
    rest = jnp.take_along_axis(order, picks, axis=-1).reshape(N_VOL, N_ZONE, MROWS, NNZ - 2)
    return jnp.concatenate([first[..., None], second[..., None], rest], axis=-1).astype(jnp.int32)


def draw_mortar(key, part):
    key = jax.random.fold_in(key, 5)
    diag_key, off_key = jax.random.split(key)
    shape = (N_VOL, N_ZONE, MROWS, NNZ, BLK, BLK)
    identity = (jnp.arange(BLK)[:, None] == jnp.arange(BLK)[None, :]).astype(jnp.float32)
    diagonal = jax.random.uniform(diag_key, shape[:-1], jnp.float32, 0.8, 1.2)
    spread = jnp.clip(jax.random.normal(off_key, shape, jnp.float32), -4.0, 4.0) * (0.5 / math.sqrt(BLK))
    return diagonal[..., None] * identity + spread * (1.0 - identity)


def draw_load(key, part):
    key = jax.random.fold_in(key, 1)
    rows_pos = jnp.arange(NX, dtype=jnp.float32)[None, :, None]
    rising = 1.0 + 2.0 * rows_pos / NX
    return rising * jnp.clip(jax.random.normal(key, (3, NX, NY), jnp.float32), -4.0, 4.0)


def place_ends(values, key, smallest, high):
    longest = values.shape.index(max(values.shape))
    spots = []
    for shift in (0, 1):
        where = [jax.random.randint(jax.random.fold_in(key, axis), (), 0, length) for axis, length in enumerate(values.shape)]
        where[longest] = (where[longest] + shift) % values.shape[longest]
        spots.append(tuple(where))
    return values.at[spots[0]].set(smallest).at[spots[1]].set(high)


def block_scale(own_key, shape, cuts, low, largest):
    loudness, own = 1.0, jax.random.fold_in(own_key, 6)
    for axis_at, blocks in cuts:
        draws = jnp.exp(jax.random.uniform(jax.random.fold_in(own, axis_at), (blocks,), jnp.float32, low / len(cuts), largest / len(cuts)))
        loudness = loudness * jnp.repeat(draws, shape[axis_at] // blocks).reshape([-1 if axis == axis_at else 1 for axis in range(len(shape))])
    return loudness


def setup_inputs(seed: int = 0) -> dict:
    splits = jax.random.split(jax.random.key(seed), 8)
    return {
        "load": draw_load(jax.random.fold_in(splits[7], 71), 0),
        "support_stiffness": jnp.clip(jnp.exp(math.log(4.0) - 2.0794415 * jax.random.uniform(splits[1], (NX, NY), jnp.float32) ** block_scale(splits[1], (NX, NY), ((0, 16), (1, 8)), -0.2, 0.2)), 0.5, 4.0),
        "plastic_flags": place_ends((jax.random.randint(splits[2], (NX, NY // BLK), 0, 2) < 1).astype(jnp.int32), jax.random.fold_in(splits[2], 1), 0, 1),
        "owner_map": draw_owner_map(jax.random.fold_in(splits[7], 71), 0),
        "pattern": draw_pattern(jax.random.fold_in(splits[7], 71), 0),
        "active": place_ends((jax.random.randint(splits[5], (N_VOL, N_ZONE, MROWS), 0, 4) < 3).astype(jnp.int32), jax.random.fold_in(splits[5], 1), 0, 1),
        "mortar": draw_mortar(jax.random.fold_in(splits[7], 71), 0),
    }


yield_scale = 0.5
penalty = 2.0
plastic_hardening = 0.2


def grid_part(grid_values):
    padded = jnp.pad(grid_values, ((0, 0), (1, 1), (1, 1)))
    beside = padded[:, 2:, 1:-1] + padded[:, :-2, 1:-1] + padded[:, 1:-1, 2:] + padded[:, 1:-1, :-2]
    return 4.0 * grid_values - beside


def block_ranks(owners):
    number = owners.shape[-1]
    matching = owners[..., :, None] == owners[..., None, :]
    earlier = jnp.arange(number)[:, None] < jnp.arange(number)[None, :]
    return jnp.sum((matching & earlier).astype(jnp.int32), axis=-2)


def mortar_forces(slot_values, slot_links, switches, couplings):
    orient = jnp.where(jnp.arange(slot_links.shape[1]) == 0, 1.0, -1.0).astype(jnp.float32)
    picked = slot_values[slot_links] * orient[None, :, None, None]
    gap_values = jnp.einsum("rkij,rkcj->rci", couplings, picked, precision=lax.Precision.HIGHEST)
    multipliers = penalty * switches.astype(jnp.float32)[:, None, None] * gap_values
    pushed = jnp.einsum("rkij,rci->rkcj", couplings, multipliers, precision=lax.Precision.HIGHEST)
    pushed = pushed * orient[None, :, None, None]
    flattened = pushed.reshape(-1, pushed.shape[2], pushed.shape[3])
    return jax.ops.segment_sum(flattened, slot_links.reshape(-1), num_segments=slot_values.shape[0])


def reference(load, support_stiffness, plastic_flags, owner_map, pattern, active, mortar):
    hardness = jnp.repeat(jnp.where(plastic_flags == 1, plastic_hardening, 1.0), BLK, axis=1).astype(jnp.float32)
    block_order = block_ranks(owner_map)
    target = (jnp.arange(N_ZONE, dtype=jnp.int32)[None, :, None] * CAP + block_order).astype(jnp.int32)
    vol_ids = jnp.arange(N_VOL, dtype=jnp.int32)[:, None, None]
    column_blocks = CY // BLK

    def contact(grid_values):
        parts = grid_values.reshape(3, N_VOL, CX, N_ZONE, column_blocks, BLK)[:, :, :SROWS]
        blocks = parts.transpose(1, 3, 2, 4, 0, 5).reshape(N_VOL, N_ZONE, SB, 3, BLK)
        slot_values = jnp.zeros((N_VOL, N_ZONE, SLOTS, 3, BLK), jnp.float32)
        slot_values = slot_values.at[vol_ids, owner_map, target].set(blocks)
        forces = jax.vmap(jax.vmap(mortar_forces))(slot_values, pattern, active, mortar)
        returned = forces[vol_ids, owner_map, target]
        returned = returned.reshape(N_VOL, N_ZONE, SROWS, column_blocks, 3, BLK).transpose(4, 0, 2, 1, 3, 5)
        returned = jnp.pad(returned, ((0, 0), (0, 0), (0, CX - SROWS), (0, 0), (0, 0), (0, 0)))
        return returned.reshape(3, NX, NY)

    def residual_of(moved):
        material = support_stiffness * (hardness * moved + (1.0 - hardness) * yield_scale * jnp.tanh(moved / yield_scale))
        return grid_part(moved) + material + contact(moved) - load

    displacement = jnp.zeros_like(load)
    for newton_step in range(NEWTON):
        saturation = jnp.tanh(displacement / yield_scale)
        onsite = support_stiffness * (hardness + (1.0 - hardness) * (1.0 - saturation * saturation))
        update = jnp.zeros_like(load)
        remainder = -residual_of(displacement)
        direction = remainder
        norm_now = jnp.sum(remainder * remainder)
        for krylov_step in range(KRY):
            applied = grid_part(direction) + onsite * direction + contact(direction)
            step_length = norm_now / jnp.sum(direction * applied)
            update = update + step_length * direction
            remainder = remainder - step_length * applied
            norm_next = jnp.sum(remainder * remainder)
            direction = remainder + (norm_next / norm_now) * direction
            norm_now = norm_next
        displacement = displacement + update
    return displacement, residual_of(displacement)
```

```python
import functools

import jax
import jax.numpy as jnp
from jax import lax
from jax.experimental import pallas as pl
from jax.experimental.pallas import tpu as pltpu
from jax.sharding import PartitionSpec as P

SROWS = 8
BLK = 128
NNZ = 3
CAP = 4
KRY = 3
NEWTON = 2
STEPS = KRY * NEWTON
PAD = 8

yield_scale = 0.5
penalty = 2.0
plastic_hardening = 0.2

F32 = jnp.float32
BF16 = jnp.bfloat16


def kernel(
    n_vol, n_zone,
    load_ref, stiff_ref, flags_ref, owner_ref, pattern_ref, active_ref, mortar_ref,
    u_ref, res_ref,
    x_ref, p_ref, t_ref, l_ref, d_ref, lu_ref, hard_ref,
    mort_ref, mhi_ref, mlo_ref, spread_ref, push_ref,
    surf_ref, block_ref, back_ref,
    pack_tab, unpack_tab,
    fsend, frecv, bsend, brecv, rsend, rrecv, csend, crecv, zsend, zrecv, vsend, vrecv,
    msem, fs, fr, bs, br, rs, rr, cs, cr, zs, zr, vs, vr,
):
    comps, height = load_ref.shape[0], load_ref.shape[1]
    halves = load_ref.shape[2] // BLK
    groups = height // 8
    blocks = SROWS * halves
    rows = active_ref.shape[2]
    zone = lax.axis_index("zone")
    vol = lax.axis_index("vol")

    mortar_copy = pltpu.make_async_copy(mortar_ref.at[0, 0], mort_ref, msem)
    mortar_copy.start()

    def at_zone(step):
        return lax.rem(zone + step, n_zone)

    def at_vol(step):
        return lax.rem(vol + step, n_vol)

    barrier = pltpu.get_barrier_semaphore()
    for step in range(1, n_zone):
        pl.semaphore_signal(barrier, inc=1, device_id={"zone": at_zone(step)})
    for step in range(1, n_vol):
        pl.semaphore_signal(barrier, inc=1, device_id={"vol": at_vol(step)})

    owners = [owner_ref[0, 0, m] for m in range(blocks)]
    weights = []
    for m in range(blocks):
        weight, rank = jnp.int32(1), jnp.int32(0)
        for e in range(m):
            same = owners[e] == owners[m]
            weight = jnp.where(same, weight * 32, weight)
            rank = rank + jnp.where(same, 1, 0)
        weights.append(weight)
        unpack_tab[m] = owners[m] * CAP + rank
    for z in range(n_zone):
        code = jnp.int32(0)
        for m in range(blocks):
            code = code + jnp.where(owners[m] == z, weights[m] * (blocks + m), 0)
        for k in range(CAP):
            field = lax.shift_right_logical(code, 5 * k) & 31
            pack_tab[z * CAP + k] = jnp.where(field >= blocks, field - blocks, blocks)

    sub = lax.broadcasted_iota(jnp.int32, (8, BLK), 0)
    lane = lax.broadcasted_iota(jnp.int32, (8, BLK), 1)

    wide = rows * NNZ * 8
    link_lane = lax.broadcasted_iota(jnp.int32, (1, wide), 1)
    links = jnp.zeros((1, wide), jnp.int32)
    for r in range(rows):
        for k in range(NNZ):
            links = jnp.where(link_lane // 8 == r * NNZ + k, pattern_ref[0, 0, r, k], links)
    out_row = lax.broadcasted_iota(jnp.int32, (n_zone * CAP * 4, wide), 0)
    out_lane = lax.broadcasted_iota(jnp.int32, (n_zone * CAP * 4, wide), 1)
    hit = (out_row // 4 == links) & (lax.rem(out_row, 4) == lax.rem(out_lane, 4))
    spread_ref[...] = jnp.where(hit, 1.0, 0.0).astype(BF16)

    surf_ref[...] = jnp.zeros_like(surf_ref)
    block_ref[blocks] = jnp.zeros((8, BLK), F32)
    back_ref[...] = jnp.zeros_like(back_ref)
    rsend[...] = jnp.zeros_like(rsend)
    u_ref[...] = jnp.zeros_like(u_ref)
    lu_ref[...] = jnp.zeros_like(lu_ref)
    p_ref[...] = jnp.zeros_like(p_ref)
    t_ref[...] = jnp.zeros_like(t_ref)
    for c in range(comps):
        for b in range(halves):
            x_ref[c, b, 0:PAD, :] = jnp.zeros((PAD, BLK), F32)
            x_ref[c, b, PAD + height:, :] = jnp.zeros((PAD, BLK), F32)
            x_ref[c, b, PAD:PAD + height, :] = load_ref[c, :, b * BLK:(b + 1) * BLK]
            d_ref[c, b] = stiff_ref[:, b * BLK:(b + 1) * BLK]
    for b in range(halves):
        flag = jnp.broadcast_to(flags_ref[:, b:b + 1], (height, BLK))
        hard_ref[b] = jnp.where(flag == 1, plastic_hardening, 1.0).astype(F32)

    pl.semaphore_wait(barrier, n_zone - 1 + n_vol - 1)

    def remote(src, dst, send, recv, target):
        return pltpu.make_async_remote_copy(
            src_ref=src, dst_ref=dst, send_sem=send, recv_sem=recv, device_id=target
        )

    def await_bytes(ref, sem):
        pltpu.make_async_copy(ref, ref, sem).wait()

    def slots_of(z):
        return pl.ds(z * CAP, CAP)

    def group_rows(g):
        return pl.ds(pl.multiple_of(PAD + g * 8, 8), 8)

    def tile_rows(g):
        return pl.ds(pl.multiple_of(g * 8, 8), 8)

    def fold(total):
        return jnp.sum(total, axis=0, keepdims=True)

    def hardened(b, g):
        return stiff_ref[tile_rows(g), b * BLK:(b + 1) * BLK], hard_ref[b, tile_rows(g), :]

    def iteration(it, carry):
        gamma_old, step_old, pq_old, cross = carry
        first = lax.rem(it, KRY) == 0

        for c in range(comps):
            for b in range(halves):
                surf_ref[pl.ds(b * 8 + c, SROWS, stride=8 * halves), :] = x_ref[c, b, PAD:PAD + SROWS, :]

        for m in range(blocks):
            block_ref[m] = surf_ref[m * 8:m * 8 + 8, :]

        def packed(z, k):
            return block_ref[pack_tab[z * CAP + k]][0:4]

        for step in range(1, n_zone):
            z = at_zone(step)
            for k in range(CAP):
                fsend[it, step, k] = packed(z, k)
            remote(
                fsend.at[it, step], frecv.at[it, slots_of(zone)], fs.at[it], fr.at[it], {"zone": z}
            ).start()
        for k in range(CAP):
            frecv[it, zone * CAP + k] = packed(zone, k)

        for c in range(comps):
            for b in range(halves):
                j = c * halves + b
                rsend[it, 0, j:j + 1, :] = x_ref[c, b, PAD:PAD + 1, :]
                rsend[it, 1, j:j + 1, :] = x_ref[c, b, PAD + height - 1:PAD + height, :]
        remote(rsend.at[it, 0], rrecv.at[it, 1], rs.at[it], rr.at[it], {"vol": at_vol(n_vol - 1)}).start()
        remote(rsend.at[it, 1], rrecv.at[it, 0], rs.at[it], rr.at[it], {"vol": at_vol(1)}).start()
        for side, b, column in ((0, 0, 0), (1, halves - 1, BLK - 1)):
            strip = jnp.zeros((8, BLK), F32)
            for c in range(comps):
                for g in range(groups):
                    tile = x_ref[c, b, PAD + g * 8:PAD + g * 8 + 8, :]
                    strip = jnp.where(
                        lane == c * groups + g, jnp.broadcast_to(tile[:, column:column + 1], (8, BLK)), strip
                    )
            csend[it, side] = strip
        remote(csend.at[it, 0], crecv.at[it, 1], cs.at[it], cr.at[it], {"zone": at_zone(n_zone - 1)}).start()
        remote(csend.at[it, 1], crecv.at[it, 0], cs.at[it], cr.at[it], {"zone": at_zone(1)}).start()

        def inner(g, sums):
            gamma, delta = sums
            for c in range(comps):
                tiles = [x_ref[c, b, group_rows(g), :] for b in range(halves)]
                to_right = [pltpu.roll(tile, 1, axis=1) for tile in tiles]
                to_left = [pltpu.roll(tile, BLK - 1, axis=1) for tile in tiles]
                for b in range(halves):
                    x = tiles[b]
                    before = to_right[b - 1] if b > 0 else jnp.zeros_like(x)
                    after = to_left[b + 1] if b < halves - 1 else jnp.zeros_like(x)
                    left = jnp.where(lane == 0, before, to_right[b])
                    right = jnp.where(lane == BLK - 1, after, to_left[b])
                    over = x_ref[c, b, pl.ds(PAD + g * 8 - 1, 8), :]
                    under = x_ref[c, b, pl.ds(PAD + g * 8 + 1, 8), :]
                    image = 4.0 * x - (over + under + left + right)
                    l_ref[c, b, tile_rows(g), :] = image
                    gamma = gamma + x * x
                    delta = delta + x * (image + d_ref[c, b, tile_rows(g), :] * x)
            return gamma, delta

        zero = jnp.zeros((8, BLK), F32)
        gamma, delta = lax.fori_loop(0, groups, inner, (zero, zero), unroll=2)

        await_bytes(rrecv.at[it], rr.at[it])
        await_bytes(crecv.at[it], cr.at[it])
        over = jnp.where(vol == 0, 0.0, rrecv[it, 0])
        under = jnp.where(vol == n_vol - 1, 0.0, rrecv[it, 1])
        left = jnp.where(zone == 0, 0.0, crecv[it, 0])
        right = jnp.where(zone == n_zone - 1, 0.0, crecv[it, 1])
        delta = delta - (rsend[it, 0] * over + rsend[it, 1] * under)
        delta = delta - (csend[it, 0] * left + csend[it, 1] * right)

        @pl.when(it == 0)
        def _():
            mortar_copy.wait()

            def split(r, _):
                for k in range(NNZ):
                    piece = mort_ref[r, k] if k == 0 else -mort_ref[r, k]
                    high = piece.astype(BF16)
                    mhi_ref[r, :, k * BLK:(k + 1) * BLK] = high
                    mlo_ref[r, :, k * BLK:(k + 1) * BLK] = (piece - high.astype(F32)).astype(BF16)
                return 0

            lax.fori_loop(0, rows, split, 0)

        await_bytes(frecv.at[it, 0:(n_zone - 1) * CAP], fr.at[it])

        upper = lax.broadcasted_iota(jnp.int32, (8, NNZ * BLK), 0) < 4
        contract_last = (((1,), (1,)), ((), ()))

        def split_rows(both, mask):
            high = both.astype(BF16).astype(F32)
            return jnp.where(mask, high, both - high).astype(BF16)

        energy = zero
        pushes = []
        for r in range(rows):
            picked = jnp.concatenate([frecv[it, pattern_ref[0, 0, r, k]] for k in range(NNZ)], axis=1)
            picked = split_rows(jnp.concatenate([picked, picked], axis=0), upper)
            gap = lax.dot_general(picked, mhi_ref[r], contract_last, preferred_element_type=F32)
            gap = gap + lax.dot_general(picked, mlo_ref[r], contract_last, preferred_element_type=F32)
            gap = gap + pltpu.roll(gap, 4, axis=0)
            multiplier = (penalty * active_ref[0, 0, r].astype(F32)) * gap
            energy = energy + multiplier * gap
            pushes.append(multiplier)
        delta = delta + 0.5 * energy

        local = jnp.where(sub == 0, fold(gamma), jnp.where(sub == 1, fold(delta), fold(cross)))
        zsend[it] = local[0:4]
        zrecv[it, zone] = local[0:4]
        for step in range(1, n_zone):
            remote(zsend.at[it], zrecv.at[it, zone], zs.at[it], zr.at[it], {"zone": at_zone(step)}).start()

        for r in range(rows):
            multiplier = split_rows(pushes[r], sub < 4)
            force = jnp.dot(multiplier, mhi_ref[r], preferred_element_type=F32)
            force = force + jnp.dot(multiplier, mlo_ref[r], preferred_element_type=F32)
            force = force + pltpu.roll(force, 4, axis=0)
            high = force.astype(BF16).astype(F32)
            force = jnp.where(upper, high, force - high)
            for k in range(NNZ):
                at = (r * NNZ + k) * 8
                push_ref[at:at + 8, :] = force[:, k * BLK:(k + 1) * BLK]
        summed = jnp.dot(spread_ref[...], push_ref[...].astype(BF16), preferred_element_type=F32)
        bsend[it] = summed.reshape(n_zone * CAP, 4, BLK)
        for step in range(1, n_zone):
            z = at_zone(step)
            remote(
                bsend.at[it, slots_of(z)], brecv.at[it, slots_of(zone)], bs.at[it], br.at[it], {"zone": z}
            ).start()
        brecv[it, slots_of(zone)] = bsend[it, slots_of(zone)]

        for c in range(comps):
            for b in range(halves):
                j = c * halves + b
                l_ref[c, b, 0:1, :] = l_ref[c, b, 0:1, :] - over[j:j + 1]
                l_ref[c, b, height - 1:height, :] = l_ref[c, b, height - 1:height, :] - under[j:j + 1]
        for halo, b, column in ((left, 0, 0), (right, halves - 1, BLK - 1)):
            for c in range(comps):
                for g in range(groups):
                    j = c * groups + g
                    spread = jnp.broadcast_to(halo[:, j:j + 1], (8, BLK))
                    image = l_ref[c, b, g * 8:g * 8 + 8, :]
                    l_ref[c, b, g * 8:g * 8 + 8, :] = jnp.where(lane == column, image - spread, image)

        await_bytes(zrecv.at[it, 0:n_zone - 1], zr.at[it])
        part = jnp.sum(zrecv[it], axis=0)
        vsend[it] = part
        vrecv[it, vol] = part
        for step in range(1, n_vol):
            remote(vsend.at[it], vrecv.at[it, vol], vs.at[it], vr.at[it], {"vol": at_vol(step)}).start()

        await_bytes(brecv.at[it, 0:(n_zone - 1) * CAP], br.at[it])
        for m in range(blocks):
            back_ref[m * 8:m * 8 + 4, :] = brecv[it, unpack_tab[m]]
        for c in range(comps):
            for b in range(halves):
                contact = back_ref[pl.ds(b * 8 + c, SROWS, stride=8 * halves), :]
                l_ref[c, b, 0:SROWS, :] = l_ref[c, b, 0:SROWS, :] + contact

        await_bytes(vrecv.at[it, 0:n_vol - 1], vr.at[it])
        total = jnp.sum(jnp.sum(vrecv[it], axis=0), axis=1, keepdims=True)
        gamma, delta, cross = total[0:1], total[1:2], total[2:3]
        beta = jnp.where(first, 0.0, gamma / gamma_old)
        pq = delta + beta * (2.0 * cross + beta * pq_old)
        step_length = gamma / pq
        wide_beta = jnp.broadcast_to(beta, (8, BLK))
        wide_step = jnp.broadcast_to(step_length, (8, BLK))

        def update(g, cross):
            at = tile_rows(g)
            for c in range(comps):
                for b in range(halves):
                    x = x_ref[c, b, group_rows(g), :]
                    p = x + wide_beta * p_ref[c, b, at, :]
                    t = l_ref[c, b, at, :] + wide_beta * t_ref[c, b, at, :]
                    q = t + d_ref[c, b, at, :] * p
                    x = x - wide_step * q
                    p_ref[c, b, at, :] = p
                    t_ref[c, b, at, :] = t
                    x_ref[c, b, group_rows(g), :] = x
                    half = slice(b * BLK, (b + 1) * BLK)
                    u_ref[c, at, half] = u_ref[c, at, half] + wide_step * p
                    lu_ref[c, b, at, :] = lu_ref[c, b, at, :] + wide_step * t
                    cross = cross + x * q
            return cross

        cross = lax.fori_loop(0, groups, update, zero, unroll=2)

        @pl.when(lax.rem(it, KRY) == KRY - 1)
        def _():
            def newton(g, _):
                at = tile_rows(g)
                for b in range(halves):
                    stiff, hard = hardened(b, g)
                    half = slice(b * BLK, (b + 1) * BLK)
                    for c in range(comps):
                        u = u_ref[c, at, half]
                        bent = jnp.tanh(u / yield_scale)
                        material = stiff * (hard * u + (1.0 - hard) * yield_scale * bent)
                        residual = lu_ref[c, b, at, :] + material - load_ref[c, at, half]
                        res_ref[c, at, half] = residual
                        x_ref[c, b, group_rows(g), :] = -residual
                        d_ref[c, b, at, :] = stiff * (hard + (1.0 - hard) * (1.0 - bent * bent))
                return 0

            lax.fori_loop(0, groups, newton, 0)

        return gamma, step_length, pq, cross

    one = jnp.ones((1, 1), F32)
    lax.fori_loop(0, STEPS, iteration, (one, one, one, jnp.zeros((8, BLK), F32)))

    def drain(it, _):
        await_bytes(fsend.at[it, 0:n_zone - 1], fs.at[it])
        await_bytes(bsend.at[it, 0:(n_zone - 1) * CAP], bs.at[it])
        await_bytes(rsend.at[it], rs.at[it])
        await_bytes(csend.at[it], cs.at[it])
        await_bytes(zrecv.at[it, 0:n_zone - 1], zs.at[it])
        await_bytes(vrecv.at[it, 0:n_vol - 1], vs.at[it])
        return 0

    lax.fori_loop(0, STEPS, drain, 0)


def local(n_vol, n_zone, load, support_stiffness, plastic_flags, owner_map, pattern, active, mortar):
    comps, height, breadth = load.shape
    halves = breadth // BLK
    rows = active.shape[2]
    field = pltpu.VMEM((comps, halves, height, BLK), F32)
    slots = n_zone * CAP
    dma = pltpu.SemaphoreType.DMA
    vmem = pl.BlockSpec(memory_space=pltpu.VMEM)
    smem = pl.BlockSpec(memory_space=pltpu.SMEM)
    return pl.pallas_call(
        functools.partial(kernel, n_vol, n_zone),
        out_shape=[jax.ShapeDtypeStruct(load.shape, F32)] * 2,
        in_specs=[vmem, vmem, vmem, smem, smem, smem, pl.BlockSpec(memory_space=pl.ANY)],
        out_specs=[vmem, vmem],
        scratch_shapes=[
            pltpu.VMEM((comps, halves, height + 2 * PAD, BLK), F32),
            field, field, field, field, field,
            pltpu.VMEM((halves, height, BLK), F32),
            pltpu.VMEM(mortar.shape[2:], F32),
            pltpu.VMEM((rows, BLK, NNZ * BLK), BF16),
            pltpu.VMEM((rows, BLK, NNZ * BLK), BF16),
            pltpu.VMEM((slots * 4, rows * NNZ * 8), BF16),
            pltpu.VMEM((rows * NNZ * 8, BLK), F32),
            pltpu.VMEM((SROWS * halves * 8, BLK), F32),
            pltpu.VMEM((SROWS * halves + 1, 8, BLK), F32),
            pltpu.VMEM((SROWS * halves * 8, BLK), F32),
            pltpu.SMEM((slots,), jnp.int32),
            pltpu.SMEM((SROWS * halves,), jnp.int32),
            pltpu.VMEM((STEPS, n_zone, CAP, 4, BLK), F32),
            pltpu.VMEM((STEPS, slots, 4, BLK), F32),
            pltpu.VMEM((STEPS, slots, 4, BLK), F32),
            pltpu.VMEM((STEPS, slots, 4, BLK), F32),
            pltpu.VMEM((STEPS, 2, 8, BLK), F32),
            pltpu.VMEM((STEPS, 2, 8, BLK), F32),
            pltpu.VMEM((STEPS, 2, 8, BLK), F32),
            pltpu.VMEM((STEPS, 2, 8, BLK), F32),
            pltpu.VMEM((STEPS, 4, BLK), F32),
            pltpu.VMEM((STEPS, n_zone, 4, BLK), F32),
            pltpu.VMEM((STEPS, 4, BLK), F32),
            pltpu.VMEM((STEPS, n_vol, 4, BLK), F32),
            dma,
        ] + [dma((STEPS,))] * 12,
        compiler_params=pltpu.CompilerParams(
            collective_id=0, has_side_effects=True, vmem_limit_bytes=32 * 1024 * 1024
        ),
    )(load, support_stiffness, plastic_flags, owner_map, pattern, active, mortar)


def solution(mesh):
    in_specs = (
        P(None, "vol", "zone"),
        P("vol", "zone"),
        P("vol", "zone"),
        P("vol", "zone", None),
        P("vol", "zone", None, None),
        P("vol", "zone", None),
        P("vol", "zone", None, None, None, None),
    )
    out_specs = (P(None, "vol", "zone"), P(None, "vol", "zone"))
    body = functools.partial(local, mesh.shape["vol"], mesh.shape["zone"])
    return jax.shard_map(body, mesh=mesh, in_specs=in_specs, out_specs=out_specs, check_vma=False)
```

```python
import functools

import jax
import jax.numpy as jnp
from jax import lax
from jax.experimental import pallas as pl
from jax.experimental.pallas import tpu as pltpu
from jax.sharding import PartitionSpec as P

SROWS = 8
BLK = 128
NNZ = 3
CAP = 4
KRY = 3
NEWTON = 2
STEPS = KRY * NEWTON
PAD = 8

yield_scale = 0.5
penalty = 2.0
plastic_hardening = 0.2

F32 = jnp.float32
BF16 = jnp.bfloat16


def kernel(
    n_vol, n_zone,
    load_hbm, stiff_hbm, flags_hbm, owner_hbm, pattern_hbm, active_hbm, mortar_ref,
    u_ref, res_ref,
    load_ref, stiff_ref, flags_ref, owner_ref, pattern_ref, active_ref, mort_ref,
    x_ref, l_ref, r_ref, d_ref, lu_ref, hard_ref, contact_ref, gap_ref, scale_ref,
    mhi_ref, mlo_ref, spread_ref, push_ref,
    surf_ref, block_ref, back_ref,
    pack_tab, unpack_tab,
    fsend, frecv, bsend, brecv, rsend, rrecv, csend, crecv, ssend, srecv,
    in_sem, fs, fr, bs, br, rs, rr, cs, cr, ss, sr,
):
    comps, height = load_ref.shape[0], load_ref.shape[1]
    halves = load_ref.shape[2] // BLK
    groups = height // 8
    blocks = SROWS * halves
    rows = active_ref.shape[2]
    devices = n_vol * n_zone
    zone = lax.axis_index("zone")
    vol = lax.axis_index("vol")

    inputs = [
        (owner_hbm, owner_ref), (pattern_hbm, pattern_ref), (active_hbm, active_ref), (flags_hbm, flags_ref),
        (load_hbm, load_ref), (stiff_hbm, stiff_ref), (mortar_ref.at[0, 0], mort_ref),
    ]
    fetches = [pltpu.make_async_copy(src, dst, in_sem.at[i]) for i, (src, dst) in enumerate(inputs)]
    for fetch in fetches:
        fetch.start()

    def at_zone(step):
        return lax.rem(zone + step, n_zone) if step else zone

    def at_vol(step):
        return lax.rem(vol + step, n_vol) if step else vol

    side = 4

    def hops(offset):
        around = [offset[0] // side, offset[0] % side, (offset[1] + 1) // 2]
        return sum(min(a % side, side - a % side) for a in around)

    others = [(v, z) for v in range(n_vol) for z in range(n_zone) if (v, z) != (0, 0)]
    others.sort(key=lambda offset: -hops(offset))

    barrier = pltpu.get_barrier_semaphore()
    for v, z in others:
        pl.semaphore_signal(barrier, inc=1, device_id={"vol": at_vol(v), "zone": at_zone(z)})

    sub = lax.broadcasted_iota(jnp.int32, (8, BLK), 0)
    lane = lax.broadcasted_iota(jnp.int32, (8, BLK), 1)
    zero = jnp.zeros((8, BLK), F32)

    for fetch in fetches[:4]:
        fetch.wait()
    owners = [owner_ref[0, 0, m] for m in range(blocks)]
    weights = []
    for m in range(blocks):
        weight, rank = jnp.int32(1), jnp.int32(0)
        for e in range(m):
            same = owners[e] == owners[m]
            weight = jnp.where(same, weight * 32, weight)
            rank = rank + jnp.where(same, 1, 0)
        weights.append(weight)
        unpack_tab[m] = owners[m] * CAP + rank
    for z in range(n_zone):
        code = jnp.int32(0)
        for m in range(blocks):
            code = code + jnp.where(owners[m] == z, weights[m] * (blocks + m), 0)
        for k in range(CAP):
            field = lax.shift_right_logical(code, 5 * k) & 31
            pack_tab[z * CAP + k] = jnp.where(field >= blocks, field - blocks, blocks)

    def link(r, k):
        return pattern_ref[0, k, 0, r]

    wide = rows * NNZ * 8
    link_lane = lax.broadcasted_iota(jnp.int32, (1, wide), 1)
    links = jnp.zeros((1, wide), jnp.int32)
    for r in range(rows):
        scale_ref[r * 8:r * 8 + 8, :] = jnp.full((8, BLK), penalty * active_ref[0, 0, r].astype(F32))
        for k in range(NNZ):
            links = jnp.where(link_lane // 8 == r * NNZ + k, link(r, k), links)
    out_row = lax.broadcasted_iota(jnp.int32, (n_zone * CAP * 4, wide), 0)
    out_lane = lax.broadcasted_iota(jnp.int32, (n_zone * CAP * 4, wide), 1)
    hit = (out_row // 4 == links) & (lax.rem(out_row, 4) == lax.rem(out_lane, 4))
    spread_ref[...] = jnp.where(hit, 1.0, 0.0).astype(BF16)

    surf_ref[...] = jnp.zeros_like(surf_ref)
    block_ref[blocks] = zero
    back_ref[...] = jnp.zeros_like(back_ref)
    rsend[...] = jnp.zeros_like(rsend)
    u_ref[...] = jnp.zeros_like(u_ref)
    lu_ref[...] = jnp.zeros_like(lu_ref)
    for b in range(halves):
        flag = jnp.transpose(jnp.broadcast_to(flags_ref[b:b + 1, :], (height, BLK)))
        hard_ref[b] = jnp.where(flag == 1, plastic_hardening, 1.0).astype(F32)
    for fetch in fetches[4:6]:
        fetch.wait()
    for c in range(comps):
        for b in range(halves):
            for j in range(KRY):
                x_ref[j, c, b, 0:PAD, :] = jnp.zeros((PAD, BLK), F32)
                x_ref[j, c, b, PAD + height:, :] = jnp.zeros((PAD, BLK), F32)
            x_ref[0, c, b, PAD:PAD + height, :] = load_ref[c, :, b * BLK:(b + 1) * BLK]
            d_ref[c, b] = stiff_ref[:, b * BLK:(b + 1) * BLK]
    fetches[6].wait()

    def split(r, _):
        for k in range(NNZ):
            piece = mort_ref[r, k] if k == 0 else -mort_ref[r, k]
            high = piece.astype(BF16)
            mhi_ref[r, :, k * BLK:(k + 1) * BLK] = high
            mlo_ref[r, :, k * BLK:(k + 1) * BLK] = (piece - high.astype(F32)).astype(BF16)
        return 0

    lax.fori_loop(0, rows, split, 0)

    pl.semaphore_wait(barrier, devices - 1)

    def remote(src, dst, send, recv, target):
        return pltpu.make_async_remote_copy(
            src_ref=src, dst_ref=dst, send_sem=send, recv_sem=recv, device_id=target
        )

    def await_bytes(ref, sem):
        pltpu.make_async_copy(ref, ref, sem).wait()

    def slots_of(z):
        return pl.ds(z * CAP, CAP)

    def group_rows(g):
        return pl.ds(pl.multiple_of(PAD + g * 8, 8), 8)

    def tile_rows(g):
        return pl.ds(pl.multiple_of(g * 8, 8), 8)

    def over_tiles(body, init):
        def group(g, carry):
            for c in range(comps):
                for b in range(halves):
                    carry = body(c, b, group_rows(g), tile_rows(g), carry)
            return carry

        return lax.fori_loop(0, groups, group, init, unroll=2)

    def send_field(j, it):
        for c in range(comps):
            for b in range(halves):
                surf_ref[pl.ds(b * 8 + c, SROWS, stride=8 * halves), :] = x_ref[j, c, b, PAD:PAD + SROWS, :]
        for m in range(blocks):
            block_ref[m] = surf_ref[m * 8:m * 8 + 8, :]
        for step in (4, 3, 5, 2, 6, 1, 7, 0):
            z = at_zone(step)
            for k in range(CAP):
                block = block_ref[pack_tab[z * CAP + k]][0:4]
                if step:
                    fsend[it, step, k] = block
                else:
                    frecv[it, zone * CAP + k] = block
            if step:
                remote(
                    fsend.at[it, step], frecv.at[it, slots_of(zone)], fs.at[it], fr.at[it], {"zone": z}
                ).start()
        for c in range(comps):
            for b in range(halves):
                i = c * halves + b
                rsend[it, 0, i:i + 1, :] = x_ref[j, c, b, PAD:PAD + 1, :]
                rsend[it, 1, i:i + 1, :] = x_ref[j, c, b, PAD + height - 1:PAD + height, :]
        remote(rsend.at[it, 0], rrecv.at[it, 1], rs.at[it], rr.at[it], {"vol": at_vol(n_vol - 1)}).start()
        remote(rsend.at[it, 1], rrecv.at[it, 0], rs.at[it], rr.at[it], {"vol": at_vol(1)}).start()
        for end, b, column in ((0, 0, 0), (1, halves - 1, BLK - 1)):
            strip = zero
            for c in range(comps):
                for g in range(groups):
                    tile = x_ref[j, c, b, PAD + g * 8:PAD + g * 8 + 8, :]
                    strip = jnp.where(
                        lane == c * groups + g, jnp.broadcast_to(tile[:, column:column + 1], (8, BLK)), strip
                    )
            csend[it, end] = strip
        remote(csend.at[it, 0], crecv.at[it, 1], cs.at[it], cr.at[it], {"zone": at_zone(n_zone - 1)}).start()
        remote(csend.at[it, 1], crecv.at[it, 0], cs.at[it], cr.at[it], {"zone": at_zone(1)}).start()

    def inner(j):
        def group(g, _):
            for c in range(comps):
                tiles = [x_ref[j, c, b, group_rows(g), :] for b in range(halves)]
                to_right = [pltpu.roll(tile, 1, axis=1) for tile in tiles]
                to_left = [pltpu.roll(tile, BLK - 1, axis=1) for tile in tiles]
                for b in range(halves):
                    before = to_right[b - 1] if b > 0 else zero
                    after = to_left[b + 1] if b < halves - 1 else zero
                    left = jnp.where(lane == 0, before, to_right[b])
                    right = jnp.where(lane == BLK - 1, after, to_left[b])
                    over = x_ref[j, c, b, pl.ds(PAD + g * 8 - 1, 8), :]
                    under = x_ref[j, c, b, pl.ds(PAD + g * 8 + 1, 8), :]
                    l_ref[j, c, b, tile_rows(g), :] = 4.0 * tiles[b] - (over + under + left + right)
            return 0

        lax.fori_loop(0, groups, group, 0, unroll=2)

    def outer(j, it):
        await_bytes(rrecv.at[it], rr.at[it])
        await_bytes(crecv.at[it], cr.at[it])
        over = jnp.where(vol == 0, 0.0, rrecv[it, 0])
        under = jnp.where(vol == n_vol - 1, 0.0, rrecv[it, 1])
        left = jnp.where(zone == 0, 0.0, crecv[it, 0])
        right = jnp.where(zone == n_zone - 1, 0.0, crecv[it, 1])
        for c in range(comps):
            for b in range(halves):
                i = c * halves + b
                l_ref[j, c, b, 0:1, :] = l_ref[j, c, b, 0:1, :] - over[i:i + 1]
                l_ref[j, c, b, height - 1:height, :] = l_ref[j, c, b, height - 1:height, :] - under[i:i + 1]
        for halo, b, column in ((left, 0, 0), (right, halves - 1, BLK - 1)):
            for c in range(comps):
                for g in range(groups):
                    i = c * groups + g
                    spread = jnp.broadcast_to(halo[:, i:i + 1], (8, BLK))
                    image = l_ref[j, c, b, g * 8:g * 8 + 8, :]
                    l_ref[j, c, b, g * 8:g * 8 + 8, :] = jnp.where(lane == column, image - spread, image)

    upper = lax.broadcasted_iota(jnp.int32, (8, NNZ * BLK), 0) < 4
    contract_last = (((1,), (1,)), ((), ()))

    def split_rows(both, mask):
        high = both.astype(BF16).astype(F32)
        return jnp.where(mask, high, both - high).astype(BF16)

    def find_gaps(j, it):
        await_bytes(frecv.at[it, 0:(n_zone - 1) * CAP], fr.at[it])
        for r in range(rows):
            picked = jnp.concatenate([frecv[it, link(r, k)] for k in range(NNZ)], axis=1)
            picked = split_rows(jnp.concatenate([picked, picked], axis=0), upper)
            gap = lax.dot_general(picked, mhi_ref[r], contract_last, preferred_element_type=F32)
            gap = gap + lax.dot_general(picked, mlo_ref[r], contract_last, preferred_element_type=F32)
            gap_ref[j, r * 8:r * 8 + 8, :] = gap + pltpu.roll(gap, 4, axis=0)

    def push_forces(j, it):
        for r in range(rows):
            at = slice(r * 8, r * 8 + 8)
            multiplier = split_rows(scale_ref[at, :] * gap_ref[j, at, :], sub < 4)
            force = jnp.dot(multiplier, mhi_ref[r], preferred_element_type=F32)
            force = force + jnp.dot(multiplier, mlo_ref[r], preferred_element_type=F32)
            force = force + pltpu.roll(force, 4, axis=0)
            high = force.astype(BF16).astype(F32)
            force = jnp.where(upper, high, force - high)
            for k in range(NNZ):
                to = (r * NNZ + k) * 8
                push_ref[to:to + 8, :] = force[:, k * BLK:(k + 1) * BLK]
        summed = jnp.dot(spread_ref[...], push_ref[...].astype(BF16), preferred_element_type=F32)
        bsend[it] = summed.reshape(n_zone * CAP, 4, BLK)
        for step in (4, 3, 5, 2, 6, 1, 7):
            z = at_zone(step)
            remote(
                bsend.at[it, slots_of(z)], brecv.at[it, slots_of(zone)], bs.at[it], br.at[it], {"zone": z}
            ).start()
        brecv[it, slots_of(zone)] = bsend[it, slots_of(zone)]

    def receive_forces(j, it):
        await_bytes(brecv.at[it, 0:(n_zone - 1) * CAP], br.at[it])
        for m in range(blocks):
            back_ref[m * 8:m * 8 + 4, :] = brecv[it, unpack_tab[m]]
        for c in range(comps):
            for b in range(halves):
                contact_ref[j, c, b] = back_ref[pl.ds(b * 8 + c, SROWS, stride=8 * halves), :]

    def energy(gaps):
        total = zero
        for r in range(rows):
            at = slice(r * 8, r * 8 + 8)
            gap = gaps(at)
            total = total + scale_ref[at, :] * (gap * gap)
        return 0.5 * total

    def start_sums(it, gamma, delta, cross):
        parts = []
        for part in (gamma, delta, cross):
            part = part + pltpu.roll(part, 64, axis=1)
            parts.append(part + pltpu.roll(part, 32, axis=1))
        mixed = jnp.where(lane < 32, parts[0], jnp.where(lane < 64, parts[1], parts[2]))
        mixed = jnp.sum(mixed, axis=0, keepdims=True)
        me = vol * n_zone + zone
        ssend[it] = mixed
        srecv[it, me] = mixed
        for v, z in others:
            target = {"vol": at_vol(v), "zone": at_zone(z)}
            remote(ssend.at[it], srecv.at[it, me], ss.at[it], sr.at[it], target).start()

    def finish_sums(it):
        await_bytes(srecv.at[it, 0:devices - 1], sr.at[it])
        total = jnp.sum(srecv[it], axis=0)
        place = lane[0:1]
        return [
            jnp.sum(jnp.where(place // 32 == i, total, 0.0), axis=1, keepdims=True) for i in range(3)
        ]

    def full(scalar):
        return jnp.broadcast_to(scalar, (8, BLK))

    def next_field(j):
        def tile(c, b, padded, at, _):
            x_ref[j + 1, c, b, padded, :] = l_ref[j, c, b, at, :] + d_ref[c, b, at, :] * x_ref[j, c, b, padded, :]
            return 0

        over_tiles(tile, 0)

    def add_contact(j):
        for c in range(comps):
            for b in range(halves):
                at = slice(PAD, PAD + SROWS)
                x_ref[j + 1, c, b, at, :] = x_ref[j + 1, c, b, at, :] + contact_ref[j, c, b]

    def newton(n, _):
        it = n * KRY

        send_field(0, it)
        inner(0)
        find_gaps(0, it)
        push_forces(0, it)
        outer(0, it)

        def dots0(c, b, padded, at, sums):
            x = x_ref[0, c, b, padded, :]
            q = l_ref[0, c, b, at, :] + d_ref[c, b, at, :] * x
            x_ref[1, c, b, padded, :] = q
            return sums[0] + x * x, sums[1] + x * q

        gamma, delta = over_tiles(dots0, (zero, zero))
        start_sums(it, gamma, delta + energy(lambda at: gap_ref[0, at, :]), zero)
        receive_forces(0, it)
        add_contact(0)

        send_field(1, it + 1)
        inner(1)
        gamma0, pq0, _ = finish_sums(it)
        a0 = gamma0 / pq0
        find_gaps(1, it + 1)
        push_forces(1, it + 1)
        outer(1, it + 1)
        w0 = full(a0)

        def dots1(c, b, padded, at, sums):
            x1 = x_ref[1, c, b, padded, :]
            r = x_ref[0, c, b, padded, :] - w0 * x1
            r_ref[c, b, at, :] = r
            q = (l_ref[0, c, b, at, :] - w0 * l_ref[1, c, b, at, :]) + d_ref[c, b, at, :] * r
            x_ref[2, c, b, padded, :] = l_ref[1, c, b, at, :] + d_ref[c, b, at, :] * x1
            return sums[0] + r * r, sums[1] + r * q, sums[2] + r * x1

        gamma, delta, cross = over_tiles(dots1, (zero, zero, zero))
        start_sums(it + 1, gamma, delta + energy(lambda at: gap_ref[0, at, :] - w0 * gap_ref[1, at, :]), cross)
        receive_forces(1, it + 1)
        add_contact(1)

        send_field(2, it + 2)
        inner(2)
        gamma1, delta, cross = finish_sums(it + 1)
        beta1 = gamma1 / gamma0
        pq1 = delta + beta1 * (2.0 * cross + beta1 * pq0)
        a1 = gamma1 / pq1
        find_gaps(2, it + 2)
        outer(2, it + 2)
        more, w1 = full(1.0 + beta1), full(a1)

        def second(x0, x1, x2):
            image = more * x1 - w0 * x2
            return image, (x0 - w0 * x1) - w1 * image

        def dots2(c, b, padded, at, sums):
            image = more * x_ref[1, c, b, padded, :] - w0 * x_ref[2, c, b, padded, :]
            r = r_ref[c, b, at, :] - w1 * image
            _, q = second(l_ref[0, c, b, at, :], l_ref[1, c, b, at, :], l_ref[2, c, b, at, :])
            q = q + d_ref[c, b, at, :] * r
            return sums[0] + r * r, sums[1] + r * q, sums[2] + r * image

        gamma, delta, cross = over_tiles(dots2, (zero, zero, zero))
        stored = energy(lambda at: second(gap_ref[0, at, :], gap_ref[1, at, :], gap_ref[2, at, :])[1])
        start_sums(it + 2, gamma, delta + stored, cross)
        push_forces(2, it + 2)
        receive_forces(2, it + 2)
        gamma2, delta, cross = finish_sums(it + 2)
        beta2 = gamma2 / gamma1
        pq2 = delta + beta2 * (2.0 * cross + beta2 * pq1)
        a2 = gamma2 / pq2
        turned = beta2 * (1.0 + beta1)
        k0 = full(a0 + a1 * (1.0 + beta1) + a2 * (1.0 + turned))
        k1 = full(-(a1 * a0 + a2 * (a0 + a1 * (1.0 + beta1) + beta2 * a0)))
        k2 = full(a2 * a1 * a0)

        def mix(fields):
            return k0 * fields(0) + k1 * fields(1) + k2 * fields(2)

        for c in range(comps):
            for b in range(halves):
                lu_ref[c, b, 0:SROWS, :] = lu_ref[c, b, 0:SROWS, :] + mix(lambda j: contact_ref[j, c, b])

        def finish(g, _):
            at = tile_rows(g)
            for b in range(halves):
                half = slice(b * BLK, (b + 1) * BLK)
                stiff, hard = stiff_ref[at, half], hard_ref[b, at, :]
                for c in range(comps):
                    u = u_ref[c, at, half] + mix(lambda j: x_ref[j, c, b, group_rows(g), :])
                    image = lu_ref[c, b, at, :] + mix(lambda j: l_ref[j, c, b, at, :])
                    bent = jnp.tanh(u / yield_scale)
                    material = stiff * (hard * u + (1.0 - hard) * yield_scale * bent)
                    residual = image + material - load_ref[c, at, half]
                    u_ref[c, at, half] = u
                    res_ref[c, at, half] = residual
                    lu_ref[c, b, at, :] = image
                    x_ref[0, c, b, group_rows(g), :] = -residual
                    d_ref[c, b, at, :] = stiff * (hard + (1.0 - hard) * (1.0 - bent * bent))
            return 0

        lax.fori_loop(0, groups, finish, 0)
        return 0

    lax.fori_loop(0, NEWTON, newton, 0)

    def drain(it, _):
        await_bytes(fsend.at[it, 0:n_zone - 1], fs.at[it])
        await_bytes(bsend.at[it, 0:(n_zone - 1) * CAP], bs.at[it])
        await_bytes(rsend.at[it], rs.at[it])
        await_bytes(csend.at[it], cs.at[it])
        await_bytes(srecv.at[it, 0:devices - 1], ss.at[it])
        return 0

    lax.fori_loop(0, STEPS, drain, 0)


def local(n_vol, n_zone, load, support_stiffness, plastic_flags, owner_map, pattern, active, mortar):
    comps, height, breadth = load.shape
    halves = breadth // BLK
    rows = active.shape[2]
    field = pltpu.VMEM((comps, halves, height, BLK), F32)
    slots = n_zone * CAP
    blocks = SROWS * halves
    devices = n_vol * n_zone
    dma = pltpu.SemaphoreType.DMA
    vmem = pl.BlockSpec(memory_space=pltpu.VMEM)
    hbm = pl.BlockSpec(memory_space=pltpu.HBM)
    flags = plastic_flags.T
    links = jnp.transpose(pattern, (0, 3, 1, 2))
    return pl.pallas_call(
        functools.partial(kernel, n_vol, n_zone),
        out_shape=[jax.ShapeDtypeStruct(load.shape, F32)] * 2,
        in_specs=[hbm] * 7,
        out_specs=[vmem, vmem],
        scratch_shapes=[
            pltpu.VMEM(load.shape, F32),
            pltpu.VMEM(support_stiffness.shape, F32),
            pltpu.VMEM(flags.shape, jnp.int32),
            pltpu.SMEM(owner_map.shape, jnp.int32),
            pltpu.SMEM(links.shape, jnp.int32),
            pltpu.SMEM(active.shape, jnp.int32),
            pltpu.VMEM(mortar.shape[2:], F32),
            pltpu.VMEM((KRY, comps, halves, height + 2 * PAD, BLK), F32),
            pltpu.VMEM((KRY, comps, halves, height, BLK), F32),
            field, field, field,
            pltpu.VMEM((halves, height, BLK), F32),
            pltpu.VMEM((KRY, comps, halves, SROWS, BLK), F32),
            pltpu.VMEM((KRY, rows * 8, BLK), F32),
            pltpu.VMEM((rows * 8, BLK), F32),
            pltpu.VMEM((rows, BLK, NNZ * BLK), BF16),
            pltpu.VMEM((rows, BLK, NNZ * BLK), BF16),
            pltpu.VMEM((slots * 4, rows * NNZ * 8), BF16),
            pltpu.VMEM((rows * NNZ * 8, BLK), F32),
            pltpu.VMEM((blocks * 8, BLK), F32),
            pltpu.VMEM((blocks + 1, 8, BLK), F32),
            pltpu.VMEM((blocks * 8, BLK), F32),
            pltpu.SMEM((slots,), jnp.int32),
            pltpu.SMEM((blocks,), jnp.int32),
            pltpu.VMEM((STEPS, n_zone, CAP, 4, BLK), F32),
            pltpu.VMEM((STEPS, slots, 4, BLK), F32),
            pltpu.VMEM((STEPS, slots, 4, BLK), F32),
            pltpu.VMEM((STEPS, slots, 4, BLK), F32),
            pltpu.VMEM((STEPS, 2, 8, BLK), F32),
            pltpu.VMEM((STEPS, 2, 8, BLK), F32),
            pltpu.VMEM((STEPS, 2, 8, BLK), F32),
            pltpu.VMEM((STEPS, 2, 8, BLK), F32),
            pltpu.VMEM((STEPS, 1, BLK), F32),
            pltpu.VMEM((STEPS, devices, 1, BLK), F32),
            dma((7,)),
        ] + [dma((STEPS,))] * 10,
        compiler_params=pltpu.CompilerParams(
            collective_id=0, has_side_effects=True, vmem_limit_bytes=32 * 1024 * 1024
        ),
    )(load, support_stiffness, flags, owner_map, links, active, mortar)


def solution(mesh):
    in_specs = (
        P(None, "vol", "zone"),
        P("vol", "zone"),
        P("vol", "zone"),
        P("vol", "zone", None),
        P("vol", "zone", None, None),
        P("vol", "zone", None),
        P("vol", "zone", None, None, None, None),
    )
    out_specs = (P(None, "vol", "zone"), P(None, "vol", "zone"))
    body = functools.partial(local, mesh.shape["vol"], mesh.shape["zone"])
    return jax.shard_map(body, mesh=mesh, in_specs=in_specs, out_specs=out_specs, check_vma=False)
```

```python
import functools

import jax
import jax.numpy as jnp
from jax import lax
from jax.experimental import pallas as pl
from jax.experimental.pallas import tpu as pltpu
from jax.sharding import PartitionSpec as P

SROWS = 8
BLK = 128
NNZ = 3
CAP = 4
KRY = 3
NEWTON = 2
STEPS = KRY * NEWTON
PAD = 8

yield_scale = 0.5
penalty = 2.0
plastic_hardening = 0.2

F32 = jnp.float32
BF16 = jnp.bfloat16


def kernel(
    n_vol, n_zone,
    load_hbm, stiff_hbm, flags_hbm, owner_hbm, pattern_hbm, active_hbm, mortar_ref,
    u_ref, res_ref,
    load_ref, stiff_ref, flags_ref, owner_ref, pattern_ref, active_ref, mort_ref,
    x_ref, l_ref, r_ref, d_ref, lu_ref, hard_ref, contact_ref, gap_ref, scale_ref,
    mhi_ref, mlo_ref, spread_ref, push_ref,
    surf_ref, block_ref, back_ref,
    pack_tab, unpack_tab,
    fsend, frecv, bsend, brecv, rsend, rrecv, csend, crecv, ssend, srecv,
    in_sem, fs, fr, bs, br, rs, rr, cs, cr, ss, sr,
):
    comps, height = load_ref.shape[0], load_ref.shape[1]
    halves = load_ref.shape[2] // BLK
    groups = height // 8
    blocks = SROWS * halves
    rows = active_ref.shape[2]
    devices = n_vol * n_zone
    zone = lax.axis_index("zone")
    vol = lax.axis_index("vol")

    inputs = [
        (owner_hbm, owner_ref), (pattern_hbm, pattern_ref), (active_hbm, active_ref), (flags_hbm, flags_ref),
        (load_hbm, load_ref), (stiff_hbm, stiff_ref), (mortar_ref.at[0, 0], mort_ref),
    ]
    fetches = [pltpu.make_async_copy(src, dst, in_sem.at[i]) for i, (src, dst) in enumerate(inputs)]
    for fetch in fetches:
        fetch.start()

    def at_zone(step):
        return lax.rem(zone + step, n_zone) if step else zone

    def at_vol(step):
        return lax.rem(vol + step, n_vol) if step else vol

    side = 4

    def hops(offset):
        around = [offset[0] // side, offset[0] % side, (offset[1] + 1) // 2]
        return sum(min(a % side, side - a % side) for a in around)

    others = [(v, z) for v in range(n_vol) for z in range(n_zone) if (v, z) != (0, 0)]
    others.sort(key=lambda offset: -hops(offset))

    barrier = pltpu.get_barrier_semaphore()
    for v, z in others:
        pl.semaphore_signal(barrier, inc=1, device_id={"vol": at_vol(v), "zone": at_zone(z)})

    sub = lax.broadcasted_iota(jnp.int32, (8, BLK), 0)
    lane = lax.broadcasted_iota(jnp.int32, (8, BLK), 1)
    zero = jnp.zeros((8, BLK), F32)

    for fetch in fetches[:4]:
        fetch.wait()
    owners = [owner_ref[0, 0, m] for m in range(blocks)]
    weights = []
    for m in range(blocks):
        weight, rank = jnp.int32(1), jnp.int32(0)
        for e in range(m):
            same = owners[e] == owners[m]
            weight = jnp.where(same, weight * 32, weight)
            rank = rank + jnp.where(same, 1, 0)
        weights.append(weight)
        unpack_tab[m] = owners[m] * CAP + rank
    for z in range(n_zone):
        code = jnp.int32(0)
        for m in range(blocks):
            code = code + jnp.where(owners[m] == z, weights[m] * (blocks + m), 0)
        for k in range(CAP):
            field = lax.shift_right_logical(code, 5 * k) & 31
            pack_tab[z * CAP + k] = jnp.where(field >= blocks, field - blocks, blocks)

    def link(r, k):
        return pattern_ref[0, k, 0, r]

    wide = rows * NNZ * 8
    link_lane = lax.broadcasted_iota(jnp.int32, (1, wide), 1)
    links = jnp.zeros((1, wide), jnp.int32)
    for r in range(rows):
        scale_ref[r * 8:r * 8 + 8, :] = jnp.full((8, BLK), penalty * active_ref[0, 0, r].astype(F32))
        for k in range(NNZ):
            links = jnp.where(link_lane // 8 == r * NNZ + k, link(r, k), links)
    out_row = lax.broadcasted_iota(jnp.int32, (n_zone * CAP * 4, wide), 0)
    out_lane = lax.broadcasted_iota(jnp.int32, (n_zone * CAP * 4, wide), 1)
    hit = (out_row // 4 == links) & (lax.rem(out_row, 4) == lax.rem(out_lane, 4))
    spread_ref[...] = jnp.where(hit, 1.0, 0.0).astype(BF16)

    surf_ref[...] = jnp.zeros_like(surf_ref)
    block_ref[blocks] = zero
    back_ref[...] = jnp.zeros_like(back_ref)
    rsend[...] = jnp.zeros_like(rsend)
    u_ref[...] = jnp.zeros_like(u_ref)
    lu_ref[...] = jnp.zeros_like(lu_ref)
    for b in range(halves):
        flag = jnp.transpose(jnp.broadcast_to(flags_ref[b:b + 1, :], (height, BLK)))
        hard_ref[b] = jnp.where(flag == 1, plastic_hardening, 1.0).astype(F32)
    for fetch in fetches[4:6]:
        fetch.wait()
    for c in range(comps):
        for b in range(halves):
            for j in range(KRY):
                x_ref[j, c, b, 0:PAD, :] = jnp.zeros((PAD, BLK), F32)
                x_ref[j, c, b, PAD + height:, :] = jnp.zeros((PAD, BLK), F32)
            x_ref[0, c, b, PAD:PAD + height, :] = load_ref[c, :, b * BLK:(b + 1) * BLK]
            d_ref[c, b] = stiff_ref[:, b * BLK:(b + 1) * BLK]
    fetches[6].wait()

    def split(r, _):
        for k in range(NNZ):
            piece = mort_ref[r, k] if k == 0 else -mort_ref[r, k]
            high = piece.astype(BF16)
            mhi_ref[r, :, k * BLK:(k + 1) * BLK] = high
            mlo_ref[r, :, k * BLK:(k + 1) * BLK] = (piece - high.astype(F32)).astype(BF16)
        return 0

    lax.fori_loop(0, rows, split, 0)

    pl.semaphore_wait(barrier, devices - 1)

    def remote(src, dst, send, recv, target):
        return pltpu.make_async_remote_copy(
            src_ref=src, dst_ref=dst, send_sem=send, recv_sem=recv, device_id=target
        )

    def await_bytes(ref, sem):
        pltpu.make_async_copy(ref, ref, sem).wait()

    def slots_of(z):
        return pl.ds(z * CAP, CAP)

    def group_rows(g):
        return pl.ds(pl.multiple_of(PAD + g * 8, 8), 8)

    def tile_rows(g):
        return pl.ds(pl.multiple_of(g * 8, 8), 8)

    def over_tiles(body, init):
        def group(g, carry):
            for c in range(comps):
                for b in range(halves):
                    carry = body(c, b, group_rows(g), tile_rows(g), carry)
            return carry

        return lax.fori_loop(0, groups, group, init, unroll=2)

    def send_field(j, it):
        for c in range(comps):
            for b in range(halves):
                surf_ref[pl.ds(b * 8 + c, SROWS, stride=8 * halves), :] = x_ref[j, c, b, PAD:PAD + SROWS, :]
        for m in range(blocks):
            block_ref[m] = surf_ref[m * 8:m * 8 + 8, :]
        for step in (4, 3, 5, 2, 6, 1, 7, 0):
            z = at_zone(step)
            for k in range(CAP):
                block = block_ref[pack_tab[z * CAP + k]][0:4]
                if step:
                    fsend[it, step, k] = block
                else:
                    frecv[it, zone * CAP + k] = block
            if step:
                remote(
                    fsend.at[it, step], frecv.at[it, slots_of(zone)], fs.at[it], fr.at[it], {"zone": z}
                ).start()
        for c in range(comps):
            for b in range(halves):
                i = c * halves + b
                rsend[it, 0, i:i + 1, :] = x_ref[j, c, b, PAD:PAD + 1, :]
                rsend[it, 1, i:i + 1, :] = x_ref[j, c, b, PAD + height - 1:PAD + height, :]
        remote(rsend.at[it, 0], rrecv.at[it, 1], rs.at[it], rr.at[it], {"vol": at_vol(n_vol - 1)}).start()
        remote(rsend.at[it, 1], rrecv.at[it, 0], rs.at[it], rr.at[it], {"vol": at_vol(1)}).start()
        for end, b, column in ((0, 0, 0), (1, halves - 1, BLK - 1)):
            strip = zero
            for c in range(comps):
                for g in range(groups):
                    tile = x_ref[j, c, b, PAD + g * 8:PAD + g * 8 + 8, :]
                    strip = jnp.where(
                        lane == c * groups + g, jnp.broadcast_to(tile[:, column:column + 1], (8, BLK)), strip
                    )
            csend[it, end] = strip
        remote(csend.at[it, 0], crecv.at[it, 1], cs.at[it], cr.at[it], {"zone": at_zone(n_zone - 1)}).start()
        remote(csend.at[it, 1], crecv.at[it, 0], cs.at[it], cr.at[it], {"zone": at_zone(1)}).start()

    def inner(j):
        def group(g, _):
            for c in range(comps):
                tiles = [x_ref[j, c, b, group_rows(g), :] for b in range(halves)]
                to_right = [pltpu.roll(tile, 1, axis=1) for tile in tiles]
                to_left = [pltpu.roll(tile, BLK - 1, axis=1) for tile in tiles]
                for b in range(halves):
                    before = to_right[b - 1] if b > 0 else zero
                    after = to_left[b + 1] if b < halves - 1 else zero
                    left = jnp.where(lane == 0, before, to_right[b])
                    right = jnp.where(lane == BLK - 1, after, to_left[b])
                    over = x_ref[j, c, b, pl.ds(PAD + g * 8 - 1, 8), :]
                    under = x_ref[j, c, b, pl.ds(PAD + g * 8 + 1, 8), :]
                    l_ref[j, c, b, tile_rows(g), :] = 4.0 * tiles[b] - (over + under + left + right)
            return 0

        lax.fori_loop(0, groups, group, 0, unroll=2)

    def outer(j, it):
        await_bytes(rrecv.at[it], rr.at[it])
        await_bytes(crecv.at[it], cr.at[it])
        over = jnp.where(vol == 0, 0.0, rrecv[it, 0])
        under = jnp.where(vol == n_vol - 1, 0.0, rrecv[it, 1])
        left = jnp.where(zone == 0, 0.0, crecv[it, 0])
        right = jnp.where(zone == n_zone - 1, 0.0, crecv[it, 1])
        for c in range(comps):
            for b in range(halves):
                i = c * halves + b
                l_ref[j, c, b, 0:1, :] = l_ref[j, c, b, 0:1, :] - over[i:i + 1]
                l_ref[j, c, b, height - 1:height, :] = l_ref[j, c, b, height - 1:height, :] - under[i:i + 1]
        for halo, b, column in ((left, 0, 0), (right, halves - 1, BLK - 1)):
            for c in range(comps):
                for g in range(groups):
                    i = c * groups + g
                    spread = jnp.broadcast_to(halo[:, i:i + 1], (8, BLK))
                    image = l_ref[j, c, b, g * 8:g * 8 + 8, :]
                    l_ref[j, c, b, g * 8:g * 8 + 8, :] = jnp.where(lane == column, image - spread, image)

    upper = lax.broadcasted_iota(jnp.int32, (8, NNZ * BLK), 0) < 4
    contract_last = (((1,), (1,)), ((), ()))

    def split_rows(both, mask):
        high = both.astype(BF16).astype(F32)
        return jnp.where(mask, high, both - high).astype(BF16)

    def find_gaps(j, it):
        await_bytes(frecv.at[it, 0:(n_zone - 1) * CAP], fr.at[it])
        for r in range(rows):
            picked = jnp.concatenate([frecv[it, link(r, k)] for k in range(NNZ)], axis=1)
            picked = split_rows(jnp.concatenate([picked, picked], axis=0), upper)
            gap = lax.dot_general(picked, mhi_ref[r], contract_last, preferred_element_type=F32)
            gap = gap + lax.dot_general(picked, mlo_ref[r], contract_last, preferred_element_type=F32)
            gap_ref[j, r * 8:r * 8 + 8, :] = gap + pltpu.roll(gap, 4, axis=0)

    def push_forces(j, it):
        for r in range(rows):
            at = slice(r * 8, r * 8 + 8)
            multiplier = split_rows(scale_ref[at, :] * gap_ref[j, at, :], sub < 4)
            force = jnp.dot(multiplier, mhi_ref[r], preferred_element_type=F32)
            force = force + jnp.dot(multiplier, mlo_ref[r], preferred_element_type=F32)
            force = force + pltpu.roll(force, 4, axis=0)
            high = force.astype(BF16).astype(F32)
            force = jnp.where(upper, high, force - high)
            for k in range(NNZ):
                to = (r * NNZ + k) * 8
                push_ref[to:to + 8, :] = force[:, k * BLK:(k + 1) * BLK]
        summed = jnp.dot(spread_ref[...], push_ref[...].astype(BF16), preferred_element_type=F32)
        bsend[it] = summed.reshape(n_zone * CAP, 4, BLK)
        for step in (4, 3, 5, 2, 6, 1, 7):
            z = at_zone(step)
            remote(
                bsend.at[it, slots_of(z)], brecv.at[it, slots_of(zone)], bs.at[it], br.at[it], {"zone": z}
            ).start()
        brecv[it, slots_of(zone)] = bsend[it, slots_of(zone)]

    def receive_forces(j, it):
        await_bytes(brecv.at[it, 0:(n_zone - 1) * CAP], br.at[it])
        for m in range(blocks):
            back_ref[m * 8:m * 8 + 4, :] = brecv[it, unpack_tab[m]]
        for c in range(comps):
            for b in range(halves):
                contact_ref[j, c, b] = back_ref[pl.ds(b * 8 + c, SROWS, stride=8 * halves), :]

    def energy(gaps):
        total = zero
        for r in range(rows):
            at = slice(r * 8, r * 8 + 8)
            gap = gaps(at)
            total = total + scale_ref[at, :] * (gap * gap)
        return 0.5 * total

    def start_sums(it, gamma, delta, cross):
        parts = []
        for part in (gamma, delta, cross):
            part = part + pltpu.roll(part, 64, axis=1)
            parts.append(part + pltpu.roll(part, 32, axis=1))
        mixed = jnp.where(lane < 32, parts[0], jnp.where(lane < 64, parts[1], parts[2]))
        mixed = jnp.sum(mixed, axis=0, keepdims=True)
        me = vol * n_zone + zone
        ssend[it] = mixed
        srecv[it, me] = mixed
        for v, z in others:
            target = {"vol": at_vol(v), "zone": at_zone(z)}
            remote(ssend.at[it], srecv.at[it, me], ss.at[it], sr.at[it], target).start()

    def finish_sums(it):
        await_bytes(srecv.at[it, 0:devices - 1], sr.at[it])
        total = jnp.sum(srecv[it], axis=0)
        place = lane[0:1]
        return [
            jnp.sum(jnp.where(place // 32 == i, total, 0.0), axis=1, keepdims=True) for i in range(3)
        ]

    def full(scalar):
        return jnp.broadcast_to(scalar, (8, BLK))

    def next_field(j):
        def tile(c, b, padded, at, _):
            x_ref[j + 1, c, b, padded, :] = l_ref[j, c, b, at, :] + d_ref[c, b, at, :] * x_ref[j, c, b, padded, :]
            return 0

        over_tiles(tile, 0)

    def add_contact(j):
        for c in range(comps):
            for b in range(halves):
                at = slice(PAD, PAD + SROWS)
                x_ref[j + 1, c, b, at, :] = x_ref[j + 1, c, b, at, :] + contact_ref[j, c, b]

    def newton(n, _):
        it = n * KRY

        send_field(0, it)
        inner(0)
        find_gaps(0, it)
        push_forces(0, it)
        outer(0, it)

        def dots0(c, b, padded, at, sums):
            x = x_ref[0, c, b, padded, :]
            q = l_ref[0, c, b, at, :] + d_ref[c, b, at, :] * x
            x_ref[1, c, b, padded, :] = q
            return sums[0] + x * x, sums[1] + x * q

        gamma, delta = over_tiles(dots0, (zero, zero))
        start_sums(it, gamma, delta + energy(lambda at: gap_ref[0, at, :]), zero)
        receive_forces(0, it)
        add_contact(0)

        send_field(1, it + 1)
        inner(1)
        gamma0, pq0, _ = finish_sums(it)
        a0 = gamma0 / pq0
        find_gaps(1, it + 1)
        push_forces(1, it + 1)
        outer(1, it + 1)
        w0 = full(a0)

        def dots1(c, b, padded, at, sums):
            x1 = x_ref[1, c, b, padded, :]
            r = x_ref[0, c, b, padded, :] - w0 * x1
            r_ref[c, b, at, :] = r
            q = (l_ref[0, c, b, at, :] - w0 * l_ref[1, c, b, at, :]) + d_ref[c, b, at, :] * r
            x_ref[2, c, b, padded, :] = l_ref[1, c, b, at, :] + d_ref[c, b, at, :] * x1
            return sums[0] + r * r, sums[1] + r * q, sums[2] + r * x1

        gamma, delta, cross = over_tiles(dots1, (zero, zero, zero))
        start_sums(it + 1, gamma, delta + energy(lambda at: gap_ref[0, at, :] - w0 * gap_ref[1, at, :]), cross)
        receive_forces(1, it + 1)
        add_contact(1)

        send_field(2, it + 2)
        inner(2)
        gamma1, delta, cross = finish_sums(it + 1)
        beta1 = gamma1 / gamma0
        pq1 = delta + beta1 * (2.0 * cross + beta1 * pq0)
        a1 = gamma1 / pq1
        find_gaps(2, it + 2)
        outer(2, it + 2)
        more, w1 = full(1.0 + beta1), full(a1)

        def second(x0, x1, x2):
            image = more * x1 - w0 * x2
            return image, (x0 - w0 * x1) - w1 * image

        def dots2(c, b, padded, at, sums):
            image = more * x_ref[1, c, b, padded, :] - w0 * x_ref[2, c, b, padded, :]
            r = r_ref[c, b, at, :] - w1 * image
            _, q = second(l_ref[0, c, b, at, :], l_ref[1, c, b, at, :], l_ref[2, c, b, at, :])
            q = q + d_ref[c, b, at, :] * r
            return sums[0] + r * r, sums[1] + r * q, sums[2] + r * image

        gamma, delta, cross = over_tiles(dots2, (zero, zero, zero))
        stored = energy(lambda at: second(gap_ref[0, at, :], gap_ref[1, at, :], gap_ref[2, at, :])[1])
        start_sums(it + 2, gamma, delta + stored, cross)
        push_forces(2, it + 2)
        receive_forces(2, it + 2)
        gamma2, delta, cross = finish_sums(it + 2)
        beta2 = gamma2 / gamma1
        pq2 = delta + beta2 * (2.0 * cross + beta2 * pq1)
        a2 = gamma2 / pq2
        turned = beta2 * (1.0 + beta1)
        k0 = full(a0 + a1 * (1.0 + beta1) + a2 * (1.0 + turned))
        k1 = full(-(a1 * a0 + a2 * (a0 + a1 * (1.0 + beta1) + beta2 * a0)))
        k2 = full(a2 * a1 * a0)

        def mix(fields):
            return k0 * fields(0) + k1 * fields(1) + k2 * fields(2)

        for c in range(comps):
            for b in range(halves):
                lu_ref[c, b, 0:SROWS, :] = lu_ref[c, b, 0:SROWS, :] + mix(lambda j: contact_ref[j, c, b])

        def finish(g, _):
            at = tile_rows(g)
            for b in range(halves):
                half = slice(b * BLK, (b + 1) * BLK)
                stiff, hard = stiff_ref[at, half], hard_ref[b, at, :]
                for c in range(comps):
                    u = u_ref[c, at, half] + mix(lambda j: x_ref[j, c, b, group_rows(g), :])
                    image = lu_ref[c, b, at, :] + mix(lambda j: l_ref[j, c, b, at, :])
                    bent = jnp.tanh(u / yield_scale)
                    material = stiff * (hard * u + (1.0 - hard) * yield_scale * bent)
                    residual = image + material - load_ref[c, at, half]
                    u_ref[c, at, half] = u
                    res_ref[c, at, half] = residual
                    lu_ref[c, b, at, :] = image
                    x_ref[0, c, b, group_rows(g), :] = -residual
                    d_ref[c, b, at, :] = stiff * (hard + (1.0 - hard) * (1.0 - bent * bent))
            return 0

        lax.fori_loop(0, groups, finish, 0)
        return 0

    lax.fori_loop(0, NEWTON, newton, 0)

    def drain(it, _):
        await_bytes(fsend.at[it, 0:n_zone - 1], fs.at[it])
        await_bytes(bsend.at[it, 0:(n_zone - 1) * CAP], bs.at[it])
        await_bytes(rsend.at[it], rs.at[it])
        await_bytes(csend.at[it], cs.at[it])
        await_bytes(srecv.at[it, 0:devices - 1], ss.at[it])
        return 0

    lax.fori_loop(0, STEPS, drain, 0)


def local(n_vol, n_zone, load, support_stiffness, plastic_flags, owner_map, pattern, active, mortar):
    comps, height, breadth = load.shape
    halves = breadth // BLK
    rows = active.shape[2]
    field = pltpu.VMEM((comps, halves, height, BLK), F32)
    slots = n_zone * CAP
    blocks = SROWS * halves
    devices = n_vol * n_zone
    dma = pltpu.SemaphoreType.DMA
    vmem = pl.BlockSpec(memory_space=pltpu.VMEM)
    hbm = pl.BlockSpec(memory_space=pltpu.HBM)
    flags = plastic_flags.T
    links = jnp.transpose(pattern, (0, 3, 1, 2))
    return pl.pallas_call(
        functools.partial(kernel, n_vol, n_zone),
        out_shape=[jax.ShapeDtypeStruct(load.shape, F32)] * 2,
        in_specs=[hbm] * 7,
        out_specs=[vmem, vmem],
        scratch_shapes=[
            pltpu.VMEM(load.shape, F32),
            pltpu.VMEM(support_stiffness.shape, F32),
            pltpu.VMEM(flags.shape, jnp.int32),
            pltpu.SMEM(owner_map.shape, jnp.int32),
            pltpu.SMEM(links.shape, jnp.int32),
            pltpu.SMEM(active.shape, jnp.int32),
            pltpu.VMEM(mortar.shape[2:], F32),
            pltpu.VMEM((KRY, comps, halves, height + 2 * PAD, BLK), F32),
            pltpu.VMEM((KRY, comps, halves, height, BLK), F32),
            field, field, field,
            pltpu.VMEM((halves, height, BLK), F32),
            pltpu.VMEM((KRY, comps, halves, SROWS, BLK), F32),
            pltpu.VMEM((KRY, rows * 8, BLK), F32),
            pltpu.VMEM((rows * 8, BLK), F32),
            pltpu.VMEM((rows, BLK, NNZ * BLK), BF16),
            pltpu.VMEM((rows, BLK, NNZ * BLK), BF16),
            pltpu.VMEM((slots * 4, rows * NNZ * 8), BF16),
            pltpu.VMEM((rows * NNZ * 8, BLK), F32),
            pltpu.VMEM((blocks * 8, BLK), F32),
            pltpu.VMEM((blocks + 1, 8, BLK), F32),
            pltpu.VMEM((blocks * 8, BLK), F32),
            pltpu.SMEM((slots,), jnp.int32),
            pltpu.SMEM((blocks,), jnp.int32),
            pltpu.VMEM((STEPS, n_zone, CAP, 4, BLK), F32),
            pltpu.VMEM((STEPS, slots, 4, BLK), F32),
            pltpu.VMEM((STEPS, slots, 4, BLK), F32),
            pltpu.VMEM((STEPS, slots, 4, BLK), F32),
            pltpu.VMEM((STEPS, 2, 8, BLK), F32),
            pltpu.VMEM((STEPS, 2, 8, BLK), F32),
            pltpu.VMEM((STEPS, 2, 8, BLK), F32),
            pltpu.VMEM((STEPS, 2, 8, BLK), F32),
            pltpu.VMEM((STEPS, 1, BLK), F32),
            pltpu.VMEM((STEPS, devices, 1, BLK), F32),
            dma((7,)),
        ] + [dma((STEPS,))] * 10,
        compiler_params=pltpu.CompilerParams(
            collective_id=0, has_side_effects=True, vmem_limit_bytes=60 * 1024 * 1024
        ),
    )(load, support_stiffness, flags, owner_map, links, active, mortar)


def solution(mesh):
    in_specs = (
        P(None, "vol", "zone"),
        P("vol", "zone"),
        P("vol", "zone"),
        P("vol", "zone", None),
        P("vol", "zone", None, None),
        P("vol", "zone", None),
        P("vol", "zone", None, None, None, None),
    )
    out_specs = (P(None, "vol", "zone"), P(None, "vol", "zone"))
    body = functools.partial(local, mesh.shape["vol"], mesh.shape["zone"])
    return jax.shard_map(body, mesh=mesh, in_specs=in_specs, out_specs=out_specs, check_vma=False)
```

```python
import functools

import jax
import jax.numpy as jnp
from jax import lax
from jax.experimental import pallas as pl
from jax.experimental.pallas import tpu as pltpu
from jax.sharding import PartitionSpec as P

SROWS = 8
BLK = 128
NNZ = 3
CAP = 4
KRY = 3
NEWTON = 2
STEPS = KRY * NEWTON
PAD = 8

yield_scale = 0.5
penalty = 2.0
plastic_hardening = 0.2

F32 = jnp.float32
BF16 = jnp.bfloat16


def kernel(
    n_vol, n_zone,
    load_hbm, stiff_hbm, flags_hbm, owner_hbm, pattern_hbm, active_hbm, mortar_ref,
    u_ref, res_ref,
    load_ref, stiff_ref, flags_ref, owner_ref, pattern_ref, active_ref, mort_ref,
    x_ref, l_ref, r_ref, d_ref, lu_ref, hard_ref, contact_ref, gap_ref, scale_ref,
    mhi_ref, mlo_ref, spread_ref, push_ref,
    surf_ref, block_ref, back_ref,
    pack_tab, unpack_tab,
    fsend, frecv0, frecv1, frecv2, bsend, brecv0, brecv1, brecv2, rsend, rrecv, csend, crecv, ssend, srecv,
    in_sem, fs, fr, bs, br, rs, rr, cs, cr, ss, sr,
):
    frecv, brecv = (frecv0, frecv1, frecv2), (brecv0, brecv1, brecv2)
    comps, height = load_ref.shape[0], load_ref.shape[1]
    halves = load_ref.shape[2] // BLK
    groups = height // 8
    blocks = SROWS * halves
    rows = active_ref.shape[2]
    devices = n_vol * n_zone
    zone = lax.axis_index("zone")
    vol = lax.axis_index("vol")

    inputs = [
        (owner_hbm, owner_ref), (pattern_hbm, pattern_ref), (active_hbm, active_ref), (flags_hbm, flags_ref),
        (load_hbm, load_ref), (stiff_hbm, stiff_ref), (mortar_ref.at[0, 0], mort_ref),
    ]
    fetches = [pltpu.make_async_copy(src, dst, in_sem.at[i]) for i, (src, dst) in enumerate(inputs)]
    for fetch in fetches:
        fetch.start()

    def at_zone(step):
        return lax.rem(zone + step, n_zone) if step else zone

    def at_vol(step):
        return lax.rem(vol + step, n_vol) if step else vol

    side = 4

    def hops(offset):
        around = [offset[0] // side, offset[0] % side, (offset[1] + 1) // 2]
        return sum(min(a % side, side - a % side) for a in around)

    others = [(v, z) for v in range(n_vol) for z in range(n_zone) if (v, z) != (0, 0)]
    others.sort(key=lambda offset: -hops(offset))

    barrier = pltpu.get_barrier_semaphore()
    for v, z in others:
        pl.semaphore_signal(barrier, inc=1, device_id={"vol": at_vol(v), "zone": at_zone(z)})

    sub = lax.broadcasted_iota(jnp.int32, (8, BLK), 0)
    lane = lax.broadcasted_iota(jnp.int32, (8, BLK), 1)
    zero = jnp.zeros((8, BLK), F32)

    for fetch in fetches[:4]:
        fetch.wait()
    owners = [owner_ref[0, 0, m] for m in range(blocks)]
    weights = []
    for m in range(blocks):
        weight, rank = jnp.int32(1), jnp.int32(0)
        for e in range(m):
            same = owners[e] == owners[m]
            weight = jnp.where(same, weight * 32, weight)
            rank = rank + jnp.where(same, 1, 0)
        weights.append(weight)
        unpack_tab[m] = owners[m] * CAP + rank
    for z in range(n_zone):
        code = jnp.int32(0)
        for m in range(blocks):
            code = code + jnp.where(owners[m] == z, weights[m] * (blocks + m), 0)
        for k in range(CAP):
            field = lax.shift_right_logical(code, 5 * k) & 31
            pack_tab[z * CAP + k] = jnp.where(field >= blocks, field - blocks, blocks)

    def link(r, k):
        return pattern_ref[0, k, 0, r]

    wide = rows * NNZ * 8
    link_lane = lax.broadcasted_iota(jnp.int32, (1, wide), 1)
    links = jnp.zeros((1, wide), jnp.int32)
    for r in range(rows):
        scale_ref[r * 8:r * 8 + 8, :] = jnp.full((8, BLK), penalty * active_ref[0, 0, r].astype(F32))
        for k in range(NNZ):
            links = jnp.where(link_lane // 8 == r * NNZ + k, link(r, k), links)
    out_row = lax.broadcasted_iota(jnp.int32, (n_zone * CAP * 4, wide), 0)
    out_lane = lax.broadcasted_iota(jnp.int32, (n_zone * CAP * 4, wide), 1)
    hit = (out_row // 4 == links) & (lax.rem(out_row, 4) == lax.rem(out_lane, 4))
    spread_ref[...] = jnp.where(hit, 1.0, 0.0).astype(BF16)

    surf_ref[...] = jnp.zeros_like(surf_ref)
    block_ref[blocks] = zero
    back_ref[...] = jnp.zeros_like(back_ref)
    rsend[...] = jnp.zeros_like(rsend)
    u_ref[...] = jnp.zeros_like(u_ref)
    lu_ref[...] = jnp.zeros_like(lu_ref)
    for b in range(halves):
        flag = jnp.transpose(jnp.broadcast_to(flags_ref[b:b + 1, :], (height, BLK)))
        hard_ref[b] = jnp.where(flag == 1, plastic_hardening, 1.0).astype(F32)
    for fetch in fetches[4:6]:
        fetch.wait()
    for c in range(comps):
        for b in range(halves):
            for j in range(KRY):
                x_ref[j, c, b, 0:PAD, :] = jnp.zeros((PAD, BLK), F32)
                x_ref[j, c, b, PAD + height:, :] = jnp.zeros((PAD, BLK), F32)
            x_ref[0, c, b, PAD:PAD + height, :] = load_ref[c, :, b * BLK:(b + 1) * BLK]
            d_ref[c, b] = stiff_ref[:, b * BLK:(b + 1) * BLK]
    fetches[6].wait()

    def split(r, _):
        for k in range(NNZ):
            piece = mort_ref[r, k] if k == 0 else -mort_ref[r, k]
            high = piece.astype(BF16)
            mhi_ref[r, :, k * BLK:(k + 1) * BLK] = high
            mlo_ref[r, :, k * BLK:(k + 1) * BLK] = (piece - high.astype(F32)).astype(BF16)
        return 0

    lax.fori_loop(0, rows, split, 0)

    pl.semaphore_wait(barrier, devices - 1)

    def remote(src, dst, send, recv, target):
        return pltpu.make_async_remote_copy(
            src_ref=src, dst_ref=dst, send_sem=send, recv_sem=recv, device_id=target
        )

    def await_bytes(ref, sem):
        pltpu.make_async_copy(ref, ref, sem).wait()

    def slots_of(z):
        return pl.ds(z * CAP, CAP)

    def group_rows(g):
        return pl.ds(pl.multiple_of(PAD + g * 8, 8), 8)

    def tile_rows(g):
        return pl.ds(pl.multiple_of(g * 8, 8), 8)

    def over_tiles(body, init):
        def group(g, carry):
            for c in range(comps):
                for b in range(halves):
                    carry = body(c, b, group_rows(g), tile_rows(g), carry)
            return carry

        return lax.fori_loop(0, groups, group, init, unroll=2)

    def send_surface(j, n, tile):
        it = n * KRY + j
        for c in range(comps):
            for b in range(halves):
                surf_ref[pl.ds(b * 8 + c, SROWS, stride=8 * halves), :] = tile(c, b)
        for m in range(blocks):
            block_ref[m] = surf_ref[m * 8:m * 8 + 8, :]
        for step in (4, 3, 5, 2, 6, 1, 7, 0):
            z = at_zone(step)
            for k in range(CAP):
                block = block_ref[pack_tab[z * CAP + k]][0:4]
                if step:
                    fsend[it, step, k] = block
                else:
                    frecv[j][n, zone * CAP + k] = block
            if step:
                remote(
                    fsend.at[it, step], frecv[j].at[n, slots_of(zone)], fs.at[it], fr.at[it], {"zone": z}
                ).start()

    def field_surface(n):
        send_surface(0, n, lambda c, b: x_ref[0, c, b, PAD:PAD + SROWS, :])

    def grid_surface(j, n):
        send_surface(
            j + 1, n,
            lambda c, b: l_ref[j, c, b, 0:SROWS, :] + d_ref[c, b, 0:SROWS, :] * x_ref[j, c, b, PAD:PAD + SROWS, :],
        )

    def send_halo(j, it):
        for c in range(comps):
            for b in range(halves):
                i = c * halves + b
                rsend[it, 0, i:i + 1, :] = x_ref[j, c, b, PAD:PAD + 1, :]
                rsend[it, 1, i:i + 1, :] = x_ref[j, c, b, PAD + height - 1:PAD + height, :]
        remote(rsend.at[it, 0], rrecv.at[it, 1], rs.at[it], rr.at[it], {"vol": at_vol(n_vol - 1)}).start()
        remote(rsend.at[it, 1], rrecv.at[it, 0], rs.at[it], rr.at[it], {"vol": at_vol(1)}).start()
        for end, b, column in ((0, 0, 0), (1, halves - 1, BLK - 1)):
            strip = zero
            for c in range(comps):
                for g in range(groups):
                    tile = x_ref[j, c, b, PAD + g * 8:PAD + g * 8 + 8, :]
                    strip = jnp.where(
                        lane == c * groups + g, jnp.broadcast_to(tile[:, column:column + 1], (8, BLK)), strip
                    )
            csend[it, end] = strip
        remote(csend.at[it, 0], crecv.at[it, 1], cs.at[it], cr.at[it], {"zone": at_zone(n_zone - 1)}).start()
        remote(csend.at[it, 1], crecv.at[it, 0], cs.at[it], cr.at[it], {"zone": at_zone(1)}).start()

    def inner(j):
        def group(g, _):
            for c in range(comps):
                tiles = [x_ref[j, c, b, group_rows(g), :] for b in range(halves)]
                to_right = [pltpu.roll(tile, 1, axis=1) for tile in tiles]
                to_left = [pltpu.roll(tile, BLK - 1, axis=1) for tile in tiles]
                for b in range(halves):
                    before = to_right[b - 1] if b > 0 else zero
                    after = to_left[b + 1] if b < halves - 1 else zero
                    left = jnp.where(lane == 0, before, to_right[b])
                    right = jnp.where(lane == BLK - 1, after, to_left[b])
                    over = x_ref[j, c, b, pl.ds(PAD + g * 8 - 1, 8), :]
                    under = x_ref[j, c, b, pl.ds(PAD + g * 8 + 1, 8), :]
                    l_ref[j, c, b, tile_rows(g), :] = 4.0 * tiles[b] - (over + under + left + right)
            return 0

        lax.fori_loop(0, groups, group, 0, unroll=2)

    def outer(j, it):
        await_bytes(rrecv.at[it], rr.at[it])
        await_bytes(crecv.at[it], cr.at[it])
        over = jnp.where(vol == 0, 0.0, rrecv[it, 0])
        under = jnp.where(vol == n_vol - 1, 0.0, rrecv[it, 1])
        left = jnp.where(zone == 0, 0.0, crecv[it, 0])
        right = jnp.where(zone == n_zone - 1, 0.0, crecv[it, 1])
        for c in range(comps):
            for b in range(halves):
                i = c * halves + b
                l_ref[j, c, b, 0:1, :] = l_ref[j, c, b, 0:1, :] - over[i:i + 1]
                l_ref[j, c, b, height - 1:height, :] = l_ref[j, c, b, height - 1:height, :] - under[i:i + 1]
        for halo, b, column in ((left, 0, 0), (right, halves - 1, BLK - 1)):
            for c in range(comps):
                for g in range(groups):
                    i = c * groups + g
                    spread = jnp.broadcast_to(halo[:, i:i + 1], (8, BLK))
                    image = l_ref[j, c, b, g * 8:g * 8 + 8, :]
                    l_ref[j, c, b, g * 8:g * 8 + 8, :] = jnp.where(lane == column, image - spread, image)

    upper = lax.broadcasted_iota(jnp.int32, (8, NNZ * BLK), 0) < 4
    contract_last = (((1,), (1,)), ((), ()))

    def split_rows(piece):
        high = piece.astype(BF16).astype(F32)
        rest = piece - high
        middle = rest.astype(BF16).astype(F32)
        return jnp.concatenate([high, middle, rest - middle, jnp.zeros_like(piece)], axis=0).astype(BF16)

    def join_rows(product):
        product = product[0:8] + product[8:16]
        return product + pltpu.roll(product, 4, axis=0)

    def find_gaps(j, n):
        it = n * KRY + j
        await_bytes(frecv[j].at[n, 0:(n_zone - 1) * CAP], fr.at[it])
        for r in range(rows):
            picked = jnp.concatenate([frecv[j][n, link(r, k)] for k in range(NNZ)], axis=1)
            if j:
                picked = picked + jnp.concatenate([bsend[it - 1, link(r, k)] for k in range(NNZ)], axis=1)
            picked = split_rows(picked)
            gap = lax.dot_general(picked, mhi_ref[r], contract_last, preferred_element_type=F32)
            gap = gap + lax.dot_general(picked, mlo_ref[r], contract_last, preferred_element_type=F32)
            gap_ref[j, r * 8:r * 8 + 8, :] = join_rows(gap)

    def push_forces(j, n):
        it = n * KRY + j
        for r in range(rows):
            at = slice(r * 8, r * 8 + 8)
            multiplier = split_rows((scale_ref[at, :] * gap_ref[j, at, :])[0:4])
            force = jnp.dot(multiplier, mhi_ref[r], preferred_element_type=F32)
            force = force + jnp.dot(multiplier, mlo_ref[r], preferred_element_type=F32)
            force = join_rows(force)
            high = force.astype(BF16).astype(F32)
            force = jnp.where(upper, high, force - high)
            for k in range(NNZ):
                to = (r * NNZ + k) * 8
                push_ref[to:to + 8, :] = force[:, k * BLK:(k + 1) * BLK]
        summed = jnp.dot(spread_ref[...], push_ref[...].astype(BF16), preferred_element_type=F32)
        bsend[it] = summed.reshape(n_zone * CAP, 4, BLK)
        for step in (4, 3, 5, 2, 6, 1, 7):
            z = at_zone(step)
            remote(
                bsend.at[it, slots_of(z)], brecv[j].at[n, slots_of(zone)], bs.at[it], br.at[it], {"zone": z}
            ).start()
        brecv[j][n, slots_of(zone)] = bsend[it, slots_of(zone)]

    def receive_forces(j, n):
        await_bytes(brecv[j].at[n, 0:(n_zone - 1) * CAP], br.at[n * KRY + j])
        for m in range(blocks):
            back_ref[m * 8:m * 8 + 4, :] = brecv[j][n, unpack_tab[m]]
        for c in range(comps):
            for b in range(halves):
                contact_ref[j, c, b] = back_ref[pl.ds(b * 8 + c, SROWS, stride=8 * halves), :]

    def energy(gaps):
        total = zero
        for r in range(rows):
            at = slice(r * 8, r * 8 + 8)
            gap = gaps(at)
            total = total + scale_ref[at, :] * (gap * gap)
        return 0.5 * total

    def start_sums(it, gamma, delta, cross):
        parts = []
        for part in (gamma, delta, cross):
            part = part + pltpu.roll(part, 64, axis=1)
            parts.append(part + pltpu.roll(part, 32, axis=1))
        mixed = jnp.where(lane < 32, parts[0], jnp.where(lane < 64, parts[1], parts[2]))
        mixed = jnp.sum(mixed, axis=0, keepdims=True)
        me = vol * n_zone + zone
        ssend[it] = mixed
        srecv[it, me] = mixed
        for v, z in others:
            target = {"vol": at_vol(v), "zone": at_zone(z)}
            remote(ssend.at[it], srecv.at[it, me], ss.at[it], sr.at[it], target).start()

    def finish_sums(it):
        await_bytes(srecv.at[it, 0:devices - 1], sr.at[it])
        total = jnp.sum(srecv[it], axis=0)
        place = lane[0:1]
        return [
            jnp.sum(jnp.where(place // 32 == i, total, 0.0), axis=1, keepdims=True) for i in range(3)
        ]

    def full(scalar):
        return jnp.broadcast_to(scalar, (8, BLK))

    def add_contact(j):
        for c in range(comps):
            for b in range(halves):
                at = slice(PAD, PAD + SROWS)
                x_ref[j + 1, c, b, at, :] = x_ref[j + 1, c, b, at, :] + contact_ref[j, c, b]

    def newton(n, _):
        it = n * KRY

        send_halo(0, it)
        inner(0)
        find_gaps(0, n)
        push_forces(0, n)
        outer(0, it)
        grid_surface(0, n)

        def dots0(c, b, padded, at, sums):
            x = x_ref[0, c, b, padded, :]
            q = l_ref[0, c, b, at, :] + d_ref[c, b, at, :] * x
            x_ref[1, c, b, padded, :] = q
            return sums[0] + x * x, sums[1] + x * q

        gamma, delta = over_tiles(dots0, (zero, zero))
        start_sums(it, gamma, delta + energy(lambda at: gap_ref[0, at, :]), zero)
        receive_forces(0, n)
        add_contact(0)
        send_halo(1, it + 1)
        inner(1)
        find_gaps(1, n)
        push_forces(1, n)
        gamma0, pq0, _ = finish_sums(it)
        a0 = gamma0 / pq0
        outer(1, it + 1)
        grid_surface(1, n)
        w0 = full(a0)

        def dots1(c, b, padded, at, sums):
            x1 = x_ref[1, c, b, padded, :]
            r = x_ref[0, c, b, padded, :] - w0 * x1
            r_ref[c, b, at, :] = r
            q = (l_ref[0, c, b, at, :] - w0 * l_ref[1, c, b, at, :]) + d_ref[c, b, at, :] * r
            x_ref[2, c, b, padded, :] = l_ref[1, c, b, at, :] + d_ref[c, b, at, :] * x1
            return sums[0] + r * r, sums[1] + r * q, sums[2] + r * x1

        gamma, delta, cross = over_tiles(dots1, (zero, zero, zero))
        start_sums(it + 1, gamma, delta + energy(lambda at: gap_ref[0, at, :] - w0 * gap_ref[1, at, :]), cross)
        receive_forces(1, n)
        add_contact(1)
        send_halo(2, it + 2)
        inner(2)
        find_gaps(2, n)
        outer(2, it + 2)
        gamma1, delta, cross = finish_sums(it + 1)
        beta1 = gamma1 / gamma0
        pq1 = delta + beta1 * (2.0 * cross + beta1 * pq0)
        a1 = gamma1 / pq1
        more, w1 = full(1.0 + beta1), full(a1)

        def second(x0, x1, x2):
            image = more * x1 - w0 * x2
            return image, (x0 - w0 * x1) - w1 * image

        def dots2(c, b, padded, at, sums):
            image = more * x_ref[1, c, b, padded, :] - w0 * x_ref[2, c, b, padded, :]
            r = r_ref[c, b, at, :] - w1 * image
            _, q = second(l_ref[0, c, b, at, :], l_ref[1, c, b, at, :], l_ref[2, c, b, at, :])
            q = q + d_ref[c, b, at, :] * r
            return sums[0] + r * r, sums[1] + r * q, sums[2] + r * image

        gamma, delta, cross = over_tiles(dots2, (zero, zero, zero))
        stored = energy(lambda at: second(gap_ref[0, at, :], gap_ref[1, at, :], gap_ref[2, at, :])[1])
        start_sums(it + 2, gamma, delta + stored, cross)
        push_forces(2, n)
        receive_forces(2, n)
        gamma2, delta, cross = finish_sums(it + 2)
        beta2 = gamma2 / gamma1
        pq2 = delta + beta2 * (2.0 * cross + beta2 * pq1)
        a2 = gamma2 / pq2
        turned = beta2 * (1.0 + beta1)
        k0 = full(a0 + a1 * (1.0 + beta1) + a2 * (1.0 + turned))
        k1 = full(-(a1 * a0 + a2 * (a0 + a1 * (1.0 + beta1) + beta2 * a0)))
        k2 = full(a2 * a1 * a0)

        def mix(fields):
            return k0 * fields(0) + k1 * fields(1) + k2 * fields(2)

        for c in range(comps):
            for b in range(halves):
                lu_ref[c, b, 0:SROWS, :] = lu_ref[c, b, 0:SROWS, :] + mix(lambda j: contact_ref[j, c, b])

        def finish(g, _):
            at = tile_rows(g)
            for b in range(halves):
                half = slice(b * BLK, (b + 1) * BLK)
                stiff, hard = stiff_ref[at, half], hard_ref[b, at, :]
                for c in range(comps):
                    u = u_ref[c, at, half] + mix(lambda j: x_ref[j, c, b, group_rows(g), :])
                    image = lu_ref[c, b, at, :] + mix(lambda j: l_ref[j, c, b, at, :])
                    bent = jnp.tanh(u / yield_scale)
                    material = stiff * (hard * u + (1.0 - hard) * yield_scale * bent)
                    residual = image + material - load_ref[c, at, half]
                    u_ref[c, at, half] = u
                    res_ref[c, at, half] = residual
                    lu_ref[c, b, at, :] = image
                    x_ref[0, c, b, group_rows(g), :] = -residual
                    d_ref[c, b, at, :] = stiff * (hard + (1.0 - hard) * (1.0 - bent * bent))
            return 0

        finish(0, 0)

        @pl.when(n < NEWTON - 1)
        def _():
            field_surface(n + 1)

        lax.fori_loop(1, groups, finish, 0)
        return 0

    field_surface(0)
    lax.fori_loop(0, NEWTON, newton, 0)

    def drain(it, _):
        await_bytes(fsend.at[it, 0:n_zone - 1], fs.at[it])
        await_bytes(bsend.at[it, 0:(n_zone - 1) * CAP], bs.at[it])
        await_bytes(rsend.at[it], rs.at[it])
        await_bytes(csend.at[it], cs.at[it])
        await_bytes(srecv.at[it, 0:devices - 1], ss.at[it])
        return 0

    lax.fori_loop(0, STEPS, drain, 0)


def local(n_vol, n_zone, load, support_stiffness, plastic_flags, owner_map, pattern, active, mortar):
    comps, height, breadth = load.shape
    halves = breadth // BLK
    rows = active.shape[2]
    field = pltpu.VMEM((comps, halves, height, BLK), F32)
    slots = n_zone * CAP
    landing = pltpu.VMEM((NEWTON, slots, 4, BLK), F32)
    blocks = SROWS * halves
    devices = n_vol * n_zone
    dma = pltpu.SemaphoreType.DMA
    vmem = pl.BlockSpec(memory_space=pltpu.VMEM)
    hbm = pl.BlockSpec(memory_space=pltpu.HBM)
    flags = plastic_flags.T
    links = jnp.transpose(pattern, (0, 3, 1, 2))
    operands = (load, support_stiffness, flags, owner_map, links, active, mortar)
    return pl.pallas_call(
        functools.partial(kernel, n_vol, n_zone),
        out_shape=[jax.ShapeDtypeStruct(load.shape, F32)] * 2,
        in_specs=[hbm] * 7,
        out_specs=[vmem, vmem],
        scratch_shapes=[
            pltpu.VMEM(load.shape, F32),
            pltpu.VMEM(support_stiffness.shape, F32),
            pltpu.VMEM(flags.shape, jnp.int32),
            pltpu.SMEM(owner_map.shape, jnp.int32),
            pltpu.SMEM(links.shape, jnp.int32),
            pltpu.SMEM(active.shape, jnp.int32),
            pltpu.VMEM(mortar.shape[2:], F32),
            pltpu.VMEM((KRY, comps, halves, height + 2 * PAD, BLK), F32),
            pltpu.VMEM((KRY, comps, halves, height, BLK), F32),
            field, field, field,
            pltpu.VMEM((halves, height, BLK), F32),
            pltpu.VMEM((KRY, comps, halves, SROWS, BLK), F32),
            pltpu.VMEM((KRY, rows * 8, BLK), F32),
            pltpu.VMEM((rows * 8, BLK), F32),
            pltpu.VMEM((rows, BLK, NNZ * BLK), BF16),
            pltpu.VMEM((rows, BLK, NNZ * BLK), BF16),
            pltpu.VMEM((slots * 4, rows * NNZ * 8), BF16),
            pltpu.VMEM((rows * NNZ * 8, BLK), F32),
            pltpu.VMEM((blocks * 8, BLK), F32),
            pltpu.VMEM((blocks + 1, 8, BLK), F32),
            pltpu.VMEM((blocks * 8, BLK), F32),
            pltpu.SMEM((slots,), jnp.int32),
            pltpu.SMEM((blocks,), jnp.int32),
            pltpu.VMEM((STEPS, n_zone, CAP, 4, BLK), F32),
            landing, landing, landing,
            pltpu.VMEM((STEPS, slots, 4, BLK), F32),
            landing, landing, landing,
            pltpu.VMEM((STEPS, 2, 8, BLK), F32),
            pltpu.VMEM((STEPS, 2, 8, BLK), F32),
            pltpu.VMEM((STEPS, 2, 8, BLK), F32),
            pltpu.VMEM((STEPS, 2, 8, BLK), F32),
            pltpu.VMEM((STEPS, 1, BLK), F32),
            pltpu.VMEM((STEPS, devices, 1, BLK), F32),
            dma((7,)),
        ] + [dma((STEPS,))] * 10,
        compiler_params=pltpu.CompilerParams(
            collective_id=0, has_side_effects=True, vmem_limit_bytes=32 * 1024 * 1024
        ),
    )(*[pltpu.with_memory_space_constraint(a, pltpu.HBM) for a in operands])


def solution(mesh):
    in_specs = (
        P(None, "vol", "zone"),
        P("vol", "zone"),
        P("vol", "zone"),
        P("vol", "zone", None),
        P("vol", "zone", None, None),
        P("vol", "zone", None),
        P("vol", "zone", None, None, None, None),
    )
    out_specs = (P(None, "vol", "zone"), P(None, "vol", "zone"))
    body = functools.partial(local, mesh.shape["vol"], mesh.shape["zone"])
    return jax.shard_map(body, mesh=mesh, in_specs=in_specs, out_specs=out_specs, check_vma=False)
```

```python
import functools

import jax
import jax.numpy as jnp
from jax import lax
from jax.experimental import pallas as pl
from jax.experimental.pallas import tpu as pltpu
from jax.sharding import PartitionSpec as P

SROWS = 8
BLK = 128
NNZ = 3
CAP = 4
KRY = 3
NEWTON = 2
STEPS = KRY * NEWTON
PAD = 8

yield_scale = 0.5
penalty = 2.0
plastic_hardening = 0.2

F32 = jnp.float32
BF16 = jnp.bfloat16


def kernel(
    n_vol, n_zone,
    load_hbm, stiff_hbm, flags_hbm, owner_hbm, pattern_hbm, active_hbm, mortar_ref,
    u_ref, res_ref,
    load_ref, stiff_ref, flags_ref, owner_ref, pattern_ref, active_ref, mort_ref,
    x_ref, l_ref, r_ref, d_ref, lu_ref, hard_ref, contact_ref, halo_ref, gap_ref, scale_ref,
    mhi_ref, mlo_ref, spread_ref, push_ref,
    surf_ref, block_ref, back_ref,
    pack_tab, unpack_tab,
    fsend, frecv0, frecv1, frecv2, bsend, brecv0, brecv1, brecv2, rsend, rrecv, csend, crecv, ssend, srecv,
    in_sem, fs, fr, bs, br, rs, rr, cs, cr, ss, sr,
):
    frecv, brecv = (frecv0, frecv1, frecv2), (brecv0, brecv1, brecv2)
    comps, height = load_ref.shape[0], load_ref.shape[1]
    halves = load_ref.shape[2] // BLK
    groups = height // 8
    blocks = SROWS * halves
    rows = active_ref.shape[2]
    devices = n_vol * n_zone
    zone = lax.axis_index("zone")
    vol = lax.axis_index("vol")

    inputs = [
        (owner_hbm, owner_ref), (pattern_hbm, pattern_ref), (active_hbm, active_ref), (flags_hbm, flags_ref),
        (load_hbm, load_ref), (stiff_hbm, stiff_ref), (mortar_ref.at[0, 0], mort_ref),
    ]
    fetches = [pltpu.make_async_copy(src, dst, in_sem.at[i]) for i, (src, dst) in enumerate(inputs)]
    for fetch in fetches:
        fetch.start()

    def at_zone(step):
        return lax.rem(zone + step, n_zone) if step else zone

    def at_vol(step):
        return lax.rem(vol + step, n_vol) if step else vol

    side = 4

    def hops(offset):
        around = [offset[0] // side, offset[0] % side, (offset[1] + 1) // 2]
        return sum(min(a % side, side - a % side) for a in around)

    others = [(v, z) for v in range(n_vol) for z in range(n_zone) if (v, z) != (0, 0)]
    others.sort(key=lambda offset: -hops(offset))

    barrier = pltpu.get_barrier_semaphore()
    for v, z in others:
        pl.semaphore_signal(barrier, inc=1, device_id={"vol": at_vol(v), "zone": at_zone(z)})

    sub = lax.broadcasted_iota(jnp.int32, (8, BLK), 0)
    lane = lax.broadcasted_iota(jnp.int32, (8, BLK), 1)
    zero = jnp.zeros((8, BLK), F32)

    for fetch in fetches[:4]:
        fetch.wait()
    owners = [owner_ref[0, 0, m] for m in range(blocks)]
    weights = []
    for m in range(blocks):
        weight, rank = jnp.int32(1), jnp.int32(0)
        for e in range(m):
            same = owners[e] == owners[m]
            weight = jnp.where(same, weight * 32, weight)
            rank = rank + jnp.where(same, 1, 0)
        weights.append(weight)
        unpack_tab[m] = owners[m] * CAP + rank
    for z in range(n_zone):
        code = jnp.int32(0)
        for m in range(blocks):
            code = code + jnp.where(owners[m] == z, weights[m] * (blocks + m), 0)
        for k in range(CAP):
            field = lax.shift_right_logical(code, 5 * k) & 31
            pack_tab[z * CAP + k] = jnp.where(field >= blocks, field - blocks, blocks)

    def link(r, k):
        return pattern_ref[0, k, 0, r]

    surf_ref[...] = jnp.zeros_like(surf_ref)
    block_ref[blocks] = zero
    rsend[...] = jnp.zeros_like(rsend)
    for fetch in fetches[4:6]:
        fetch.wait()
    for c in range(comps):
        for b in range(halves):
            for j in range(KRY):
                x_ref[j, c, b, 0:PAD, :] = jnp.zeros((PAD, BLK), F32)
                x_ref[j, c, b, PAD + height:, :] = jnp.zeros((PAD, BLK), F32)
            x_ref[0, c, b, PAD:PAD + height, :] = load_ref[c, :, b * BLK:(b + 1) * BLK]
            d_ref[c, b] = stiff_ref[:, b * BLK:(b + 1) * BLK]

    def split(r, _):
        for k in range(NNZ):
            piece = mort_ref[r, k] if k == 0 else -mort_ref[r, k]
            high = piece.astype(BF16)
            mhi_ref[r, :, k * BLK:(k + 1) * BLK] = high
            mlo_ref[r, :, k * BLK:(k + 1) * BLK] = (piece - high.astype(F32)).astype(BF16)
        return 0

    def set_up():
        pairs = rows * NNZ * 8
        wide = push_ref.shape[0]
        link_lane = lax.broadcasted_iota(jnp.int32, (1, wide), 1)
        tail = (link_lane - pairs) // 4
        entry = jnp.where(link_lane < pairs, link_lane // 8, jnp.where(tail < rows * NNZ, tail, -1))
        links = jnp.full((1, wide), -1, jnp.int32)
        for r in range(rows):
            scale_ref[r * 8:r * 8 + 8, :] = jnp.full((8, BLK), penalty * active_ref[0, 0, r].astype(F32))
            for k in range(NNZ):
                links = jnp.where(entry == r * NNZ + k, link(r, k), links)
        out_row = lax.broadcasted_iota(jnp.int32, (n_zone * CAP * 4, wide), 0)
        out_lane = lax.broadcasted_iota(jnp.int32, (n_zone * CAP * 4, wide), 1)
        hit = (out_row // 4 == links) & (lax.rem(out_row, 4) == lax.rem(out_lane, 4))
        spread_ref[...] = jnp.where(hit, 1.0, 0.0).astype(BF16)
        back_ref[...] = jnp.zeros_like(back_ref)
        push_ref[...] = jnp.zeros_like(push_ref)
        u_ref[...] = jnp.zeros_like(u_ref)
        lu_ref[...] = jnp.zeros_like(lu_ref)
        for b in range(halves):
            flag = jnp.transpose(jnp.broadcast_to(flags_ref[b:b + 1, :], (height, BLK)))
            hard_ref[b] = jnp.where(flag == 1, plastic_hardening, 1.0).astype(F32)
        fetches[6].wait()
        lax.fori_loop(0, rows, split, 0)

    pl.semaphore_wait(barrier, devices - 1)

    def remote(src, dst, send, recv, target):
        return pltpu.make_async_remote_copy(
            src_ref=src, dst_ref=dst, send_sem=send, recv_sem=recv, device_id=target
        )

    def await_bytes(ref, sem):
        pltpu.make_async_copy(ref, ref, sem).wait()

    def slots_of(z):
        return pl.ds(z * CAP, CAP)

    def group_rows(g):
        return pl.ds(pl.multiple_of(PAD + g * 8, 8), 8)

    def tile_rows(g):
        return pl.ds(pl.multiple_of(g * 8, 8), 8)

    def over_tiles(body, init):
        def group(g, carry):
            for c in range(comps):
                for b in range(halves):
                    carry = body(c, b, group_rows(g), tile_rows(g), carry)
            return carry

        return lax.fori_loop(0, groups, group, init, unroll=2)

    def send_surface(j, n):
        it = n * KRY + j
        for c in range(comps):
            for b in range(halves):
                surf_ref[pl.ds(b * 8 + c, SROWS, stride=8 * halves), :] = x_ref[j, c, b, PAD:PAD + SROWS, :]
        for m in range(blocks):
            block_ref[m] = surf_ref[m * 8:m * 8 + 8, :]
        for step in (4, 3, 5, 2, 6, 1, 7, 0):
            z = at_zone(step)
            for k in range(CAP):
                block = block_ref[pack_tab[z * CAP + k]][0:4]
                if step:
                    fsend[it, step, k] = block
                else:
                    frecv[j][n, zone * CAP + k] = block
            if step:
                remote(
                    fsend.at[it, step], frecv[j].at[n, slots_of(zone)], fs.at[it], fr.at[it], {"zone": z}
                ).start()

    def send_row(j, it, end):
        at = PAD + (height - 1 if end else 0)
        for c in range(comps):
            for b in range(halves):
                i = c * halves + b
                rsend[it, end, i:i + 1, :] = x_ref[j, c, b, at:at + 1, :]
        target = at_vol(1 if end else n_vol - 1)
        remote(
            rsend.at[it, end], rrecv.at[it, 1 - end], rs.at[it, end], rr.at[it, 1 - end], {"vol": target}
        ).start()

    def send_strips(j, it):
        for end, b, column in ((0, 0, 0), (1, halves - 1, BLK - 1)):
            strip = zero
            for c in range(comps):
                for g in range(groups):
                    tile = x_ref[j, c, b, PAD + g * 8:PAD + g * 8 + 8, :]
                    strip = jnp.where(
                        lane == c * groups + g, jnp.broadcast_to(tile[:, column:column + 1], (8, BLK)), strip
                    )
            csend[it, end] = strip
        remote(csend.at[it, 0], crecv.at[it, 1], cs.at[it], cr.at[it], {"zone": at_zone(n_zone - 1)}).start()
        remote(csend.at[it, 1], crecv.at[it, 0], cs.at[it], cr.at[it], {"zone": at_zone(1)}).start()

    def take_row(j, it, end):
        await_bytes(rrecv.at[it, end], rr.at[it, end])
        halo_ref[j, end] = jnp.where(vol == (n_vol - 1 if end else 0), 0.0, rrecv[it, end])

    def take_strips(j, it):
        await_bytes(crecv.at[it], cr.at[it])
        halo_ref[j, 2] = jnp.where(zone == 0, 0.0, crecv[it, 0])
        halo_ref[j, 3] = jnp.where(zone == n_zone - 1, 0.0, crecv[it, 1])

    def apply_row(field, offset, end, halo):
        at = offset + (height - 1 if end else 0)
        for c in range(comps):
            for b in range(halves):
                i = c * halves + b
                field[c, b, at:at + 1, :] = field[c, b, at:at + 1, :] - halo[i:i + 1]

    def apply_strips(field, offset, left, right, chosen):
        for halo, b, column in ((left, 0, 0), (right, halves - 1, BLK - 1)):
            for c in range(comps):
                for g in chosen:
                    i = c * groups + g
                    at = slice(offset + g * 8, offset + g * 8 + 8)
                    spread = jnp.broadcast_to(halo[:, i:i + 1], (8, BLK))
                    image = field[c, b, at, :]
                    field[c, b, at, :] = jnp.where(lane == column, image - spread, image)

    def inner(j):
        def group(g, _):
            for c in range(comps):
                tiles = [x_ref[j, c, b, group_rows(g), :] for b in range(halves)]
                to_right = [pltpu.roll(tile, 1, axis=1) for tile in tiles]
                to_left = [pltpu.roll(tile, BLK - 1, axis=1) for tile in tiles]
                for b in range(halves):
                    before = to_right[b - 1] if b > 0 else zero
                    after = to_left[b + 1] if b < halves - 1 else zero
                    left = jnp.where(lane == 0, before, to_right[b])
                    right = jnp.where(lane == BLK - 1, after, to_left[b])
                    over = x_ref[j, c, b, pl.ds(PAD + g * 8 - 1, 8), :]
                    under = x_ref[j, c, b, pl.ds(PAD + g * 8 + 1, 8), :]
                    l_ref[j, c, b, tile_rows(g), :] = 4.0 * tiles[b] - (over + under + left + right)
            return 0

        lax.fori_loop(0, groups, group, 0, unroll=2)

    def first_rows(j):
        for c in range(comps):
            for b in range(halves):
                at = slice(PAD, PAD + SROWS)
                x_ref[j + 1, c, b, at, :] = l_ref[j, c, b, 0:SROWS, :] + d_ref[c, b, 0:SROWS, :] * x_ref[j, c, b, at, :]
        field = x_ref.at[j + 1]
        apply_row(field, PAD, 0, halo_ref[j, 0])
        apply_strips(field, PAD, halo_ref[j, 2], halo_ref[j, 3], range(1))

    def other_rows(j):
        def group(g, _):
            for c in range(comps):
                for b in range(halves):
                    x = x_ref[j, c, b, group_rows(g), :]
                    x_ref[j + 1, c, b, group_rows(g), :] = (
                        l_ref[j, c, b, tile_rows(g), :] + d_ref[c, b, tile_rows(g), :] * x
                    )
            return 0

        lax.fori_loop(1, groups, group, 0, unroll=3)
        field = x_ref.at[j + 1]
        apply_row(field, PAD, 1, halo_ref[j, 1])
        apply_strips(field, PAD, halo_ref[j, 2], halo_ref[j, 3], range(1, groups))

    upper = lax.broadcasted_iota(jnp.int32, (8, NNZ * BLK), 0) < 4
    contract_last = (((1,), (1,)), ((), ()))

    def split_rows(piece):
        high = piece.astype(BF16).astype(F32)
        rest = piece - high
        middle = rest.astype(BF16).astype(F32)
        return jnp.concatenate([high, middle, rest - middle, jnp.zeros_like(piece)], axis=0).astype(BF16)

    def join_rows(product):
        product = product[0:8] + product[8:16]
        return product + pltpu.roll(product, 4, axis=0)

    def find_gaps(j, n):
        it = n * KRY + j
        await_bytes(frecv[j].at[n, 0:(n_zone - 1) * CAP], fr.at[it])
        for r in range(rows):
            picked = jnp.concatenate([frecv[j][n, link(r, k)] for k in range(NNZ)], axis=1)
            if j:
                picked = picked + jnp.concatenate([bsend[it - 1, link(r, k)] for k in range(NNZ)], axis=1)
            picked = split_rows(picked)
            gap = lax.dot_general(picked, mhi_ref[r], contract_last, preferred_element_type=F32)
            gap = gap + lax.dot_general(picked, mlo_ref[r], contract_last, preferred_element_type=F32)
            gap_ref[j, r * 8:r * 8 + 8, :] = join_rows(gap)

    def push_forces(j, n):
        it = n * KRY + j
        for r in range(rows):
            at = slice(r * 8, r * 8 + 8)
            multiplier = split_rows((scale_ref[at, :] * gap_ref[j, at, :])[0:4])
            force = jnp.dot(multiplier, mhi_ref[r], preferred_element_type=F32)
            force = force + jnp.dot(multiplier, mlo_ref[r], preferred_element_type=F32)
            force = join_rows(force)
            high = force.astype(BF16).astype(F32)
            rest = force - high
            middle = rest.astype(BF16).astype(F32)
            two = jnp.where(upper, high, middle)
            low = (rest - middle)[0:4]
            for k in range(NNZ):
                entry = r * NNZ + k
                part = slice(k * BLK, (k + 1) * BLK)
                push_ref[entry * 8:entry * 8 + 8, :] = two[:, part]
                to = rows * NNZ * 8 + entry * 4
                push_ref[to:to + 4, :] = low[:, part]
        summed = jnp.dot(spread_ref[...], push_ref[...].astype(BF16), preferred_element_type=F32)
        bsend[it] = summed.reshape(n_zone * CAP, 4, BLK)
        for step in (4, 3, 5, 2, 6, 1, 7):
            z = at_zone(step)
            remote(
                bsend.at[it, slots_of(z)], brecv[j].at[n, slots_of(zone)], bs.at[it], br.at[it], {"zone": z}
            ).start()
        brecv[j][n, slots_of(zone)] = bsend[it, slots_of(zone)]

    def receive_forces(j, n):
        await_bytes(brecv[j].at[n, 0:(n_zone - 1) * CAP], br.at[n * KRY + j])
        for m in range(blocks):
            back_ref[m * 8:m * 8 + 4, :] = brecv[j][n, unpack_tab[m]]
        for c in range(comps):
            for b in range(halves):
                contact_ref[j, c, b] = back_ref[pl.ds(b * 8 + c, SROWS, stride=8 * halves), :]

    def energy(gaps):
        total = zero
        for r in range(rows):
            at = slice(r * 8, r * 8 + 8)
            gap = gaps(at)
            total = total + scale_ref[at, :] * (gap * gap)
        return 0.5 * total

    def start_sums(it, gamma, delta, cross):
        parts = []
        for part in (gamma, delta, cross):
            part = part + pltpu.roll(part, 64, axis=1)
            parts.append(part + pltpu.roll(part, 32, axis=1))
        mixed = jnp.where(lane < 32, parts[0], jnp.where(lane < 64, parts[1], parts[2]))
        mixed = jnp.sum(mixed, axis=0, keepdims=True)
        me = vol * n_zone + zone
        ssend[it] = mixed
        srecv[it, me] = mixed
        for v, z in others:
            target = {"vol": at_vol(v), "zone": at_zone(z)}
            remote(ssend.at[it], srecv.at[it, me], ss.at[it], sr.at[it], target).start()

    def finish_sums(it):
        await_bytes(srecv.at[it, 0:devices - 1], sr.at[it])
        total = jnp.sum(srecv[it], axis=0)
        place = lane[0:1]
        return [
            jnp.sum(jnp.where(place // 32 == i, total, 0.0), axis=1, keepdims=True) for i in range(3)
        ]

    def full(scalar):
        return jnp.broadcast_to(scalar, (8, BLK))

    def add_contact(j):
        for c in range(comps):
            for b in range(halves):
                at = slice(PAD, PAD + SROWS)
                x_ref[j + 1, c, b, at, :] = x_ref[j + 1, c, b, at, :] + contact_ref[j, c, b]

    def edges(mix):
        return 2.0 * (
            mix(lambda j, it: rsend[it + j, 0]) * mix(lambda j, it: halo_ref[j, 0])
            + mix(lambda j, it: csend[it + j, 0]) * mix(lambda j, it: halo_ref[j, 2])
        )

    def newton(n, _):
        it = n * KRY

        inner(0)
        find_gaps(0, n)
        push_forces(0, n)
        take_row(0, it, 0)
        take_strips(0, it)
        first_rows(0)
        send_surface(1, n)

        def dots0(c, b, padded, at, sums):
            x = x_ref[0, c, b, padded, :]
            q = l_ref[0, c, b, at, :] + d_ref[c, b, at, :] * x
            return sums[0] + x * x, sums[1] + x * q

        gamma, delta = over_tiles(dots0, (zero, zero))
        delta = delta + energy(lambda at: gap_ref[0, at, :]) - edges(lambda part: part(0, it))
        start_sums(it, gamma, delta, zero)
        take_row(0, it, 1)
        other_rows(0)
        send_row(1, it + 1, 1)
        receive_forces(0, n)
        add_contact(0)
        send_strips(1, it + 1)
        send_row(1, it + 1, 0)
        inner(1)
        find_gaps(1, n)
        push_forces(1, n)
        gamma0, pq0, _ = finish_sums(it)
        a0 = gamma0 / pq0
        take_row(1, it + 1, 0)
        take_strips(1, it + 1)
        first_rows(1)
        send_surface(2, n)
        w0 = full(a0)

        def dots1(c, b, padded, at, sums):
            x1 = x_ref[1, c, b, padded, :]
            r = x_ref[0, c, b, padded, :] - w0 * x1
            r_ref[c, b, at, :] = r
            q = (l_ref[0, c, b, at, :] - w0 * l_ref[1, c, b, at, :]) + d_ref[c, b, at, :] * r
            return sums[0] + r * r, sums[1] + r * q, sums[2] + r * x1

        gamma, delta, cross = over_tiles(dots1, (zero, zero, zero))
        delta = delta + energy(lambda at: gap_ref[0, at, :] - w0 * gap_ref[1, at, :])
        delta = delta - edges(lambda part: part(0, it) - w0 * part(1, it))
        start_sums(it + 1, gamma, delta, cross)
        take_row(1, it + 1, 1)
        other_rows(1)
        send_row(2, it + 2, 1)
        receive_forces(1, n)
        add_contact(1)
        send_strips(2, it + 2)
        send_row(2, it + 2, 0)
        inner(2)
        find_gaps(2, n)
        gamma1, delta, cross = finish_sums(it + 1)
        beta1 = gamma1 / gamma0
        pq1 = delta + beta1 * (2.0 * cross + beta1 * pq0)
        a1 = gamma1 / pq1
        take_row(2, it + 2, 0)
        take_strips(2, it + 2)
        more, w1 = full(1.0 + beta1), full(a1)

        def second(x0, x1, x2):
            return (x0 - w0 * x1) - w1 * (more * x1 - w0 * x2)

        def dots2(c, b, padded, at, sums):
            image = more * x_ref[1, c, b, padded, :] - w0 * x_ref[2, c, b, padded, :]
            r = r_ref[c, b, at, :] - w1 * image
            q = second(l_ref[0, c, b, at, :], l_ref[1, c, b, at, :], l_ref[2, c, b, at, :])
            q = q + d_ref[c, b, at, :] * r
            return sums[0] + r * r, sums[1] + r * q, sums[2] + r * image

        gamma, delta, cross = over_tiles(dots2, (zero, zero, zero))
        delta = delta + energy(lambda at: second(gap_ref[0, at, :], gap_ref[1, at, :], gap_ref[2, at, :]))
        delta = delta - edges(lambda part: second(part(0, it), part(1, it), part(2, it)))
        start_sums(it + 2, gamma, delta, cross)
        push_forces(2, n)
        take_row(2, it + 2, 1)
        receive_forces(2, n)
        gamma2, delta, cross = finish_sums(it + 2)
        beta2 = gamma2 / gamma1
        pq2 = delta + beta2 * (2.0 * cross + beta2 * pq1)
        a2 = gamma2 / pq2
        turned = beta2 * (1.0 + beta1)
        k0 = full(a0 + a1 * (1.0 + beta1) + a2 * (1.0 + turned))
        k1 = full(-(a1 * a0 + a2 * (a0 + a1 * (1.0 + beta1) + beta2 * a0)))
        k2 = full(a2 * a1 * a0)

        def mix(fields):
            return k0 * fields(0) + k1 * fields(1) + k2 * fields(2)

        for c in range(comps):
            for b in range(halves):
                lu_ref[c, b, 0:SROWS, :] = lu_ref[c, b, 0:SROWS, :] + mix(lambda j: contact_ref[j, c, b])
        over, under, left, right = [mix(lambda j: halo_ref[j, i]) for i in range(4)]
        apply_row(lu_ref, 0, 0, over)
        apply_strips(lu_ref, 0, left, right, range(1))

        def finish(g, _):
            at = tile_rows(g)
            for b in range(halves):
                half = slice(b * BLK, (b + 1) * BLK)
                stiff, hard = stiff_ref[at, half], hard_ref[b, at, :]
                for c in range(comps):
                    u = u_ref[c, at, half] + mix(lambda j: x_ref[j, c, b, group_rows(g), :])
                    image = lu_ref[c, b, at, :] + mix(lambda j: l_ref[j, c, b, at, :])
                    bent = jnp.tanh(u / yield_scale)
                    material = stiff * (hard * u + (1.0 - hard) * yield_scale * bent)
                    residual = image + material - load_ref[c, at, half]
                    u_ref[c, at, half] = u
                    res_ref[c, at, half] = residual
                    lu_ref[c, b, at, :] = image
                    x_ref[0, c, b, group_rows(g), :] = -residual
                    d_ref[c, b, at, :] = stiff * (hard + (1.0 - hard) * (1.0 - bent * bent))
            return 0

        finish(0, 0)

        @pl.when(n < NEWTON - 1)
        def _():
            send_surface(0, n + 1)

        apply_row(lu_ref, 0, 1, under)
        apply_strips(lu_ref, 0, left, right, range(1, groups))
        lax.fori_loop(1, groups, finish, 0)

        @pl.when(n < NEWTON - 1)
        def _():
            send_outline(it + KRY)

        return 0

    def send_outline(it):
        send_row(0, it, 1)
        send_row(0, it, 0)
        send_strips(0, it)

    send_surface(0, 0)
    send_outline(0)
    set_up()
    lax.fori_loop(0, NEWTON, newton, 0)

    def drain(it, _):
        await_bytes(fsend.at[it, 0:n_zone - 1], fs.at[it])
        await_bytes(bsend.at[it, 0:(n_zone - 1) * CAP], bs.at[it])
        for end in range(2):
            await_bytes(rsend.at[it, end], rs.at[it, end])
        await_bytes(csend.at[it], cs.at[it])
        await_bytes(srecv.at[it, 0:devices - 1], ss.at[it])
        return 0

    lax.fori_loop(0, STEPS, drain, 0)


def local(n_vol, n_zone, load, support_stiffness, plastic_flags, owner_map, pattern, active, mortar):
    comps, height, breadth = load.shape
    halves = breadth // BLK
    rows = active.shape[2]
    field = pltpu.VMEM((comps, halves, height, BLK), F32)
    slots = n_zone * CAP
    landing = pltpu.VMEM((NEWTON, slots, 4, BLK), F32)
    blocks = SROWS * halves
    devices = n_vol * n_zone
    wide = -(-rows * NNZ * 12 // BLK) * BLK
    dma = pltpu.SemaphoreType.DMA
    vmem = pl.BlockSpec(memory_space=pltpu.VMEM)
    hbm = pl.BlockSpec(memory_space=pltpu.HBM)
    flags = plastic_flags.T
    links = jnp.transpose(pattern, (0, 3, 1, 2))
    operands = (load, support_stiffness, flags, owner_map, links, active, mortar)
    return pl.pallas_call(
        functools.partial(kernel, n_vol, n_zone),
        out_shape=[jax.ShapeDtypeStruct(load.shape, F32)] * 2,
        in_specs=[hbm] * 7,
        out_specs=[vmem, vmem],
        scratch_shapes=[
            pltpu.VMEM(load.shape, F32),
            pltpu.VMEM(support_stiffness.shape, F32),
            pltpu.VMEM(flags.shape, jnp.int32),
            pltpu.SMEM(owner_map.shape, jnp.int32),
            pltpu.SMEM(links.shape, jnp.int32),
            pltpu.SMEM(active.shape, jnp.int32),
            pltpu.VMEM(mortar.shape[2:], F32),
            pltpu.VMEM((KRY, comps, halves, height + 2 * PAD, BLK), F32),
            pltpu.VMEM((KRY, comps, halves, height, BLK), F32),
            field, field, field,
            pltpu.VMEM((halves, height, BLK), F32),
            pltpu.VMEM((KRY, comps, halves, SROWS, BLK), F32),
            pltpu.VMEM((KRY, 4, 8, BLK), F32),
            pltpu.VMEM((KRY, rows * 8, BLK), F32),
            pltpu.VMEM((rows * 8, BLK), F32),
            pltpu.VMEM((rows, BLK, NNZ * BLK), BF16),
            pltpu.VMEM((rows, BLK, NNZ * BLK), BF16),
            pltpu.VMEM((slots * 4, wide), BF16),
            pltpu.VMEM((wide, BLK), F32),
            pltpu.VMEM((blocks * 8, BLK), F32),
            pltpu.VMEM((blocks + 1, 8, BLK), F32),
            pltpu.VMEM((blocks * 8, BLK), F32),
            pltpu.SMEM((slots,), jnp.int32),
            pltpu.SMEM((blocks,), jnp.int32),
            pltpu.VMEM((STEPS, n_zone, CAP, 4, BLK), F32),
            landing, landing, landing,
            pltpu.VMEM((STEPS, slots, 4, BLK), F32),
            landing, landing, landing,
            pltpu.VMEM((STEPS, 2, 8, BLK), F32),
            pltpu.VMEM((STEPS, 2, 8, BLK), F32),
            pltpu.VMEM((STEPS, 2, 8, BLK), F32),
            pltpu.VMEM((STEPS, 2, 8, BLK), F32),
            pltpu.VMEM((STEPS, 1, BLK), F32),
            pltpu.VMEM((STEPS, devices, 1, BLK), F32),
            dma((7,)),
        ] + [dma((STEPS,))] * 4 + [dma((STEPS, 2))] * 2 + [dma((STEPS,))] * 4,
        compiler_params=pltpu.CompilerParams(
            collective_id=0, has_side_effects=True, vmem_limit_bytes=32 * 1024 * 1024
        ),
    )(*[pltpu.with_memory_space_constraint(a, pltpu.HBM) for a in operands])


def solution(mesh):
    in_specs = (
        P(None, "vol", "zone"),
        P("vol", "zone"),
        P("vol", "zone"),
        P("vol", "zone", None),
        P("vol", "zone", None, None),
        P("vol", "zone", None),
        P("vol", "zone", None, None, None, None),
    )
    out_specs = (P(None, "vol", "zone"), P(None, "vol", "zone"))
    body = functools.partial(local, mesh.shape["vol"], mesh.shape["zone"])
    return jax.shard_map(body, mesh=mesh, in_specs=in_specs, out_specs=out_specs, check_vma=False)
```

```python
import functools

import jax
import jax.numpy as jnp
from jax import lax
from jax.experimental import pallas as pl
from jax.experimental.pallas import tpu as pltpu
from jax.sharding import PartitionSpec as P

SROWS = 8
BLK = 128
NNZ = 3
CAP = 4
KRY = 3
NEWTON = 2
STEPS = KRY * NEWTON
PAD = 8

yield_scale = 0.5
penalty = 2.0
plastic_hardening = 0.2

F32 = jnp.float32
BF16 = jnp.bfloat16


def kernel(
    n_vol, n_zone,
    load_hbm, stiff_hbm, flags_hbm, owner_hbm, pattern_hbm, active_hbm, mortar_ref,
    u_ref, res_ref,
    load_ref, stiff_ref, flags_ref, owner_ref, pattern_ref, active_ref, mort_ref,
    x_ref, l_ref, r_ref, d_ref, lu_ref, hard_ref, contact_ref, halo_ref, gap_ref, scale_ref,
    mhi_ref, mlo_ref, spread_ref, push_ref,
    surf_ref, block_ref, back_ref,
    pack_tab, unpack_tab,
    fsend, frecv0, frecv1, frecv2, bsend, brecv0, brecv1, brecv2, rsend, rrecv, csend, crecv, ssend, srecv,
    here, in_sem, fs, fr, bs, br, rs, rr, cs, cr, ss, sr,
):
    frecv, brecv = (frecv0, frecv1, frecv2), (brecv0, brecv1, brecv2)
    comps, height = load_ref.shape[0], load_ref.shape[1]
    halves = load_ref.shape[2] // BLK
    groups = height // 8
    blocks = SROWS * halves
    rows = active_ref.shape[2]
    devices = n_vol * n_zone
    zone = lax.axis_index("zone")
    vol = lax.axis_index("vol")

    inputs = [
        (owner_hbm, owner_ref), (pattern_hbm, pattern_ref), (active_hbm, active_ref), (flags_hbm, flags_ref),
        (load_hbm, load_ref), (stiff_hbm, stiff_ref), (mortar_ref.at[0, 0], mort_ref),
    ]
    fetches = [pltpu.make_async_copy(src, dst, in_sem.at[i]) for i, (src, dst) in enumerate(inputs)]
    for fetch in fetches:
        fetch.start()

    def at_zone(step):
        return lax.rem(zone + step, n_zone) if step else zone

    def at_vol(step):
        return lax.rem(vol + step, n_vol) if step else vol

    side = 4

    def hops(offset):
        around = [offset[0] // side, offset[0] % side, (offset[1] + 1) // 2]
        return sum(min(a % side, side - a % side) for a in around)

    others = [(v, z) for v in range(n_vol) for z in range(n_zone) if (v, z) != (0, 0)]
    others.sort(key=lambda offset: -hops(offset))

    barrier = pltpu.get_barrier_semaphore()
    for v in (10, 9, 11, 6, 14, 8, 2, 5, 7, 13, 15, 4, 12, 1, 3):
        pl.semaphore_signal(barrier, inc=1, device_id={"vol": at_vol(v)})
    for z in (4, 3, 5, 2, 6, 1, 7):
        pl.semaphore_signal(barrier, inc=1, device_id={"zone": at_zone(z)})

    sub = lax.broadcasted_iota(jnp.int32, (8, BLK), 0)
    lane = lax.broadcasted_iota(jnp.int32, (8, BLK), 1)
    zero = jnp.zeros((8, BLK), F32)

    for fetch in fetches[:4]:
        fetch.wait()
    owners = [owner_ref[0, 0, m] for m in range(blocks)]
    weights = []
    for m in range(blocks):
        weight, rank = jnp.int32(1), jnp.int32(0)
        for e in range(m):
            same = owners[e] == owners[m]
            weight = jnp.where(same, weight * 32, weight)
            rank = rank + jnp.where(same, 1, 0)
        weights.append(weight)
        unpack_tab[m] = owners[m] * CAP + rank
    for z in range(n_zone):
        code = jnp.int32(0)
        for m in range(blocks):
            code = code + jnp.where(owners[m] == z, weights[m] * (blocks + m), 0)
        for k in range(CAP):
            field = lax.shift_right_logical(code, 5 * k) & 31
            pack_tab[z * CAP + k] = jnp.where(field >= blocks, field - blocks, blocks)

    def link(r, k):
        return pattern_ref[0, k, 0, r]

    surf_ref[...] = jnp.zeros_like(surf_ref)
    block_ref[blocks] = zero
    rsend[...] = jnp.zeros_like(rsend)
    for fetch in fetches[4:6]:
        fetch.wait()
    for c in range(comps):
        for b in range(halves):
            for j in range(KRY):
                x_ref[j, c, b, 0:PAD, :] = jnp.zeros((PAD, BLK), F32)
                x_ref[j, c, b, PAD + height:, :] = jnp.zeros((PAD, BLK), F32)
            x_ref[0, c, b, PAD:PAD + height, :] = load_ref[c, :, b * BLK:(b + 1) * BLK]
            d_ref[c, b] = stiff_ref[:, b * BLK:(b + 1) * BLK]

    def split(r, _):
        for k in range(NNZ):
            piece = mort_ref[r, k] if k == 0 else -mort_ref[r, k]
            high = piece.astype(BF16)
            mhi_ref[r, :, k * BLK:(k + 1) * BLK] = high
            mlo_ref[r, :, k * BLK:(k + 1) * BLK] = (piece - high.astype(F32)).astype(BF16)
        return 0

    def set_up():
        pairs = rows * NNZ * 8
        wide = push_ref.shape[0]
        link_lane = lax.broadcasted_iota(jnp.int32, (1, wide), 1)
        tail = (link_lane - pairs) // 4
        entry = jnp.where(link_lane < pairs, link_lane // 8, jnp.where(tail < rows * NNZ, tail, -1))
        links = jnp.full((1, wide), -1, jnp.int32)
        for r in range(rows):
            scale_ref[r * 8:r * 8 + 8, :] = jnp.full((8, BLK), penalty * active_ref[0, 0, r].astype(F32))
            for k in range(NNZ):
                links = jnp.where(entry == r * NNZ + k, link(r, k), links)
        out_row = lax.broadcasted_iota(jnp.int32, (n_zone * CAP * 4, wide), 0)
        out_lane = lax.broadcasted_iota(jnp.int32, (n_zone * CAP * 4, wide), 1)
        hit = (out_row // 4 == links) & (lax.rem(out_row, 4) == lax.rem(out_lane, 4))
        spread_ref[...] = jnp.where(hit, 1.0, 0.0).astype(BF16)
        back_ref[...] = jnp.zeros_like(back_ref)
        push_ref[...] = jnp.zeros_like(push_ref)
        u_ref[...] = jnp.zeros_like(u_ref)
        lu_ref[...] = jnp.zeros_like(lu_ref)
        for b in range(halves):
            flag = jnp.transpose(jnp.broadcast_to(flags_ref[b:b + 1, :], (height, BLK)))
            hard_ref[b] = jnp.where(flag == 1, plastic_hardening, 1.0).astype(F32)
        fetches[6].wait()
        lax.fori_loop(0, rows, split, 0)

    pl.semaphore_wait(barrier, n_vol - 1 + n_zone - 1)
    for v in range(1, n_vol):
        pl.semaphore_signal(here, inc=1, device_id={"vol": at_vol(v)})

    def remote(src, dst, send, recv, target):
        return pltpu.make_async_remote_copy(
            src_ref=src, dst_ref=dst, send_sem=send, recv_sem=recv, device_id=target
        )

    def await_bytes(ref, sem):
        pltpu.make_async_copy(ref, ref, sem).wait()

    def slots_of(z):
        return pl.ds(z * CAP, CAP)

    def group_rows(g):
        return pl.ds(pl.multiple_of(PAD + g * 8, 8), 8)

    def tile_rows(g):
        return pl.ds(pl.multiple_of(g * 8, 8), 8)

    def over_tiles(body, init):
        def group(g, carry):
            for c in range(comps):
                for b in range(halves):
                    carry = body(c, b, group_rows(g), tile_rows(g), carry)
            return carry

        return lax.fori_loop(0, groups, group, init, unroll=2)

    def send_surface(j, n):
        it = n * KRY + j
        for c in range(comps):
            for b in range(halves):
                surf_ref[pl.ds(b * 8 + c, SROWS, stride=8 * halves), :] = x_ref[j, c, b, PAD:PAD + SROWS, :]
        for m in range(blocks):
            block_ref[m] = surf_ref[m * 8:m * 8 + 8, :]
        for step in (4, 3, 5, 2, 6, 1, 7, 0):
            z = at_zone(step)
            for k in range(CAP):
                block = block_ref[pack_tab[z * CAP + k]][0:4]
                if step:
                    fsend[it, step, k] = block
                else:
                    frecv[j][n, zone * CAP + k] = block
            if step:
                remote(
                    fsend.at[it, step], frecv[j].at[n, slots_of(zone)], fs.at[it], fr.at[it], {"zone": z}
                ).start()

    def send_row(j, it, end):
        at = PAD + (height - 1 if end else 0)
        for c in range(comps):
            for b in range(halves):
                i = c * halves + b
                rsend[it, end, i:i + 1, :] = x_ref[j, c, b, at:at + 1, :]
        target = at_vol(1 if end else n_vol - 1)
        remote(
            rsend.at[it, end], rrecv.at[it, 1 - end], rs.at[it, end], rr.at[it, 1 - end], {"vol": target}
        ).start()

    def pack_strips(j, it, chosen, strips):
        for end, b, column in ((0, 0, 0), (1, halves - 1, BLK - 1)):
            strip = strips(end)
            for c in range(comps):
                for g in chosen:
                    tile = x_ref[j, c, b, PAD + g * 8:PAD + g * 8 + 8, :]
                    strip = jnp.where(
                        lane == c * groups + g, jnp.broadcast_to(tile[:, column:column + 1], (8, BLK)), strip
                    )
            csend[it, end] = strip

    def send_strips(j, it):
        pack_strips(j, it, range(1), lambda end: csend[it, end])
        remote(csend.at[it, 0], crecv.at[it, 1], cs.at[it], cr.at[it], {"zone": at_zone(n_zone - 1)}).start()
        remote(csend.at[it, 1], crecv.at[it, 0], cs.at[it], cr.at[it], {"zone": at_zone(1)}).start()

    def take_row(j, it, end):
        await_bytes(rrecv.at[it, end], rr.at[it, end])
        halo_ref[j, end] = jnp.where(vol == (n_vol - 1 if end else 0), 0.0, rrecv[it, end])

    def take_strips(j, it):
        await_bytes(crecv.at[it], cr.at[it])
        halo_ref[j, 2] = jnp.where(zone == 0, 0.0, crecv[it, 0])
        halo_ref[j, 3] = jnp.where(zone == n_zone - 1, 0.0, crecv[it, 1])

    def apply_row(field, offset, end, halo):
        at = offset + (height - 1 if end else 0)
        for c in range(comps):
            for b in range(halves):
                i = c * halves + b
                field[c, b, at:at + 1, :] = field[c, b, at:at + 1, :] - halo[i:i + 1]

    def apply_strips(field, offset, left, right, chosen):
        for halo, b, column in ((left, 0, 0), (right, halves - 1, BLK - 1)):
            for c in range(comps):
                for g in chosen:
                    i = c * groups + g
                    at = slice(offset + g * 8, offset + g * 8 + 8)
                    spread = jnp.broadcast_to(halo[:, i:i + 1], (8, BLK))
                    image = field[c, b, at, :]
                    field[c, b, at, :] = jnp.where(lane == column, image - spread, image)

    def inner(j):
        def group(g, _):
            for c in range(comps):
                tiles = [x_ref[j, c, b, group_rows(g), :] for b in range(halves)]
                to_right = [pltpu.roll(tile, 1, axis=1) for tile in tiles]
                to_left = [pltpu.roll(tile, BLK - 1, axis=1) for tile in tiles]
                for b in range(halves):
                    before = to_right[b - 1] if b > 0 else zero
                    after = to_left[b + 1] if b < halves - 1 else zero
                    left = jnp.where(lane == 0, before, to_right[b])
                    right = jnp.where(lane == BLK - 1, after, to_left[b])
                    over = x_ref[j, c, b, pl.ds(PAD + g * 8 - 1, 8), :]
                    under = x_ref[j, c, b, pl.ds(PAD + g * 8 + 1, 8), :]
                    l_ref[j, c, b, tile_rows(g), :] = 4.0 * tiles[b] - (over + under + left + right)
            return 0

        lax.fori_loop(0, groups, group, 0, unroll=2)

    def first_rows(j):
        for c in range(comps):
            for b in range(halves):
                at = slice(PAD, PAD + SROWS)
                x_ref[j + 1, c, b, at, :] = l_ref[j, c, b, 0:SROWS, :] + d_ref[c, b, 0:SROWS, :] * x_ref[j, c, b, at, :]
        field = x_ref.at[j + 1]
        apply_row(field, PAD, 0, halo_ref[j, 0])
        apply_strips(field, PAD, halo_ref[j, 2], halo_ref[j, 3], range(1))

    def other_rows(j):
        def group(g, _):
            for c in range(comps):
                for b in range(halves):
                    x = x_ref[j, c, b, group_rows(g), :]
                    x_ref[j + 1, c, b, group_rows(g), :] = (
                        l_ref[j, c, b, tile_rows(g), :] + d_ref[c, b, tile_rows(g), :] * x
                    )
            return 0

        lax.fori_loop(1, groups, group, 0, unroll=3)
        field = x_ref.at[j + 1]
        apply_row(field, PAD, 1, halo_ref[j, 1])
        apply_strips(field, PAD, halo_ref[j, 2], halo_ref[j, 3], range(1, groups))

    upper = lax.broadcasted_iota(jnp.int32, (8, NNZ * BLK), 0) < 4
    contract_last = (((1,), (1,)), ((), ()))

    def split_rows(piece):
        high = piece.astype(BF16).astype(F32)
        rest = piece - high
        middle = rest.astype(BF16).astype(F32)
        return jnp.concatenate([high, middle, rest - middle, jnp.zeros_like(piece)], axis=0).astype(BF16)

    def join_rows(product):
        product = product[0:8] + product[8:16]
        return product + pltpu.roll(product, 4, axis=0)

    def find_gaps(j, n):
        it = n * KRY + j
        await_bytes(frecv[j].at[n, 0:(n_zone - 1) * CAP], fr.at[it])
        for r in range(rows):
            picked = jnp.concatenate([frecv[j][n, link(r, k)] for k in range(NNZ)], axis=1)
            if j:
                picked = picked + jnp.concatenate([bsend[it - 1, link(r, k)] for k in range(NNZ)], axis=1)
            picked = split_rows(picked)
            gap = lax.dot_general(picked, mhi_ref[r], contract_last, preferred_element_type=F32)
            gap = gap + lax.dot_general(picked, mlo_ref[r], contract_last, preferred_element_type=F32)
            gap_ref[j, r * 8:r * 8 + 8, :] = join_rows(gap)

    def push_forces(j, n):
        it = n * KRY + j
        for r in range(rows):
            at = slice(r * 8, r * 8 + 8)
            multiplier = split_rows((scale_ref[at, :] * gap_ref[j, at, :])[0:4])
            force = jnp.dot(multiplier, mhi_ref[r], preferred_element_type=F32)
            force = force + jnp.dot(multiplier, mlo_ref[r], preferred_element_type=F32)
            force = join_rows(force)
            high = force.astype(BF16).astype(F32)
            rest = force - high
            middle = rest.astype(BF16).astype(F32)
            two = jnp.where(upper, high, middle)
            low = (rest - middle)[0:4]
            for k in range(NNZ):
                entry = r * NNZ + k
                part = slice(k * BLK, (k + 1) * BLK)
                push_ref[entry * 8:entry * 8 + 8, :] = two[:, part]
                to = rows * NNZ * 8 + entry * 4
                push_ref[to:to + 4, :] = low[:, part]
        summed = jnp.dot(spread_ref[...], push_ref[...].astype(BF16), preferred_element_type=F32)
        bsend[it] = summed.reshape(n_zone * CAP, 4, BLK)
        for step in (4, 3, 5, 2, 6, 1, 7):
            z = at_zone(step)
            remote(
                bsend.at[it, slots_of(z)], brecv[j].at[n, slots_of(zone)], bs.at[it], br.at[it], {"zone": z}
            ).start()
        brecv[j][n, slots_of(zone)] = bsend[it, slots_of(zone)]

    def receive_forces(j, n):
        await_bytes(brecv[j].at[n, 0:(n_zone - 1) * CAP], br.at[n * KRY + j])
        for m in range(blocks):
            back_ref[m * 8:m * 8 + 4, :] = brecv[j][n, unpack_tab[m]]
        for c in range(comps):
            for b in range(halves):
                contact_ref[j, c, b] = back_ref[pl.ds(b * 8 + c, SROWS, stride=8 * halves), :]

    def energy(gaps):
        total = zero
        for r in range(rows):
            at = slice(r * 8, r * 8 + 8)
            gap = gaps(at)
            total = total + scale_ref[at, :] * (gap * gap)
        return 0.5 * total

    def start_sums(it, gamma, delta, cross):
        parts = []
        for part in (gamma, delta, cross):
            part = part + pltpu.roll(part, 64, axis=1)
            parts.append(part + pltpu.roll(part, 32, axis=1))
        mixed = jnp.where(lane < 32, parts[0], jnp.where(lane < 64, parts[1], parts[2]))
        mixed = jnp.sum(mixed, axis=0, keepdims=True)
        me = vol * n_zone + zone
        ssend[it] = mixed
        srecv[it, me] = mixed
        for v, z in others:
            target = {"vol": at_vol(v), "zone": at_zone(z)}
            remote(ssend.at[it], srecv.at[it, me], ss.at[it], sr.at[it], target).start()

    def finish_sums(it):
        await_bytes(srecv.at[it, 0:devices - 1], sr.at[it])
        total = srecv[it]
        while total.shape[0] > 1:
            half = total.shape[0] // 2
            total = total[:half] + total[half:]
        total = total[0]
        place = lane[0:1]
        return [
            jnp.sum(jnp.where(place // 32 == i, total, 0.0), axis=1, keepdims=True) for i in range(3)
        ]

    def full(scalar):
        return jnp.broadcast_to(scalar, (8, BLK))

    def add_contact(j):
        for c in range(comps):
            for b in range(halves):
                at = slice(PAD, PAD + SROWS)
                x_ref[j + 1, c, b, at, :] = x_ref[j + 1, c, b, at, :] + contact_ref[j, c, b]

    def edges(mix):
        return 2.0 * (
            mix(lambda j, it: rsend[it + j, 0]) * mix(lambda j, it: halo_ref[j, 0])
            + mix(lambda j, it: csend[it + j, 0]) * mix(lambda j, it: halo_ref[j, 2])
        )

    def newton(n, _):
        it = n * KRY

        inner(0)

        def dots0(c, b, padded, at, sums):
            x = x_ref[0, c, b, padded, :]
            q = l_ref[0, c, b, at, :] + d_ref[c, b, at, :] * x
            return sums[0] + x * x, sums[1] + x * q

        gamma, delta = over_tiles(dots0, (zero, zero))
        find_gaps(0, n)
        push_forces(0, n)
        take_row(0, it, 0)
        take_strips(0, it)
        delta = delta + energy(lambda at: gap_ref[0, at, :]) - edges(lambda part: part(0, it))

        @pl.when(n == 0)
        def _():
            pl.semaphore_wait(here, n_vol - 1)

        start_sums(it, gamma, delta, zero)
        first_rows(0)
        send_surface(1, n)
        take_row(0, it, 1)
        other_rows(0)
        send_row(1, it + 1, 1)
        pack_strips(1, it + 1, range(1, groups), lambda end: zero)
        receive_forces(0, n)
        add_contact(0)
        send_strips(1, it + 1)
        send_row(1, it + 1, 0)
        inner(1)
        find_gaps(1, n)
        push_forces(1, n)
        gamma0, pq0, _ = finish_sums(it)
        a0 = gamma0 / pq0
        take_row(1, it + 1, 0)
        take_strips(1, it + 1)
        first_rows(1)
        send_surface(2, n)
        w0 = full(a0)

        def dots1(c, b, padded, at, sums):
            x1 = x_ref[1, c, b, padded, :]
            r = x_ref[0, c, b, padded, :] - w0 * x1
            r_ref[c, b, at, :] = r
            q = (l_ref[0, c, b, at, :] - w0 * l_ref[1, c, b, at, :]) + d_ref[c, b, at, :] * r
            return sums[0] + r * r, sums[1] + r * q, sums[2] + r * x1

        gamma, delta, cross = over_tiles(dots1, (zero, zero, zero))
        delta = delta + energy(lambda at: gap_ref[0, at, :] - w0 * gap_ref[1, at, :])
        delta = delta - edges(lambda part: part(0, it) - w0 * part(1, it))
        start_sums(it + 1, gamma, delta, cross)
        take_row(1, it + 1, 1)
        other_rows(1)
        send_row(2, it + 2, 1)
        pack_strips(2, it + 2, range(1, groups), lambda end: zero)
        receive_forces(1, n)
        add_contact(1)
        send_strips(2, it + 2)
        send_row(2, it + 2, 0)
        inner(2)
        find_gaps(2, n)
        gamma1, delta, cross = finish_sums(it + 1)
        beta1 = gamma1 / gamma0
        pq1 = delta + beta1 * (2.0 * cross + beta1 * pq0)
        a1 = gamma1 / pq1
        take_row(2, it + 2, 0)
        take_strips(2, it + 2)
        more, w1 = full(1.0 + beta1), full(a1)

        def second(x0, x1, x2):
            return (x0 - w0 * x1) - w1 * (more * x1 - w0 * x2)

        def dots2(c, b, padded, at, sums):
            image = more * x_ref[1, c, b, padded, :] - w0 * x_ref[2, c, b, padded, :]
            r = r_ref[c, b, at, :] - w1 * image
            q = second(l_ref[0, c, b, at, :], l_ref[1, c, b, at, :], l_ref[2, c, b, at, :])
            q = q + d_ref[c, b, at, :] * r
            return sums[0] + r * r, sums[1] + r * q, sums[2] + r * image

        gamma, delta, cross = over_tiles(dots2, (zero, zero, zero))
        delta = delta + energy(lambda at: second(gap_ref[0, at, :], gap_ref[1, at, :], gap_ref[2, at, :]))
        delta = delta - edges(lambda part: second(part(0, it), part(1, it), part(2, it)))
        start_sums(it + 2, gamma, delta, cross)
        push_forces(2, n)
        take_row(2, it + 2, 1)
        receive_forces(2, n)
        gamma2, delta, cross = finish_sums(it + 2)
        beta2 = gamma2 / gamma1
        pq2 = delta + beta2 * (2.0 * cross + beta2 * pq1)
        a2 = gamma2 / pq2
        turned = beta2 * (1.0 + beta1)
        k0 = full(a0 + a1 * (1.0 + beta1) + a2 * (1.0 + turned))
        k1 = full(-(a1 * a0 + a2 * (a0 + a1 * (1.0 + beta1) + beta2 * a0)))
        k2 = full(a2 * a1 * a0)

        def mix(fields):
            return k0 * fields(0) + k1 * fields(1) + k2 * fields(2)

        for c in range(comps):
            for b in range(halves):
                lu_ref[c, b, 0:SROWS, :] = lu_ref[c, b, 0:SROWS, :] + mix(lambda j: contact_ref[j, c, b])
        over, under, left, right = [mix(lambda j: halo_ref[j, i]) for i in range(4)]
        apply_row(lu_ref, 0, 0, over)
        apply_strips(lu_ref, 0, left, right, range(1))

        def finish(g, _):
            at = tile_rows(g)
            for b in range(halves):
                half = slice(b * BLK, (b + 1) * BLK)
                stiff, hard = stiff_ref[at, half], hard_ref[b, at, :]
                for c in range(comps):
                    u = u_ref[c, at, half] + mix(lambda j: x_ref[j, c, b, group_rows(g), :])
                    image = lu_ref[c, b, at, :] + mix(lambda j: l_ref[j, c, b, at, :])
                    bent = jnp.tanh(u / yield_scale)
                    material = stiff * (hard * u + (1.0 - hard) * yield_scale * bent)
                    residual = image + material - load_ref[c, at, half]
                    u_ref[c, at, half] = u
                    res_ref[c, at, half] = residual
                    lu_ref[c, b, at, :] = image
                    x_ref[0, c, b, group_rows(g), :] = -residual
                    d_ref[c, b, at, :] = stiff * (hard + (1.0 - hard) * (1.0 - bent * bent))
            return 0

        finish(0, 0)

        @pl.when(n < NEWTON - 1)
        def _():
            send_surface(0, n + 1)

        apply_row(lu_ref, 0, 1, under)
        apply_strips(lu_ref, 0, left, right, range(1, groups))
        finish(groups - 1, 0)

        @pl.when(n < NEWTON - 1)
        def _():
            send_row(0, it + KRY, 1)

        lax.fori_loop(1, groups - 1, finish, 0)

        @pl.when(n < NEWTON - 1)
        def _():
            send_outline(it + KRY)

        return 0

    def send_outline(it):
        pack_strips(0, it, range(1, groups), lambda end: zero)
        send_strips(0, it)
        send_row(0, it, 0)

    send_row(0, 0, 1)
    send_surface(0, 0)
    send_outline(0)
    set_up()
    lax.fori_loop(0, NEWTON, newton, 0)

    def drain(it, _):
        await_bytes(fsend.at[it, 0:n_zone - 1], fs.at[it])
        await_bytes(bsend.at[it, 0:(n_zone - 1) * CAP], bs.at[it])
        for end in range(2):
            await_bytes(rsend.at[it, end], rs.at[it, end])
        await_bytes(csend.at[it], cs.at[it])
        await_bytes(srecv.at[it, 0:devices - 1], ss.at[it])
        return 0

    lax.fori_loop(0, STEPS, drain, 0)


def local(n_vol, n_zone, load, support_stiffness, plastic_flags, owner_map, pattern, active, mortar):
    comps, height, breadth = load.shape
    halves = breadth // BLK
    rows = active.shape[2]
    field = pltpu.VMEM((comps, halves, height, BLK), F32)
    slots = n_zone * CAP
    landing = pltpu.VMEM((NEWTON, slots, 4, BLK), F32)
    blocks = SROWS * halves
    devices = n_vol * n_zone
    wide = -(-rows * NNZ * 12 // BLK) * BLK
    dma = pltpu.SemaphoreType.DMA
    vmem = pl.BlockSpec(memory_space=pltpu.VMEM)
    hbm = pl.BlockSpec(memory_space=pltpu.HBM)
    flags = plastic_flags.T
    links = jnp.transpose(pattern, (0, 3, 1, 2))
    operands = (load, support_stiffness, flags, owner_map, links, active, mortar)
    return pl.pallas_call(
        functools.partial(kernel, n_vol, n_zone),
        out_shape=[jax.ShapeDtypeStruct(load.shape, F32)] * 2,
        in_specs=[hbm] * 7,
        out_specs=[vmem, vmem],
        scratch_shapes=[
            pltpu.VMEM(load.shape, F32),
            pltpu.VMEM(support_stiffness.shape, F32),
            pltpu.VMEM(flags.shape, jnp.int32),
            pltpu.SMEM(owner_map.shape, jnp.int32),
            pltpu.SMEM(links.shape, jnp.int32),
            pltpu.SMEM(active.shape, jnp.int32),
            pltpu.VMEM(mortar.shape[2:], F32),
            pltpu.VMEM((KRY, comps, halves, height + 2 * PAD, BLK), F32),
            pltpu.VMEM((KRY, comps, halves, height, BLK), F32),
            field, field, field,
            pltpu.VMEM((halves, height, BLK), F32),
            pltpu.VMEM((KRY, comps, halves, SROWS, BLK), F32),
            pltpu.VMEM((KRY, 4, 8, BLK), F32),
            pltpu.VMEM((KRY, rows * 8, BLK), F32),
            pltpu.VMEM((rows * 8, BLK), F32),
            pltpu.VMEM((rows, BLK, NNZ * BLK), BF16),
            pltpu.VMEM((rows, BLK, NNZ * BLK), BF16),
            pltpu.VMEM((slots * 4, wide), BF16),
            pltpu.VMEM((wide, BLK), F32),
            pltpu.VMEM((blocks * 8, BLK), F32),
            pltpu.VMEM((blocks + 1, 8, BLK), F32),
            pltpu.VMEM((blocks * 8, BLK), F32),
            pltpu.SMEM((slots,), jnp.int32),
            pltpu.SMEM((blocks,), jnp.int32),
            pltpu.VMEM((STEPS, n_zone, CAP, 4, BLK), F32),
            landing, landing, landing,
            pltpu.VMEM((STEPS, slots, 4, BLK), F32),
            landing, landing, landing,
            pltpu.VMEM((STEPS, 2, 8, BLK), F32),
            pltpu.VMEM((STEPS, 2, 8, BLK), F32),
            pltpu.VMEM((STEPS, 2, 8, BLK), F32),
            pltpu.VMEM((STEPS, 2, 8, BLK), F32),
            pltpu.VMEM((STEPS, 1, BLK), F32),
            pltpu.VMEM((STEPS, devices, 1, BLK), F32),
            pltpu.SemaphoreType.REGULAR,
            dma((7,)),
        ] + [dma((STEPS,))] * 4 + [dma((STEPS, 2))] * 2 + [dma((STEPS,))] * 4,
        compiler_params=pltpu.CompilerParams(
            collective_id=0, has_side_effects=True, vmem_limit_bytes=32 * 1024 * 1024
        ),
    )(*[pltpu.with_memory_space_constraint(a, pltpu.HBM) for a in operands])


def solution(mesh):
    in_specs = (
        P(None, "vol", "zone"),
        P("vol", "zone"),
        P("vol", "zone"),
        P("vol", "zone", None),
        P("vol", "zone", None, None),
        P("vol", "zone", None),
        P("vol", "zone", None, None, None, None),
    )
    out_specs = (P(None, "vol", "zone"), P(None, "vol", "zone"))
    body = functools.partial(local, mesh.shape["vol"], mesh.shape["zone"])
    return jax.shard_map(body, mesh=mesh, in_specs=in_specs, out_specs=out_specs, check_vma=False)
```

```python
import functools

import jax
import jax.numpy as jnp
from jax import lax
from jax.experimental import pallas as pl
from jax.experimental.pallas import tpu as pltpu
from jax.sharding import PartitionSpec as P

SROWS = 8
BLK = 128
NNZ = 3
CAP = 4
KRY = 3
NEWTON = 2
STEPS = KRY * NEWTON
PAD = 8

yield_scale = 0.5
penalty = 2.0
plastic_hardening = 0.2

F32 = jnp.float32
BF16 = jnp.bfloat16


def kernel(
    n_vol, n_zone,
    load_hbm, stiff_hbm, flags_hbm, owner_hbm, pattern_hbm, active_hbm, mortar_ref,
    u_ref, res_ref,
    load_ref, stiff_ref, flags_ref, owner_ref, pattern_ref, active_ref, mort_ref,
    x_ref, l_ref, r_ref, d_ref, lu_ref, hard_ref, contact_ref, halo_ref, own_ref, slot_ref, coef_ref, gap_ref, scale_ref,
    mhi_ref, mlo_ref, spread_ref, push_ref,
    surf_ref, block_ref, back_ref,
    pack_tab, unpack_tab,
    fsend, frecv0, frecv1, frecv2, fixed, bsend, brecv0, brecv1, brecv2, rsend, rrecv, csend, crecv, ssend, srecv,
    here, in_sem, fs, fr, bs, br, rs, rr, cs, cr, ss, sr,
):
    frecv, brecv = (frecv0, frecv1, frecv2), (brecv0, brecv1, brecv2)
    comps, height = load_ref.shape[0], load_ref.shape[1]
    halves = load_ref.shape[2] // BLK
    groups = height // 8
    blocks = SROWS * halves
    rows = active_ref.shape[2]
    devices = n_vol * n_zone
    zone = lax.axis_index("zone")
    vol = lax.axis_index("vol")

    inputs = [
        (owner_hbm, owner_ref), (pattern_hbm, pattern_ref), (active_hbm, active_ref), (flags_hbm, flags_ref),
        (load_hbm, load_ref), (stiff_hbm, stiff_ref), (mortar_ref.at[0, 0], mort_ref),
    ]
    fetches = [pltpu.make_async_copy(src, dst, in_sem.at[i]) for i, (src, dst) in enumerate(inputs)]
    for fetch in fetches:
        fetch.start()

    def at_zone(step):
        return lax.rem(zone + step, n_zone) if step else zone

    def at_vol(step):
        return lax.rem(vol + step, n_vol) if step else vol

    side = 4

    def hops(offset):
        around = [offset[0] // side, offset[0] % side, (offset[1] + 1) // 2]
        return sum(min(a % side, side - a % side) for a in around)

    others = [(v, z) for v in range(n_vol) for z in range(n_zone) if (v, z) != (0, 0)]
    others.sort(key=lambda offset: -hops(offset))

    barrier = pltpu.get_barrier_semaphore()
    for v in (10, 9, 11, 6, 14, 8, 2, 5, 7, 13, 15, 4, 12, 1, 3):
        pl.semaphore_signal(barrier, inc=1, device_id={"vol": at_vol(v)})
    for z in (4, 3, 5, 2, 6, 1, 7):
        pl.semaphore_signal(barrier, inc=1, device_id={"zone": at_zone(z)})

    sub = lax.broadcasted_iota(jnp.int32, (8, BLK), 0)
    lane = lax.broadcasted_iota(jnp.int32, (8, BLK), 1)
    zero = jnp.zeros((8, BLK), F32)

    for fetch in fetches[:4]:
        fetch.wait()
    owners = [owner_ref[0, 0, m] for m in range(blocks)]
    weights = []
    for m in range(blocks):
        weight, rank = jnp.int32(1), jnp.int32(0)
        for e in range(m):
            same = owners[e] == owners[m]
            weight = jnp.where(same, weight * 32, weight)
            rank = rank + jnp.where(same, 1, 0)
        weights.append(weight)
        unpack_tab[m] = owners[m] * CAP + rank
    for z in range(n_zone):
        code = jnp.int32(0)
        for m in range(blocks):
            code = code + jnp.where(owners[m] == z, weights[m] * (blocks + m), 0)
        for k in range(CAP):
            field = lax.shift_right_logical(code, 5 * k) & 31
            pack_tab[z * CAP + k] = jnp.where(field >= blocks, field - blocks, blocks)

    def link(r, k):
        return pattern_ref[0, k, 0, r]

    surf_ref[...] = jnp.zeros_like(surf_ref)
    block_ref[blocks] = zero
    rsend[...] = jnp.zeros_like(rsend)
    for fetch in fetches[4:6]:
        fetch.wait()
    for c in range(comps):
        for b in range(halves):
            for j in range(KRY + 1):
                x_ref[j, c, b, 0:PAD, :] = jnp.zeros((PAD, BLK), F32)
                x_ref[j, c, b, PAD + height:, :] = jnp.zeros((PAD, BLK), F32)
            x_ref[0, c, b, PAD:PAD + height, :] = load_ref[c, :, b * BLK:(b + 1) * BLK]
            d_ref[c, b] = stiff_ref[:, b * BLK:(b + 1) * BLK]

    def split(r, _):
        for k in range(NNZ):
            piece = mort_ref[r, k] if k == 0 else -mort_ref[r, k]
            high = piece.astype(BF16)
            mhi_ref[r, :, k * BLK:(k + 1) * BLK] = high
            mlo_ref[r, :, k * BLK:(k + 1) * BLK] = (piece - high.astype(F32)).astype(BF16)
        return 0

    def set_up():
        pairs = rows * NNZ * 8
        wide = push_ref.shape[0]
        link_lane = lax.broadcasted_iota(jnp.int32, (1, wide), 1)
        tail = (link_lane - pairs) // 4
        entry = jnp.where(link_lane < pairs, link_lane // 8, jnp.where(tail < rows * NNZ, tail, -1))
        links = jnp.full((1, wide), -1, jnp.int32)
        for r in range(rows):
            scale_ref[r * 8:r * 8 + 8, :] = jnp.full((8, BLK), penalty * active_ref[0, 0, r].astype(F32))
            for k in range(NNZ):
                links = jnp.where(entry == r * NNZ + k, link(r, k), links)
        out_row = lax.broadcasted_iota(jnp.int32, (n_zone * CAP * 4, wide), 0)
        out_lane = lax.broadcasted_iota(jnp.int32, (n_zone * CAP * 4, wide), 1)
        hit = (out_row // 4 == links) & (lax.rem(out_row, 4) == lax.rem(out_lane, 4))
        spread_ref[...] = jnp.where(hit, 1.0, 0.0).astype(BF16)
        back_ref[...] = jnp.zeros_like(back_ref)
        push_ref[...] = jnp.zeros_like(push_ref)
        u_ref[...] = jnp.zeros_like(u_ref)
        lu_ref[...] = jnp.zeros_like(lu_ref)
        for b in range(halves):
            flag = jnp.transpose(jnp.broadcast_to(flags_ref[b:b + 1, :], (height, BLK)))
            hard_ref[b] = jnp.where(flag == 1, plastic_hardening, 1.0).astype(F32)
        fetches[6].wait()
        lax.fori_loop(0, rows, split, 0)

    pl.semaphore_wait(barrier, n_vol - 1 + n_zone - 1)
    for v in range(1, n_vol):
        pl.semaphore_signal(here, inc=1, device_id={"vol": at_vol(v)})

    def remote(src, dst, send, recv, target):
        return pltpu.make_async_remote_copy(
            src_ref=src, dst_ref=dst, send_sem=send, recv_sem=recv, device_id=target
        )

    def await_bytes(ref, sem):
        pltpu.make_async_copy(ref, ref, sem).wait()

    def slots_of(z):
        return pl.ds(z * CAP, CAP)

    def group_rows(g):
        return pl.ds(pl.multiple_of(PAD + g * 8, 8), 8)

    def tile_rows(g):
        return pl.ds(pl.multiple_of(g * 8, 8), 8)

    def over_tiles(body, init):
        def group(g, carry):
            for c in range(comps):
                for b in range(halves):
                    carry = body(c, b, group_rows(g), tile_rows(g), carry)
            return carry

        return lax.fori_loop(0, groups, group, init, unroll=2)

    def send_surface(it, tile, landing):
        for c in range(comps):
            for b in range(halves):
                surf_ref[pl.ds(b * 8 + c, SROWS, stride=8 * halves), :] = tile(c, b)
        for m in range(blocks):
            block_ref[m] = surf_ref[m * 8:m * 8 + 8, :]
        for step in (4, 3, 5, 2, 6, 1, 7, 0):
            z = at_zone(step)
            for k in range(CAP):
                block = block_ref[pack_tab[z * CAP + k]][0:4]
                if step:
                    fsend[it, step, k] = block
                else:
                    landing[zone * CAP + k] = block
            if step:
                remote(fsend.at[it, step], landing.at[slots_of(zone)], fs.at[it], fr.at[it], {"zone": z}).start()

    def send_field(j, it, landing):
        send_surface(it, lambda c, b: x_ref[j, c, b, PAD:PAD + SROWS, :], landing)

    def send_row(j, it, end):
        at = PAD + (height - 1 if end else 0)
        for c in range(comps):
            for b in range(halves):
                i = c * halves + b
                rsend[it, end, i:i + 1, :] = x_ref[j, c, b, at:at + 1, :]
        if end == 0:
            own_ref[j, 0] = rsend[it, 0]
        ship_row(it, end)

    def ship_row(it, end):
        target = at_vol(1 if end else n_vol - 1)
        remote(
            rsend.at[it, end], rrecv.at[it, 1 - end], rs.at[it, end], rr.at[it, 1 - end], {"vol": target}
        ).start()

    def strip_of(field, end, chosen, strip):
        b, column = (halves - 1, BLK - 1) if end else (0, 0)
        for c in range(comps):
            for g in chosen:
                tile = field[c, b, PAD + g * 8:PAD + g * 8 + 8, :]
                strip = jnp.where(
                    lane == c * groups + g, jnp.broadcast_to(tile[:, column:column + 1], (8, BLK)), strip
                )
        return strip

    def pack_strips(j, it, chosen, strips):
        for end in range(2):
            csend[it, end] = strip_of(x_ref.at[j], end, chosen, strips(end))

    def send_strips(j, it):
        pack_strips(j, it, range(1), lambda end: csend[it, end])
        own_ref[j, 1] = csend[it, 0]
        ship_strips(it)

    def ship_strips(it):
        remote(csend.at[it, 0], crecv.at[it, 1], cs.at[it], cr.at[it], {"zone": at_zone(n_zone - 1)}).start()
        remote(csend.at[it, 1], crecv.at[it, 0], cs.at[it], cr.at[it], {"zone": at_zone(1)}).start()

    def take_row(j, it, end):
        await_bytes(rrecv.at[it, end], rr.at[it, end])
        halo_ref[j, end] = jnp.where(vol == (n_vol - 1 if end else 0), 0.0, rrecv[it, end])

    def take_strips(j, it):
        await_bytes(crecv.at[it], cr.at[it])
        halo_ref[j, 2] = jnp.where(zone == 0, 0.0, crecv[it, 0])
        halo_ref[j, 3] = jnp.where(zone == n_zone - 1, 0.0, crecv[it, 1])

    def apply_row(field, offset, end, halo):
        at = offset + (height - 1 if end else 0)
        for c in range(comps):
            for b in range(halves):
                i = c * halves + b
                field[c, b, at:at + 1, :] = field[c, b, at:at + 1, :] - halo[i:i + 1]

    def apply_strips(field, offset, left, right, chosen):
        for halo, b, column in ((left, 0, 0), (right, halves - 1, BLK - 1)):
            for c in range(comps):
                for g in chosen:
                    i = c * groups + g
                    at = slice(offset + g * 8, offset + g * 8 + 8)
                    spread = jnp.broadcast_to(halo[:, i:i + 1], (8, BLK))
                    image = field[c, b, at, :]
                    field[c, b, at, :] = jnp.where(lane == column, image - spread, image)

    def inner(j):
        def group(g, _):
            for c in range(comps):
                tiles = [x_ref[j, c, b, group_rows(g), :] for b in range(halves)]
                to_right = [pltpu.roll(tile, 1, axis=1) for tile in tiles]
                to_left = [pltpu.roll(tile, BLK - 1, axis=1) for tile in tiles]
                for b in range(halves):
                    before = to_right[b - 1] if b > 0 else zero
                    after = to_left[b + 1] if b < halves - 1 else zero
                    left = jnp.where(lane == 0, before, to_right[b])
                    right = jnp.where(lane == BLK - 1, after, to_left[b])
                    over = x_ref[j, c, b, pl.ds(PAD + g * 8 - 1, 8), :]
                    under = x_ref[j, c, b, pl.ds(PAD + g * 8 + 1, 8), :]
                    l_ref[j, c, b, tile_rows(g), :] = 4.0 * tiles[b] - (over + under + left + right)
            return 0

        lax.fori_loop(0, groups, group, 0, unroll=2)

    def image(j, c, b, at, padded):
        part = l_ref[j, c, b, at, :]
        return part + d_ref[c, b, at, :] * x_ref[j, c, b, padded, :] if j < KRY - 1 else part

    def first_rows(j):
        for c in range(comps):
            for b in range(halves):
                at = slice(PAD, PAD + SROWS)
                x_ref[j + 1, c, b, at, :] = image(j, c, b, slice(0, SROWS), at)
        field = x_ref.at[j + 1]
        apply_row(field, PAD, 0, halo_ref[j, 0])
        apply_strips(field, PAD, halo_ref[j, 2], halo_ref[j, 3], range(1))

    def other_rows(j):
        def group(g, _):
            for c in range(comps):
                for b in range(halves):
                    x_ref[j + 1, c, b, group_rows(g), :] = image(j, c, b, tile_rows(g), group_rows(g))
            return 0

        lax.fori_loop(1, groups, group, 0, unroll=3)
        field = x_ref.at[j + 1]
        apply_row(field, PAD, 1, halo_ref[j, 1])
        apply_strips(field, PAD, halo_ref[j, 2], halo_ref[j, 3], range(1, groups))

    upper = lax.broadcasted_iota(jnp.int32, (8, NNZ * BLK), 0) < 4
    contract_last = (((1,), (1,)), ((), ()))

    def split_rows(piece):
        high = piece.astype(BF16).astype(F32)
        rest = piece - high
        middle = rest.astype(BF16).astype(F32)
        return jnp.concatenate([high, middle, rest - middle, jnp.zeros_like(piece)], axis=0).astype(BF16)

    def join_rows(product):
        product = product[0:8] + product[8:16]
        return product + pltpu.roll(product, 4, axis=0)

    def fill_slots(j, n):
        it = n * KRY + j
        await_bytes(frecv[j].at[n, 0:(n_zone - 1) * CAP], fr.at[it])
        slot_ref[j] = frecv[j][n] + bsend[it - 1] if j else frecv[j][n]

    def find_gaps(j):
        for r in range(rows):
            picked = split_rows(jnp.concatenate([slot_ref[j, link(r, k)] for k in range(NNZ)], axis=1))
            gap = lax.dot_general(picked, mhi_ref[r], contract_last, preferred_element_type=F32)
            gap = gap + lax.dot_general(picked, mlo_ref[r], contract_last, preferred_element_type=F32)
            gap_ref[j, r * 8:r * 8 + 8, :] = join_rows(gap)

    def push_forces(j, n):
        it = n * KRY + j
        for r in range(rows):
            at = slice(r * 8, r * 8 + 8)
            multiplier = split_rows((scale_ref[at, :] * gap_ref[j, at, :])[0:4])
            force = jnp.dot(multiplier, mhi_ref[r], preferred_element_type=F32)
            force = force + jnp.dot(multiplier, mlo_ref[r], preferred_element_type=F32)
            force = join_rows(force)
            high = force.astype(BF16).astype(F32)
            rest = force - high
            middle = rest.astype(BF16).astype(F32)
            two = jnp.where(upper, high, middle)
            low = (rest - middle)[0:4]
            for k in range(NNZ):
                entry = r * NNZ + k
                part = slice(k * BLK, (k + 1) * BLK)
                push_ref[entry * 8:entry * 8 + 8, :] = two[:, part]
                to = rows * NNZ * 8 + entry * 4
                push_ref[to:to + 4, :] = low[:, part]
        summed = jnp.dot(spread_ref[...], push_ref[...].astype(BF16), preferred_element_type=F32)
        bsend[it] = summed.reshape(n_zone * CAP, 4, BLK)
        for step in (4, 3, 5, 2, 6, 1, 7):
            z = at_zone(step)
            remote(
                bsend.at[it, slots_of(z)], brecv[j].at[n, slots_of(zone)], bs.at[it], br.at[it], {"zone": z}
            ).start()
        brecv[j][n, slots_of(zone)] = bsend[it, slots_of(zone)]

    def receive_forces(j, n):
        await_bytes(brecv[j].at[n, 0:(n_zone - 1) * CAP], br.at[n * KRY + j])
        for m in range(blocks):
            back_ref[m * 8:m * 8 + 4, :] = brecv[j][n, unpack_tab[m]]
        for c in range(comps):
            for b in range(halves):
                contact_ref[j, c, b] = back_ref[pl.ds(b * 8 + c, SROWS, stride=8 * halves), :]

    def energy(gaps):
        total = zero
        for r in range(rows):
            at = slice(r * 8, r * 8 + 8)
            gap = gaps(at)
            total = total + scale_ref[at, :] * (gap * gap)
        return 0.5 * total

    def start_sums(it, gamma, delta, cross):
        parts = []
        for part in (gamma, delta, cross):
            part = part + pltpu.roll(part, 64, axis=1)
            parts.append(part + pltpu.roll(part, 32, axis=1))
        mixed = jnp.where(lane < 32, parts[0], jnp.where(lane < 64, parts[1], parts[2]))
        mixed = jnp.sum(mixed, axis=0, keepdims=True)
        me = vol * n_zone + zone
        ssend[it] = mixed
        srecv[it, me] = mixed
        for v, z in others:
            target = {"vol": at_vol(v), "zone": at_zone(z)}
            remote(ssend.at[it], srecv.at[it, me], ss.at[it], sr.at[it], target).start()

    def finish_sums(it):
        await_bytes(srecv.at[it, 0:devices - 1], sr.at[it])
        total = srecv[it]
        while total.shape[0] > 1:
            half = total.shape[0] // 2
            total = total[:half] + total[half:]
        total = total[0]
        place = lane[0:1]
        return [
            jnp.sum(jnp.where(place // 32 == i, total, 0.0), axis=1, keepdims=True) for i in range(3)
        ]

    def full(scalar):
        return jnp.broadcast_to(scalar, (8, BLK))

    def add_contact(j):
        for c in range(comps):
            for b in range(halves):
                at = slice(PAD, PAD + SROWS)
                x_ref[j + 1, c, b, at, :] = x_ref[j + 1, c, b, at, :] + contact_ref[j, c, b]

    def edges(mix):
        return 2.0 * (
            mix(lambda j: own_ref[j, 0]) * mix(lambda j: halo_ref[j, 0])
            + mix(lambda j: own_ref[j, 1]) * mix(lambda j: halo_ref[j, 2])
        )

    def newton(n, _):
        it = n * KRY

        inner(0)

        def dots0(c, b, padded, at, sums):
            x = x_ref[0, c, b, padded, :]
            q = l_ref[0, c, b, at, :] + d_ref[c, b, at, :] * x
            return sums[0] + x * x, sums[1] + x * q

        gamma, delta = over_tiles(dots0, (zero, zero))

        @pl.when(n == 0)
        def _():
            fill_slots(0, 0)
            find_gaps(0)
            push_forces(0, 0)
            take_row(0, 0, 0)
            take_strips(0, 0)

        delta = delta + energy(lambda at: gap_ref[0, at, :]) - edges(lambda part: part(0))

        @pl.when(n == 0)
        def _():
            pl.semaphore_wait(here, n_vol - 1)

        start_sums(it, gamma, delta, zero)
        first_rows(0)
        send_field(1, it + 1, frecv[1].at[n])

        @pl.when(n == 0)
        def _():
            take_row(0, 0, 1)

        @pl.when(n > 0)
        def _():
            take_row(KRY, KRY, 1)
            derive_halo(1)

        other_rows(0)
        send_row(1, it + 1, 1)
        pack_strips(1, it + 1, range(1, groups), lambda end: zero)
        receive_forces(0, n)
        add_contact(0)
        send_strips(1, it + 1)
        send_row(1, it + 1, 0)
        inner(1)
        fill_slots(1, n)
        find_gaps(1)
        push_forces(1, n)
        gamma0, pq0, _ = finish_sums(it)
        a0 = gamma0 / pq0
        take_row(1, it + 1, 0)
        take_strips(1, it + 1)
        first_rows(1)
        send_field(2, it + 2, frecv[2].at[n])
        w0 = full(a0)

        def dots1(c, b, padded, at, sums):
            x1 = x_ref[1, c, b, padded, :]
            r = x_ref[0, c, b, padded, :] - w0 * x1
            r_ref[c, b, at, :] = r
            q = (l_ref[0, c, b, at, :] - w0 * l_ref[1, c, b, at, :]) + d_ref[c, b, at, :] * r
            return sums[0] + r * r, sums[1] + r * q, sums[2] + r * x1

        gamma, delta, cross = over_tiles(dots1, (zero, zero, zero))
        delta = delta + energy(lambda at: gap_ref[0, at, :] - w0 * gap_ref[1, at, :])
        delta = delta - edges(lambda part: part(0) - w0 * part(1))
        start_sums(it + 1, gamma, delta, cross)
        take_row(1, it + 1, 1)
        other_rows(1)
        send_row(2, it + 2, 1)
        pack_strips(2, it + 2, range(1, groups), lambda end: zero)
        receive_forces(1, n)
        add_contact(1)
        send_strips(2, it + 2)
        send_row(2, it + 2, 0)
        inner(2)
        fill_slots(2, n)
        find_gaps(2)
        push_forces(2, n)
        gamma1, delta, cross = finish_sums(it + 1)
        beta1 = gamma1 / gamma0
        pq1 = delta + beta1 * (2.0 * cross + beta1 * pq0)
        a1 = gamma1 / pq1
        take_row(2, it + 2, 0)
        take_strips(2, it + 2)
        more, w1 = full(1.0 + beta1), full(a1)

        def second(x0, x1, x2):
            return (x0 - w0 * x1) - w1 * (more * x1 - w0 * x2)

        def dots2(c, b, padded, at, sums):
            image = more * x_ref[1, c, b, padded, :] - w0 * x_ref[2, c, b, padded, :]
            r = r_ref[c, b, at, :] - w1 * image
            q = second(l_ref[0, c, b, at, :], l_ref[1, c, b, at, :], l_ref[2, c, b, at, :])
            q = q + d_ref[c, b, at, :] * r
            return sums[0] + r * r, sums[1] + r * q, sums[2] + r * image

        gamma, delta, cross = over_tiles(dots2, (zero, zero, zero))
        delta = delta + energy(lambda at: second(gap_ref[0, at, :], gap_ref[1, at, :], gap_ref[2, at, :]))
        delta = delta - edges(lambda part: second(part(0), part(1), part(2)))
        start_sums(it + 2, gamma, delta, cross)

        @pl.when(n < NEWTON - 1)
        def _():
            first_rows(2)
            send_field(KRY, KRY, frecv[0].at[1])

        take_row(2, it + 2, 1)

        @pl.when(n < NEWTON - 1)
        def _():
            other_rows(2)
            send_row(KRY, KRY, 1)
            pack_strips(KRY, KRY, range(1, groups), lambda end: zero)

        receive_forces(2, n)

        @pl.when(n < NEWTON - 1)
        def _():
            add_contact(2)
            send_strips(KRY, KRY)
            send_row(KRY, KRY, 0)

        gamma2, delta, cross = finish_sums(it + 2)
        beta2 = gamma2 / gamma1
        pq2 = delta + beta2 * (2.0 * cross + beta2 * pq1)
        a2 = gamma2 / pq2
        turned = beta2 * (1.0 + beta1)
        k0 = full(a0 + a1 * (1.0 + beta1) + a2 * (1.0 + turned))
        k1 = full(-(a1 * a0 + a2 * (a0 + a1 * (1.0 + beta1) + beta2 * a0)))
        k2 = full(a2 * a1 * a0)

        coef_ref[0], coef_ref[1], coef_ref[2] = k0, k1, k2

        @pl.when(n < NEWTON - 1)
        def _():
            derive_slots()
            find_gaps(0)
            push_forces(0, 1)

        def mix(fields):
            return k0 * fields(0) + k1 * fields(1) + k2 * fields(2)

        for c in range(comps):
            for b in range(halves):
                lu_ref[c, b, 0:SROWS, :] = lu_ref[c, b, 0:SROWS, :] + mix(lambda j: contact_ref[j, c, b])
        over, under, left, right = [mix(lambda j: halo_ref[j, i]) for i in range(4)]
        apply_row(lu_ref, 0, 0, over)
        apply_strips(lu_ref, 0, left, right, range(1))

        def finish(g, _):
            at = tile_rows(g)
            for b in range(halves):
                half = slice(b * BLK, (b + 1) * BLK)
                stiff, hard = stiff_ref[at, half], hard_ref[b, at, :]
                for c in range(comps):
                    u = u_ref[c, at, half] + mix(lambda j: x_ref[j, c, b, group_rows(g), :])
                    image = lu_ref[c, b, at, :] + mix(lambda j: l_ref[j, c, b, at, :])
                    bent = jnp.tanh(u / yield_scale)
                    material = stiff * (hard * u + (1.0 - hard) * yield_scale * bent)
                    residual = image + material - load_ref[c, at, half]
                    u_ref[c, at, half] = u
                    res_ref[c, at, half] = residual
                    lu_ref[c, b, at, :] = image
                    x_ref[0, c, b, group_rows(g), :] = -residual
                    d_ref[c, b, at, :] = stiff * (hard + (1.0 - hard) * (1.0 - bent * bent))
            return 0

        finish(0, 0)
        apply_row(lu_ref, 0, 1, under)
        apply_strips(lu_ref, 0, left, right, range(1, groups))
        lax.fori_loop(1, groups, finish, 0)

        @pl.when(n < NEWTON - 1)
        def _():
            for c in range(comps):
                for b in range(halves):
                    i = c * halves + b
                    own_ref[0, 0, i:i + 1, :] = x_ref[0, c, b, PAD:PAD + 1, :]
            own_ref[0, 1] = strip_of(x_ref.at[0], 0, range(groups), zero)
            take_row(KRY, KRY, 0)
            take_strips(KRY, KRY)
            await_bytes(crecv.at[STEPS], cr.at[STEPS])
            for i in (0, 2, 3):
                derive_halo(i)

        return 0

    def next_residual(loads, stiff, hard, first, second, third, last):
        k0, k1, k2 = [coef_ref[j] for j in range(KRY)]
        if len(first.shape) == 3:
            k0, k1, k2 = k0[0:4][None], k1[0:4][None], k2[0:4][None]
        u = k0 * first + k1 * second + k2 * third
        moved = k0 * (second - stiff * first) + k1 * (third - stiff * second) + k2 * last
        material = stiff * (hard * u + (1.0 - hard) * yield_scale * jnp.tanh(u / yield_scale))
        return loads - (moved + material)

    def derive_slots():
        await_bytes(fixed.at[0:(n_zone - 1) * CAP], fr.at[STEPS])
        await_bytes(frecv[0].at[1, 0:(n_zone - 1) * CAP], fr.at[KRY])
        stiff = jnp.broadcast_to(fixed[:, 0:1, :], fixed.shape)
        hard = jnp.broadcast_to(fixed[:, 1:2, :], fixed.shape)
        fields = [slot_ref[j] for j in range(KRY)]
        slot_ref[0] = next_residual(fields[0], stiff, hard, *fields, frecv[0][1] + bsend[KRY - 1])

    def derive_halo(i):
        if i < 2:
            await_bytes(rrecv.at[STEPS, i], rr.at[STEPS, i])
            packed = rrecv[STEPS, i]
            stiff, hard = [
                jnp.where(
                    sub < comps * halves,
                    jnp.where(lax.rem(sub, halves) == 0, packed[e:e + 1], packed[e + 1:e + 2]), 0.0,
                )
                for e in (0, halves)
            ]
        else:
            packed = crecv[STEPS, i - 2]
            parts = [
                jnp.where(lane < groups, packed, 0.0),
                jnp.where(lane < groups, pltpu.roll(packed, BLK - groups, axis=1), 0.0),
            ]
            stiff, hard = [
                part + pltpu.roll(part, groups, axis=1) + pltpu.roll(part, 2 * groups, axis=1) for part in parts
            ]
        fields = [halo_ref[j, i] for j in range(KRY + 1)]
        halo_ref[0, i] = next_residual(fields[0], stiff, hard, *fields)

    def send_fixed():
        def tile(c, b):
            if c == 0:
                return stiff_ref[0:SROWS, b * BLK:(b + 1) * BLK]
            return hard_ref[b, 0:SROWS, :] if c == 1 else zero

        send_surface(STEPS, tile, fixed)
        for end, at in ((0, 0), (1, height - 1)):
            for b in range(halves):
                rsend[STEPS, end, b:b + 1, :] = stiff_ref[at:at + 1, b * BLK:(b + 1) * BLK]
                rsend[STEPS, end, halves + b:halves + b + 1, :] = hard_ref[b, at:at + 1, :]
            ship_row(STEPS, end)
        for end, b, column in ((0, 0, 0), (1, halves - 1, BLK - 1)):
            strip = zero
            for g in range(groups):
                at = slice(g * 8, g * 8 + 8)
                for e, tile8 in ((0, stiff_ref[at, b * BLK:(b + 1) * BLK]), (groups, hard_ref[b, at, :])):
                    strip = jnp.where(
                        lane == e + g, jnp.broadcast_to(tile8[:, column:column + 1], (8, BLK)), strip
                    )
            csend[STEPS, end] = strip
        ship_strips(STEPS)

    own_ref[0, 0] = zero
    send_row(0, 0, 1)
    send_field(0, 0, frecv[0].at[0])
    pack_strips(0, 0, range(1, groups), lambda end: zero)
    send_strips(0, 0)
    send_row(0, 0, 0)
    set_up()
    send_fixed()
    lax.fori_loop(0, NEWTON, newton, 0)

    def drain(it, _):
        await_bytes(fsend.at[it, 0:n_zone - 1], fs.at[it])
        for end in range(2):
            await_bytes(rsend.at[it, end], rs.at[it, end])
        await_bytes(csend.at[it], cs.at[it])
        return 0

    def drain_sums(it, _):
        await_bytes(bsend.at[it, 0:(n_zone - 1) * CAP], bs.at[it])
        await_bytes(srecv.at[it, 0:devices - 1], ss.at[it])
        return 0

    lax.fori_loop(0, STEPS + 1, drain, 0)
    lax.fori_loop(0, STEPS, drain_sums, 0)


def local(n_vol, n_zone, load, support_stiffness, plastic_flags, owner_map, pattern, active, mortar):
    comps, height, breadth = load.shape
    halves = breadth // BLK
    rows = active.shape[2]
    field = pltpu.VMEM((comps, halves, height, BLK), F32)
    slots = n_zone * CAP
    landing = pltpu.VMEM((NEWTON, slots, 4, BLK), F32)
    blocks = SROWS * halves
    devices = n_vol * n_zone
    wide = -(-rows * NNZ * 12 // BLK) * BLK
    dma = pltpu.SemaphoreType.DMA
    vmem = pl.BlockSpec(memory_space=pltpu.VMEM)
    hbm = pl.BlockSpec(memory_space=pltpu.HBM)
    flags = plastic_flags.T
    links = jnp.transpose(pattern, (0, 3, 1, 2))
    operands = (load, support_stiffness, flags, owner_map, links, active, mortar)
    return pl.pallas_call(
        functools.partial(kernel, n_vol, n_zone),
        out_shape=[jax.ShapeDtypeStruct(load.shape, F32)] * 2,
        in_specs=[hbm] * 7,
        out_specs=[vmem, vmem],
        scratch_shapes=[
            pltpu.VMEM(load.shape, F32),
            pltpu.VMEM(support_stiffness.shape, F32),
            pltpu.VMEM(flags.shape, jnp.int32),
            pltpu.SMEM(owner_map.shape, jnp.int32),
            pltpu.SMEM(links.shape, jnp.int32),
            pltpu.SMEM(active.shape, jnp.int32),
            pltpu.VMEM(mortar.shape[2:], F32),
            pltpu.VMEM((KRY + 1, comps, halves, height + 2 * PAD, BLK), F32),
            pltpu.VMEM((KRY, comps, halves, height, BLK), F32),
            field, field, field,
            pltpu.VMEM((halves, height, BLK), F32),
            pltpu.VMEM((KRY, comps, halves, SROWS, BLK), F32),
            pltpu.VMEM((KRY + 1, 4, 8, BLK), F32),
            pltpu.VMEM((KRY + 1, 2, 8, BLK), F32),
            pltpu.VMEM((KRY, slots, 4, BLK), F32),
            pltpu.VMEM((KRY, 8, BLK), F32),
            pltpu.VMEM((KRY, rows * 8, BLK), F32),
            pltpu.VMEM((rows * 8, BLK), F32),
            pltpu.VMEM((rows, BLK, NNZ * BLK), BF16),
            pltpu.VMEM((rows, BLK, NNZ * BLK), BF16),
            pltpu.VMEM((slots * 4, wide), BF16),
            pltpu.VMEM((wide, BLK), F32),
            pltpu.VMEM((blocks * 8, BLK), F32),
            pltpu.VMEM((blocks + 1, 8, BLK), F32),
            pltpu.VMEM((blocks * 8, BLK), F32),
            pltpu.SMEM((slots,), jnp.int32),
            pltpu.SMEM((blocks,), jnp.int32),
            pltpu.VMEM((STEPS + 1, n_zone, CAP, 4, BLK), F32),
            landing, landing, landing,
            pltpu.VMEM((slots, 4, BLK), F32),
            pltpu.VMEM((STEPS, slots, 4, BLK), F32),
            landing, landing, landing,
            pltpu.VMEM((STEPS + 1, 2, 8, BLK), F32),
            pltpu.VMEM((STEPS + 1, 2, 8, BLK), F32),
            pltpu.VMEM((STEPS + 1, 2, 8, BLK), F32),
            pltpu.VMEM((STEPS + 1, 2, 8, BLK), F32),
            pltpu.VMEM((STEPS, 1, BLK), F32),
            pltpu.VMEM((STEPS, devices, 1, BLK), F32),
            pltpu.SemaphoreType.REGULAR,
            dma((7,)),
        ] + [dma((STEPS + 1,))] * 4 + [dma((STEPS + 1, 2))] * 2 + [dma((STEPS + 1,))] * 4,
        compiler_params=pltpu.CompilerParams(
            collective_id=0, has_side_effects=True, vmem_limit_bytes=32 * 1024 * 1024
        ),
    )(*[pltpu.with_memory_space_constraint(a, pltpu.HBM) for a in operands])


def solution(mesh):
    in_specs = (
        P(None, "vol", "zone"),
        P("vol", "zone"),
        P("vol", "zone"),
        P("vol", "zone", None),
        P("vol", "zone", None, None),
        P("vol", "zone", None),
        P("vol", "zone", None, None, None, None),
    )
    out_specs = (P(None, "vol", "zone"), P(None, "vol", "zone"))
    body = functools.partial(local, mesh.shape["vol"], mesh.shape["zone"])
    return jax.shard_map(body, mesh=mesh, in_specs=in_specs, out_specs=out_specs, check_vma=False)
```

```python
import functools

import jax
import jax.numpy as jnp
from jax import lax
from jax.experimental import pallas as pl
from jax.experimental.pallas import tpu as pltpu
from jax.sharding import PartitionSpec as P

SROWS = 8
BLK = 128
NNZ = 3
CAP = 4
KRY = 3
NEWTON = 2
STEPS = KRY * NEWTON
PAD = 8

yield_scale = 0.5
penalty = 2.0
plastic_hardening = 0.2

F32 = jnp.float32
BF16 = jnp.bfloat16


def kernel(
    n_vol, n_zone,
    load_hbm, stiff_hbm, flags_hbm, owner_hbm, pattern_hbm, active_hbm, mortar_ref,
    u_ref, res_ref,
    load_ref, stiff_ref, flags_ref, owner_ref, pattern_ref, active_ref, mort_ref,
    x_ref, l_ref, r_ref, d_ref, lu_ref, hard_ref, contact_ref, halo_ref, own_ref, slot_ref, coef_ref, gap_ref, scale_ref,
    mhi_ref, mlo_ref, spread_ref, push_ref,
    surf_ref, block_ref, back_ref,
    pack_tab, unpack_tab,
    fsend, frecv0, frecv1, frecv2, fixed, bsend, brecv0, brecv1, brecv2, rsend, rrecv, csend, crecv, ssend, srecv,
    here, in_sem, fs, fr, bs, br, rs, rr, cs, cr, ss, sr,
):
    frecv, brecv = (frecv0, frecv1, frecv2), (brecv0, brecv1, brecv2)
    comps, height = load_ref.shape[0], load_ref.shape[1]
    halves = load_ref.shape[2] // BLK
    groups = height // 8
    blocks = SROWS * halves
    rows = active_ref.shape[2]
    devices = n_vol * n_zone
    zone = lax.axis_index("zone")
    vol = lax.axis_index("vol")

    inputs = [
        (owner_hbm, owner_ref), (pattern_hbm, pattern_ref), (active_hbm, active_ref), (flags_hbm, flags_ref),
        (load_hbm, load_ref), (stiff_hbm, stiff_ref), (mortar_ref.at[0, 0], mort_ref),
    ]
    fetches = [pltpu.make_async_copy(src, dst, in_sem.at[i]) for i, (src, dst) in enumerate(inputs)]
    for fetch in fetches:
        fetch.start()

    def at_zone(step):
        return lax.rem(zone + step, n_zone) if step else zone

    def at_vol(step):
        return lax.rem(vol + step, n_vol) if step else vol

    side = 4

    def hops(offset):
        around = [offset[0] // side, offset[0] % side, (offset[1] + 1) // 2]
        return sum(min(a % side, side - a % side) for a in around)

    others = [(v, z) for v in range(n_vol) for z in range(n_zone) if (v, z) != (0, 0)]
    others.sort(key=lambda offset: -hops(offset))

    barrier = pltpu.get_barrier_semaphore()
    for v in (10, 9, 11, 6, 14, 8, 2, 5, 7, 13, 15, 4, 12, 1, 3):
        pl.semaphore_signal(barrier, inc=1, device_id={"vol": at_vol(v)})
    for z in (4, 3, 5, 2, 6, 1, 7):
        pl.semaphore_signal(barrier, inc=1, device_id={"zone": at_zone(z)})

    sub = lax.broadcasted_iota(jnp.int32, (8, BLK), 0)
    lane = lax.broadcasted_iota(jnp.int32, (8, BLK), 1)
    zero = jnp.zeros((8, BLK), F32)

    for fetch in fetches[:4]:
        fetch.wait()
    owners = [owner_ref[0, 0, m] for m in range(blocks)]
    weights = []
    for m in range(blocks):
        weight, rank = jnp.int32(1), jnp.int32(0)
        for e in range(m):
            same = owners[e] == owners[m]
            weight = jnp.where(same, weight * 32, weight)
            rank = rank + jnp.where(same, 1, 0)
        weights.append(weight)
        unpack_tab[m] = owners[m] * CAP + rank
    for z in range(n_zone):
        code = jnp.int32(0)
        for m in range(blocks):
            code = code + jnp.where(owners[m] == z, weights[m] * (blocks + m), 0)
        for k in range(CAP):
            field = lax.shift_right_logical(code, 5 * k) & 31
            pack_tab[z * CAP + k] = jnp.where(field >= blocks, field - blocks, blocks)

    def link(r, k):
        return pattern_ref[0, k, 0, r]

    surf_ref[...] = jnp.zeros_like(surf_ref)
    block_ref[blocks] = zero
    rsend[...] = jnp.zeros_like(rsend)
    for fetch in fetches[4:6]:
        fetch.wait()
    for c in range(comps):
        for b in range(halves):
            for j in range(KRY + 1):
                x_ref[j, c, b, 0:PAD, :] = jnp.zeros((PAD, BLK), F32)
                x_ref[j, c, b, PAD + height:, :] = jnp.zeros((PAD, BLK), F32)
            x_ref[0, c, b, PAD:PAD + height, :] = load_ref[c, :, b * BLK:(b + 1) * BLK]
            d_ref[c, b] = stiff_ref[:, b * BLK:(b + 1) * BLK]

    def split(r, _):
        for k in range(NNZ):
            piece = mort_ref[r, k] if k == 0 else -mort_ref[r, k]
            high = piece.astype(BF16)
            mhi_ref[r, :, k * BLK:(k + 1) * BLK] = high
            mlo_ref[r, :, k * BLK:(k + 1) * BLK] = (piece - high.astype(F32)).astype(BF16)
        return 0

    def set_up():
        pairs = rows * NNZ * 8
        wide = push_ref.shape[0]
        link_lane = lax.broadcasted_iota(jnp.int32, (1, wide), 1)
        tail = (link_lane - pairs) // 4
        entry = jnp.where(link_lane < pairs, link_lane // 8, jnp.where(tail < rows * NNZ, tail, -1))
        links = jnp.full((1, wide), -1, jnp.int32)
        for r in range(rows):
            scale_ref[r * 8:r * 8 + 8, :] = jnp.full((8, BLK), penalty * active_ref[0, 0, r].astype(F32))
            for k in range(NNZ):
                links = jnp.where(entry == r * NNZ + k, link(r, k), links)
        out_row = lax.broadcasted_iota(jnp.int32, (n_zone * CAP * 4, wide), 0)
        out_lane = lax.broadcasted_iota(jnp.int32, (n_zone * CAP * 4, wide), 1)
        hit = (out_row // 4 == links) & (lax.rem(out_row, 4) == lax.rem(out_lane, 4))
        spread_ref[...] = jnp.where(hit, 1.0, 0.0).astype(BF16)
        back_ref[...] = jnp.zeros_like(back_ref)
        push_ref[...] = jnp.zeros_like(push_ref)
        u_ref[...] = jnp.zeros_like(u_ref)
        lu_ref[...] = jnp.zeros_like(lu_ref)
        for b in range(halves):
            flag = jnp.transpose(jnp.broadcast_to(flags_ref[b:b + 1, :], (height, BLK)))
            hard_ref[b] = jnp.where(flag == 1, plastic_hardening, 1.0).astype(F32)
        fetches[6].wait()
        lax.fori_loop(0, rows, split, 0)

    pl.semaphore_wait(barrier, n_vol - 1 + n_zone - 1)
    for v in range(1, n_vol):
        pl.semaphore_signal(here, inc=1, device_id={"vol": at_vol(v)})

    def remote(src, dst, send, recv, target):
        return pltpu.make_async_remote_copy(
            src_ref=src, dst_ref=dst, send_sem=send, recv_sem=recv, device_id=target
        )

    def await_bytes(ref, sem):
        pltpu.make_async_copy(ref, ref, sem).wait()

    def slots_of(z):
        return pl.ds(z * CAP, CAP)

    def group_rows(g):
        return pl.ds(pl.multiple_of(PAD + g * 8, 8), 8)

    def tile_rows(g):
        return pl.ds(pl.multiple_of(g * 8, 8), 8)

    def sum_tiles(body, count):
        def group(g, sums):
            added = []
            for c in range(comps):
                for b in range(halves):
                    terms = body(c, b, group_rows(g), tile_rows(g))
                    added += [total + term for total, term in zip(sums[c * halves + b], terms)]
            return tuple(tuple(added[i:i + count]) for i in range(0, len(added), count))

        start = tuple(tuple(zero for _ in range(count)) for _ in range(comps * halves))
        sums = lax.fori_loop(0, groups, group, start, unroll=4)
        return [total_of([tile[i] for tile in sums]) for i in range(count)]

    def total_of(terms):
        while len(terms) > 1:
            terms = [sum(terms[i:i + 2][1:], terms[i]) for i in range(0, len(terms), 2)]
        return terms[0]

    def send_surface(it, tile, landing):
        for c in range(comps):
            for b in range(halves):
                surf_ref[pl.ds(b * 8 + c, SROWS, stride=8 * halves), :] = tile(c, b)
        for m in range(blocks):
            block_ref[m] = surf_ref[m * 8:m * 8 + 8, :]
        for step in (4, 3, 5, 2, 6, 1, 7, 0):
            z = at_zone(step)
            for k in range(CAP):
                block = block_ref[pack_tab[z * CAP + k]][0:4]
                if step:
                    fsend[it, step, k] = block
                else:
                    landing[zone * CAP + k] = block
            if step:
                remote(fsend.at[it, step], landing.at[slots_of(zone)], fs.at[it], fr.at[it], {"zone": z}).start()

    def send_field(j, it, landing):
        send_surface(it, lambda c, b: x_ref[j, c, b, PAD:PAD + SROWS, :], landing)

    def send_row(j, it, end):
        at = PAD + (height - 1 if end else 0)
        for c in range(comps):
            for b in range(halves):
                i = c * halves + b
                rsend[it, end, i:i + 1, :] = x_ref[j, c, b, at:at + 1, :]
        if end == 0:
            own_ref[j, 0] = rsend[it, 0]
        ship_row(it, end)

    def ship_row(it, end):
        target = at_vol(1 if end else n_vol - 1)
        remote(
            rsend.at[it, end], rrecv.at[it, 1 - end], rs.at[it, end], rr.at[it, 1 - end], {"vol": target}
        ).start()

    def strip_of(field, end, chosen, strip):
        b, column = (halves - 1, BLK - 1) if end else (0, 0)
        for c in range(comps):
            for g in chosen:
                tile = field[c, b, PAD + g * 8:PAD + g * 8 + 8, :]
                strip = jnp.where(
                    lane == c * groups + g, jnp.broadcast_to(tile[:, column:column + 1], (8, BLK)), strip
                )
        return strip

    def pack_strips(j, it, chosen, strips):
        for end in range(2):
            csend[it, end] = strip_of(x_ref.at[j], end, chosen, strips(end))

    def send_strips(j, it):
        pack_strips(j, it, range(1), lambda end: csend[it, end])
        own_ref[j, 1] = csend[it, 0]
        ship_strips(it)

    def ship_strips(it):
        remote(csend.at[it, 0], crecv.at[it, 1], cs.at[it], cr.at[it], {"zone": at_zone(n_zone - 1)}).start()
        remote(csend.at[it, 1], crecv.at[it, 0], cs.at[it], cr.at[it], {"zone": at_zone(1)}).start()

    def take_row(j, it, end):
        await_bytes(rrecv.at[it, end], rr.at[it, end])
        halo_ref[j, end] = jnp.where(vol == (n_vol - 1 if end else 0), 0.0, rrecv[it, end])

    def take_strips(j, it):
        await_bytes(crecv.at[it], cr.at[it])
        halo_ref[j, 2] = jnp.where(zone == 0, 0.0, crecv[it, 0])
        halo_ref[j, 3] = jnp.where(zone == n_zone - 1, 0.0, crecv[it, 1])

    def apply_row(field, offset, end, halo):
        at = offset + (height - 1 if end else 0)
        for c in range(comps):
            for b in range(halves):
                i = c * halves + b
                field[c, b, at:at + 1, :] = field[c, b, at:at + 1, :] - halo[i:i + 1]

    def apply_strips(field, offset, left, right, chosen):
        for halo, b, column in ((left, 0, 0), (right, halves - 1, BLK - 1)):
            for c in range(comps):
                for g in chosen:
                    i = c * groups + g
                    at = slice(offset + g * 8, offset + g * 8 + 8)
                    spread = jnp.broadcast_to(halo[:, i:i + 1], (8, BLK))
                    image = field[c, b, at, :]
                    field[c, b, at, :] = jnp.where(lane == column, image - spread, image)

    def inner(j, sums=False):
        def group(g, totals):
            totals = list(totals)
            for c in range(comps):
                tiles = [x_ref[j, c, b, group_rows(g), :] for b in range(halves)]
                to_right = [pltpu.roll(tile, 1, axis=1) for tile in tiles]
                to_left = [pltpu.roll(tile, BLK - 1, axis=1) for tile in tiles]
                for b in range(halves):
                    x = tiles[b]
                    before = to_right[b - 1] if b > 0 else zero
                    after = to_left[b + 1] if b < halves - 1 else zero
                    left = jnp.where(lane == 0, before, to_right[b])
                    right = jnp.where(lane == BLK - 1, after, to_left[b])
                    over = x_ref[j, c, b, pl.ds(PAD + g * 8 - 1, 8), :]
                    under = x_ref[j, c, b, pl.ds(PAD + g * 8 + 1, 8), :]
                    part = 4.0 * x - ((over + under) + (left + right))
                    l_ref[j, c, b, tile_rows(g), :] = part
                    if sums:
                        i = 2 * (c * halves + b)
                        totals[i] = totals[i] + x * x
                        totals[i + 1] = totals[i + 1] + x * (part + d_ref[c, b, tile_rows(g), :] * x)
            return tuple(totals)

        start = (zero,) * (2 * comps * halves if sums else 0)
        totals = lax.fori_loop(0, groups, group, start, unroll=4)
        return [total_of(list(totals[i::2])) for i in range(2)] if sums else None

    def image(j, c, b, at, padded):
        part = l_ref[j, c, b, at, :]
        return part + d_ref[c, b, at, :] * x_ref[j, c, b, padded, :] if j < KRY - 1 else part

    def first_rows(j):
        for c in range(comps):
            for b in range(halves):
                at = slice(PAD, PAD + SROWS)
                x_ref[j + 1, c, b, at, :] = image(j, c, b, slice(0, SROWS), at)
        field = x_ref.at[j + 1]
        apply_row(field, PAD, 0, halo_ref[j, 0])
        apply_strips(field, PAD, halo_ref[j, 2], halo_ref[j, 3], range(1))

    def other_rows(j):
        def group(g, _):
            for c in range(comps):
                for b in range(halves):
                    x_ref[j + 1, c, b, group_rows(g), :] = image(j, c, b, tile_rows(g), group_rows(g))
            return 0

        lax.fori_loop(1, groups, group, 0, unroll=5)
        field = x_ref.at[j + 1]
        apply_row(field, PAD, 1, halo_ref[j, 1])
        apply_strips(field, PAD, halo_ref[j, 2], halo_ref[j, 3], range(1, groups))

    upper = lax.broadcasted_iota(jnp.int32, (8, NNZ * BLK), 0) < 4
    contract_last = (((1,), (1,)), ((), ()))

    def split_rows(piece):
        high = piece.astype(BF16).astype(F32)
        rest = piece - high
        middle = rest.astype(BF16).astype(F32)
        return jnp.concatenate([high, middle, rest - middle, jnp.zeros_like(piece)], axis=0).astype(BF16)

    def join_rows(product):
        product = product[0:8] + product[8:16]
        return product + pltpu.roll(product, 4, axis=0)

    def fill_slots(j, n):
        it = n * KRY + j
        await_bytes(frecv[j].at[n, 0:(n_zone - 1) * CAP], fr.at[it])
        slot_ref[j] = frecv[j][n] + bsend[it - 1] if j else frecv[j][n]

    def find_gaps(j):
        for r in range(rows):
            picked = split_rows(jnp.concatenate([slot_ref[j, link(r, k)] for k in range(NNZ)], axis=1))
            gap = lax.dot_general(picked, mhi_ref[r], contract_last, preferred_element_type=F32)
            gap = gap + lax.dot_general(picked, mlo_ref[r], contract_last, preferred_element_type=F32)
            gap_ref[j, r * 8:r * 8 + 8, :] = join_rows(gap)

    def push_forces(j, n):
        it = n * KRY + j
        for r in range(rows):
            at = slice(r * 8, r * 8 + 8)
            multiplier = split_rows((scale_ref[at, :] * gap_ref[j, at, :])[0:4])
            force = jnp.dot(multiplier, mhi_ref[r], preferred_element_type=F32)
            force = force + jnp.dot(multiplier, mlo_ref[r], preferred_element_type=F32)
            force = join_rows(force)
            high = force.astype(BF16).astype(F32)
            rest = force - high
            middle = rest.astype(BF16).astype(F32)
            two = jnp.where(upper, high, middle)
            low = (rest - middle)[0:4]
            for k in range(NNZ):
                entry = r * NNZ + k
                part = slice(k * BLK, (k + 1) * BLK)
                push_ref[entry * 8:entry * 8 + 8, :] = two[:, part]
                to = rows * NNZ * 8 + entry * 4
                push_ref[to:to + 4, :] = low[:, part]
        summed = jnp.dot(spread_ref[...], push_ref[...].astype(BF16), preferred_element_type=F32)
        bsend[it] = summed.reshape(n_zone * CAP, 4, BLK)
        for step in (4, 3, 5, 2, 6, 1, 7):
            z = at_zone(step)
            remote(
                bsend.at[it, slots_of(z)], brecv[j].at[n, slots_of(zone)], bs.at[it], br.at[it], {"zone": z}
            ).start()
        brecv[j][n, slots_of(zone)] = bsend[it, slots_of(zone)]

    def receive_forces(j, n):
        await_bytes(brecv[j].at[n, 0:(n_zone - 1) * CAP], br.at[n * KRY + j])
        for m in range(blocks):
            back_ref[m * 8:m * 8 + 4, :] = brecv[j][n, unpack_tab[m]]
        for c in range(comps):
            for b in range(halves):
                contact_ref[j, c, b] = back_ref[pl.ds(b * 8 + c, SROWS, stride=8 * halves), :]

    def energy(gaps):
        terms = []
        for r in range(rows):
            at = slice(r * 8, r * 8 + 8)
            gap = gaps(at)
            terms.append(scale_ref[at, :] * (gap * gap))
        return 0.5 * total_of(terms)

    def start_sums(it, gamma, delta, cross):
        parts = []
        for part in (gamma, delta, cross):
            part = part + pltpu.roll(part, 64, axis=1)
            parts.append(part + pltpu.roll(part, 32, axis=1))
        mixed = jnp.where(lane < 32, parts[0], jnp.where(lane < 64, parts[1], parts[2]))
        mixed = jnp.sum(mixed, axis=0, keepdims=True)
        me = vol * n_zone + zone
        ssend[it] = mixed
        srecv[it, me] = mixed
        for v, z in others:
            target = {"vol": at_vol(v), "zone": at_zone(z)}
            remote(ssend.at[it], srecv.at[it, me], ss.at[it], sr.at[it], target).start()

    def finish_sums(it):
        await_bytes(srecv.at[it, 0:devices - 1], sr.at[it])
        total = srecv[it]
        while total.shape[0] > 1:
            half = total.shape[0] // 2
            total = total[:half] + total[half:]
        total = total[0]
        place = lane[0:1]
        return [
            jnp.sum(jnp.where(place // 32 == i, total, 0.0), axis=1, keepdims=True) for i in range(3)
        ]

    def full(scalar):
        return jnp.broadcast_to(scalar, (8, BLK))

    def add_contact(j):
        for c in range(comps):
            for b in range(halves):
                at = slice(PAD, PAD + SROWS)
                x_ref[j + 1, c, b, at, :] = x_ref[j + 1, c, b, at, :] + contact_ref[j, c, b]

    def edges(mix):
        return 2.0 * (
            mix(lambda j: own_ref[j, 0]) * mix(lambda j: halo_ref[j, 0])
            + mix(lambda j: own_ref[j, 1]) * mix(lambda j: halo_ref[j, 2])
        )

    def newton(n, _):
        it = n * KRY

        gamma, delta = inner(0, sums=True)

        @pl.when(n == 0)
        def _():
            fill_slots(0, 0)
            find_gaps(0)
            push_forces(0, 0)
            take_row(0, 0, 0)
            take_strips(0, 0)


        @pl.when(n == 0)
        def _():
            pl.semaphore_wait(here, n_vol - 1)

        first_rows(0)
        send_field(1, it + 1, frecv[1].at[n])
        delta = delta + energy(lambda at: gap_ref[0, at, :]) - edges(lambda part: part(0))
        start_sums(it, gamma, delta, zero)

        @pl.when(n == 0)
        def _():
            take_row(0, 0, 1)

        @pl.when(n > 0)
        def _():
            take_row(KRY, KRY, 1)
            derive_halo(1)

        other_rows(0)
        send_row(1, it + 1, 1)
        pack_strips(1, it + 1, range(1, groups), lambda end: zero)
        receive_forces(0, n)
        add_contact(0)
        send_strips(1, it + 1)
        send_row(1, it + 1, 0)
        inner(1)
        fill_slots(1, n)
        find_gaps(1)
        push_forces(1, n)
        take_row(1, it + 1, 0)
        take_strips(1, it + 1)
        first_rows(1)
        send_field(2, it + 2, frecv[2].at[n])
        gamma0, pq0, _ = finish_sums(it)
        a0 = gamma0 / pq0
        w0 = full(a0)

        def dots1(c, b, padded, at):
            x1 = x_ref[1, c, b, padded, :]
            r = x_ref[0, c, b, padded, :] - w0 * x1
            r_ref[c, b, at, :] = r
            q = (l_ref[0, c, b, at, :] - w0 * l_ref[1, c, b, at, :]) + d_ref[c, b, at, :] * r
            return r * r, r * q, r * x1

        gamma, delta, cross = sum_tiles(dots1, 3)
        delta = delta + energy(lambda at: gap_ref[0, at, :] - w0 * gap_ref[1, at, :])
        delta = delta - edges(lambda part: part(0) - w0 * part(1))
        start_sums(it + 1, gamma, delta, cross)
        take_row(1, it + 1, 1)
        other_rows(1)
        send_row(2, it + 2, 1)
        pack_strips(2, it + 2, range(1, groups), lambda end: zero)
        receive_forces(1, n)
        add_contact(1)
        send_strips(2, it + 2)
        send_row(2, it + 2, 0)
        inner(2)
        fill_slots(2, n)
        find_gaps(2)
        push_forces(2, n)
        gamma1, delta, cross = finish_sums(it + 1)
        beta1 = gamma1 / gamma0
        pq1 = delta + beta1 * (2.0 * cross + beta1 * pq0)
        a1 = gamma1 / pq1
        take_row(2, it + 2, 0)
        take_strips(2, it + 2)
        more, w1 = full(1.0 + beta1), full(a1)

        def second(x0, x1, x2):
            return (x0 - w0 * x1) - w1 * (more * x1 - w0 * x2)

        def dots2(c, b, padded, at):
            image = more * x_ref[1, c, b, padded, :] - w0 * x_ref[2, c, b, padded, :]
            r = r_ref[c, b, at, :] - w1 * image
            q = second(l_ref[0, c, b, at, :], l_ref[1, c, b, at, :], l_ref[2, c, b, at, :])
            q = q + d_ref[c, b, at, :] * r
            return r * r, r * q, r * image

        gamma, delta, cross = sum_tiles(dots2, 3)
        delta = delta + energy(lambda at: second(gap_ref[0, at, :], gap_ref[1, at, :], gap_ref[2, at, :]))
        delta = delta - edges(lambda part: second(part(0), part(1), part(2)))
        start_sums(it + 2, gamma, delta, cross)

        @pl.when(n < NEWTON - 1)
        def _():
            first_rows(2)
            send_field(KRY, KRY, frecv[0].at[1])

        take_row(2, it + 2, 1)

        @pl.when(n < NEWTON - 1)
        def _():
            other_rows(2)
            send_row(KRY, KRY, 1)
            pack_strips(KRY, KRY, range(1, groups), lambda end: zero)

        receive_forces(2, n)

        @pl.when(n < NEWTON - 1)
        def _():
            add_contact(2)
            send_strips(KRY, KRY)
            send_row(KRY, KRY, 0)

        gamma2, delta, cross = finish_sums(it + 2)
        beta2 = gamma2 / gamma1
        pq2 = delta + beta2 * (2.0 * cross + beta2 * pq1)
        a2 = gamma2 / pq2
        turned = beta2 * (1.0 + beta1)
        k0 = full(a0 + a1 * (1.0 + beta1) + a2 * (1.0 + turned))
        k1 = full(-(a1 * a0 + a2 * (a0 + a1 * (1.0 + beta1) + beta2 * a0)))
        k2 = full(a2 * a1 * a0)

        coef_ref[0], coef_ref[1], coef_ref[2] = k0, k1, k2

        @pl.when(n < NEWTON - 1)
        def _():
            derive_slots()
            find_gaps(0)
            push_forces(0, 1)

        def mix(fields):
            return k0 * fields(0) + k1 * fields(1) + k2 * fields(2)

        for c in range(comps):
            for b in range(halves):
                lu_ref[c, b, 0:SROWS, :] = lu_ref[c, b, 0:SROWS, :] + mix(lambda j: contact_ref[j, c, b])
        over, under, left, right = [mix(lambda j: halo_ref[j, i]) for i in range(4)]
        apply_row(lu_ref, 0, 0, over)
        apply_strips(lu_ref, 0, left, right, range(1))

        def finish(g, _):
            at = tile_rows(g)
            for b in range(halves):
                half = slice(b * BLK, (b + 1) * BLK)
                stiff, hard = stiff_ref[at, half], hard_ref[b, at, :]
                for c in range(comps):
                    u = u_ref[c, at, half] + mix(lambda j: x_ref[j, c, b, group_rows(g), :])
                    image = lu_ref[c, b, at, :] + mix(lambda j: l_ref[j, c, b, at, :])
                    bent = jnp.tanh(u / yield_scale)
                    material = stiff * (hard * u + (1.0 - hard) * yield_scale * bent)
                    residual = image + material - load_ref[c, at, half]
                    u_ref[c, at, half] = u
                    res_ref[c, at, half] = residual
                    lu_ref[c, b, at, :] = image
                    x_ref[0, c, b, group_rows(g), :] = -residual
                    d_ref[c, b, at, :] = stiff * (hard + (1.0 - hard) * (1.0 - bent * bent))
            return 0

        finish(0, 0)
        apply_row(lu_ref, 0, 1, under)
        apply_strips(lu_ref, 0, left, right, range(1, groups))
        lax.fori_loop(1, groups, finish, 0, unroll=3)

        @pl.when(n < NEWTON - 1)
        def _():
            for c in range(comps):
                for b in range(halves):
                    i = c * halves + b
                    own_ref[0, 0, i:i + 1, :] = x_ref[0, c, b, PAD:PAD + 1, :]
            own_ref[0, 1] = strip_of(x_ref.at[0], 0, range(groups), zero)
            take_row(KRY, KRY, 0)
            take_strips(KRY, KRY)
            await_bytes(crecv.at[STEPS], cr.at[STEPS])
            for i in (0, 2, 3):
                derive_halo(i)

        return 0

    def next_residual(loads, stiff, hard, first, second, third, last):
        k0, k1, k2 = [coef_ref[j] for j in range(KRY)]
        if len(first.shape) == 3:
            k0, k1, k2 = k0[0:4][None], k1[0:4][None], k2[0:4][None]
        u = k0 * first + k1 * second + k2 * third
        moved = k0 * (second - stiff * first) + k1 * (third - stiff * second) + k2 * last
        material = stiff * (hard * u + (1.0 - hard) * yield_scale * jnp.tanh(u / yield_scale))
        return loads - (moved + material)

    def derive_slots():
        await_bytes(fixed.at[0:(n_zone - 1) * CAP], fr.at[STEPS])
        await_bytes(frecv[0].at[1, 0:(n_zone - 1) * CAP], fr.at[KRY])
        stiff = jnp.broadcast_to(fixed[:, 0:1, :], fixed.shape)
        hard = jnp.broadcast_to(fixed[:, 1:2, :], fixed.shape)
        fields = [slot_ref[j] for j in range(KRY)]
        slot_ref[0] = next_residual(fields[0], stiff, hard, *fields, frecv[0][1] + bsend[KRY - 1])

    def derive_halo(i):
        if i < 2:
            await_bytes(rrecv.at[STEPS, i], rr.at[STEPS, i])
            packed = rrecv[STEPS, i]
            stiff, hard = [
                jnp.where(
                    sub < comps * halves,
                    jnp.where(lax.rem(sub, halves) == 0, packed[e:e + 1], packed[e + 1:e + 2]), 0.0,
                )
                for e in (0, halves)
            ]
        else:
            packed = crecv[STEPS, i - 2]
            parts = [
                jnp.where(lane < groups, packed, 0.0),
                jnp.where(lane < groups, pltpu.roll(packed, BLK - groups, axis=1), 0.0),
            ]
            stiff, hard = [
                part + pltpu.roll(part, groups, axis=1) + pltpu.roll(part, 2 * groups, axis=1) for part in parts
            ]
        fields = [halo_ref[j, i] for j in range(KRY + 1)]
        halo_ref[0, i] = next_residual(fields[0], stiff, hard, *fields)

    def send_fixed():
        def tile(c, b):
            if c == 0:
                return stiff_ref[0:SROWS, b * BLK:(b + 1) * BLK]
            return hard_ref[b, 0:SROWS, :] if c == 1 else zero

        send_surface(STEPS, tile, fixed)
        for end, at in ((0, 0), (1, height - 1)):
            for b in range(halves):
                rsend[STEPS, end, b:b + 1, :] = stiff_ref[at:at + 1, b * BLK:(b + 1) * BLK]
                rsend[STEPS, end, halves + b:halves + b + 1, :] = hard_ref[b, at:at + 1, :]
            ship_row(STEPS, end)
        for end, b, column in ((0, 0, 0), (1, halves - 1, BLK - 1)):
            strip = zero
            for g in range(groups):
                at = slice(g * 8, g * 8 + 8)
                for e, tile8 in ((0, stiff_ref[at, b * BLK:(b + 1) * BLK]), (groups, hard_ref[b, at, :])):
                    strip = jnp.where(
                        lane == e + g, jnp.broadcast_to(tile8[:, column:column + 1], (8, BLK)), strip
                    )
            csend[STEPS, end] = strip
        ship_strips(STEPS)

    own_ref[0, 0] = zero
    send_row(0, 0, 1)
    send_field(0, 0, frecv[0].at[0])
    pack_strips(0, 0, range(1, groups), lambda end: zero)
    send_strips(0, 0)
    send_row(0, 0, 0)
    set_up()
    send_fixed()
    lax.fori_loop(0, NEWTON, newton, 0)

    def drain(it, _):
        await_bytes(fsend.at[it, 0:n_zone - 1], fs.at[it])
        for end in range(2):
            await_bytes(rsend.at[it, end], rs.at[it, end])
        await_bytes(csend.at[it], cs.at[it])
        return 0

    def drain_sums(it, _):
        await_bytes(bsend.at[it, 0:(n_zone - 1) * CAP], bs.at[it])
        await_bytes(srecv.at[it, 0:devices - 1], ss.at[it])
        return 0

    lax.fori_loop(0, STEPS + 1, drain, 0)
    lax.fori_loop(0, STEPS, drain_sums, 0)


def local(n_vol, n_zone, load, support_stiffness, plastic_flags, owner_map, pattern, active, mortar):
    comps, height, breadth = load.shape
    halves = breadth // BLK
    rows = active.shape[2]
    field = pltpu.VMEM((comps, halves, height, BLK), F32)
    slots = n_zone * CAP
    landing = pltpu.VMEM((NEWTON, slots, 4, BLK), F32)
    blocks = SROWS * halves
    devices = n_vol * n_zone
    wide = -(-rows * NNZ * 12 // BLK) * BLK
    dma = pltpu.SemaphoreType.DMA
    vmem = pl.BlockSpec(memory_space=pltpu.VMEM)
    hbm = pl.BlockSpec(memory_space=pltpu.HBM)
    flags = plastic_flags.T
    links = jnp.transpose(pattern, (0, 3, 1, 2))
    operands = (load, support_stiffness, flags, owner_map, links, active, mortar)
    return pl.pallas_call(
        functools.partial(kernel, n_vol, n_zone),
        out_shape=[jax.ShapeDtypeStruct(load.shape, F32)] * 2,
        in_specs=[hbm] * 7,
        out_specs=[vmem, vmem],
        scratch_shapes=[
            pltpu.VMEM(load.shape, F32),
            pltpu.VMEM(support_stiffness.shape, F32),
            pltpu.VMEM(flags.shape, jnp.int32),
            pltpu.SMEM(owner_map.shape, jnp.int32),
            pltpu.SMEM(links.shape, jnp.int32),
            pltpu.SMEM(active.shape, jnp.int32),
            pltpu.VMEM(mortar.shape[2:], F32),
            pltpu.VMEM((KRY + 1, comps, halves, height + 2 * PAD, BLK), F32),
            pltpu.VMEM((KRY, comps, halves, height, BLK), F32),
            field, field, field,
            pltpu.VMEM((halves, height, BLK), F32),
            pltpu.VMEM((KRY, comps, halves, SROWS, BLK), F32),
            pltpu.VMEM((KRY + 1, 4, 8, BLK), F32),
            pltpu.VMEM((KRY + 1, 2, 8, BLK), F32),
            pltpu.VMEM((KRY, slots, 4, BLK), F32),
            pltpu.VMEM((KRY, 8, BLK), F32),
            pltpu.VMEM((KRY, rows * 8, BLK), F32),
            pltpu.VMEM((rows * 8, BLK), F32),
            pltpu.VMEM((rows, BLK, NNZ * BLK), BF16),
            pltpu.VMEM((rows, BLK, NNZ * BLK), BF16),
            pltpu.VMEM((slots * 4, wide), BF16),
            pltpu.VMEM((wide, BLK), F32),
            pltpu.VMEM((blocks * 8, BLK), F32),
            pltpu.VMEM((blocks + 1, 8, BLK), F32),
            pltpu.VMEM((blocks * 8, BLK), F32),
            pltpu.SMEM((slots,), jnp.int32),
            pltpu.SMEM((blocks,), jnp.int32),
            pltpu.VMEM((STEPS + 1, n_zone, CAP, 4, BLK), F32),
            landing, landing, landing,
            pltpu.VMEM((slots, 4, BLK), F32),
            pltpu.VMEM((STEPS, slots, 4, BLK), F32),
            landing, landing, landing,
            pltpu.VMEM((STEPS + 1, 2, 8, BLK), F32),
            pltpu.VMEM((STEPS + 1, 2, 8, BLK), F32),
            pltpu.VMEM((STEPS + 1, 2, 8, BLK), F32),
            pltpu.VMEM((STEPS + 1, 2, 8, BLK), F32),
            pltpu.VMEM((STEPS, 1, BLK), F32),
            pltpu.VMEM((STEPS, devices, 1, BLK), F32),
            pltpu.SemaphoreType.REGULAR,
            dma((7,)),
        ] + [dma((STEPS + 1,))] * 4 + [dma((STEPS + 1, 2))] * 2 + [dma((STEPS + 1,))] * 4,
        compiler_params=pltpu.CompilerParams(
            collective_id=0, has_side_effects=True, vmem_limit_bytes=32 * 1024 * 1024
        ),
    )(*[pltpu.with_memory_space_constraint(a, pltpu.HBM) for a in operands])


def solution(mesh):
    in_specs = (
        P(None, "vol", "zone"),
        P("vol", "zone"),
        P("vol", "zone"),
        P("vol", "zone", None),
        P("vol", "zone", None, None),
        P("vol", "zone", None),
        P("vol", "zone", None, None, None, None),
    )
    out_specs = (P(None, "vol", "zone"), P(None, "vol", "zone"))
    body = functools.partial(local, mesh.shape["vol"], mesh.shape["zone"])
    return jax.shard_map(body, mesh=mesh, in_specs=in_specs, out_specs=out_specs, check_vma=False)
```

```python
import functools

import jax
import jax.numpy as jnp
from jax import lax
from jax.experimental import pallas as pl
from jax.experimental.pallas import tpu as pltpu
from jax.sharding import PartitionSpec as P

SROWS = 8
BLK = 128
NNZ = 3
CAP = 4
KRY = 3
NEWTON = 2
STEPS = KRY * NEWTON
PAD = 8

yield_scale = 0.5
penalty = 2.0
plastic_hardening = 0.2

F32 = jnp.float32
BF16 = jnp.bfloat16


def kernel(
    n_vol, n_zone,
    load_hbm, stiff_hbm, flags_hbm, owner_hbm, pattern_hbm, active_hbm, mortar_ref,
    u_ref, res_ref,
    load_ref, stiff_ref, flags_ref, owner_ref, pattern_ref, active_ref, mort_ref,
    x_ref, l_ref, r_ref, d_ref, lu_ref, hard_ref, contact_ref, halo_ref, own_ref, slot_ref, coef_ref, gap_ref, scale_ref,
    mhl_ref, spread_ref, push_ref,
    surf_ref, block_ref, back_ref,
    pack_tab, unpack_tab,
    fsend, frecv0, frecv1, frecv2, fixed, bsend, brecv0, brecv1, brecv2, rsend, rrecv, csend, crecv, ssend, srecv,
    here, in_sem, fs, fr, bs, br, rs, rr, cs, cr, ss, sr,
):
    frecv, brecv = (frecv0, frecv1, frecv2), (brecv0, brecv1, brecv2)
    comps, height = load_ref.shape[0], load_ref.shape[1]
    halves = load_ref.shape[2] // BLK
    groups = height // 8
    blocks = SROWS * halves
    rows = active_ref.shape[2]
    devices = n_vol * n_zone
    zone = lax.axis_index("zone")
    vol = lax.axis_index("vol")

    inputs = [
        (owner_hbm, owner_ref), (pattern_hbm, pattern_ref), (active_hbm, active_ref), (flags_hbm, flags_ref),
        (load_hbm, load_ref), (stiff_hbm, stiff_ref), (mortar_ref.at[0, 0], mort_ref),
    ]
    fetches = [pltpu.make_async_copy(src, dst, in_sem.at[i]) for i, (src, dst) in enumerate(inputs)]
    for fetch in fetches:
        fetch.start()

    def at_zone(step):
        return lax.rem(zone + step, n_zone) if step else zone

    def at_vol(step):
        return lax.rem(vol + step, n_vol) if step else vol

    side = 4

    def hops(offset):
        around = [offset[0] // side, offset[0] % side, (offset[1] + 1) // 2]
        return sum(min(a % side, side - a % side) for a in around)

    others = [(v, z) for v in range(n_vol) for z in range(n_zone) if (v, z) != (0, 0)]
    others.sort(key=lambda offset: -hops(offset))

    barrier = pltpu.get_barrier_semaphore()
    for v in (10, 9, 11, 6, 14, 8, 2, 5, 7, 13, 15, 4, 12, 1, 3):
        pl.semaphore_signal(barrier, inc=1, device_id={"vol": at_vol(v)})
    for z in (4, 3, 5, 2, 6, 1, 7):
        pl.semaphore_signal(barrier, inc=1, device_id={"zone": at_zone(z)})

    sub = lax.broadcasted_iota(jnp.int32, (8, BLK), 0)
    lane = lax.broadcasted_iota(jnp.int32, (8, BLK), 1)
    zero = jnp.zeros((8, BLK), F32)

    for fetch in fetches[:4]:
        fetch.wait()
    owners = [owner_ref[0, 0, m] for m in range(blocks)]
    weights = []
    for m in range(blocks):
        weight, rank = jnp.int32(1), jnp.int32(0)
        for e in range(m):
            same = owners[e] == owners[m]
            weight = jnp.where(same, weight * 32, weight)
            rank = rank + jnp.where(same, 1, 0)
        weights.append(weight)
        unpack_tab[m] = owners[m] * CAP + rank
    for z in range(n_zone):
        code = jnp.int32(0)
        for m in range(blocks):
            code = code + jnp.where(owners[m] == z, weights[m] * (blocks + m), 0)
        for k in range(CAP):
            field = lax.shift_right_logical(code, 5 * k) & 31
            pack_tab[z * CAP + k] = jnp.where(field >= blocks, field - blocks, blocks)

    def link(r, k):
        return pattern_ref[0, k, 0, r]

    surf_ref[...] = jnp.zeros_like(surf_ref)
    block_ref[blocks] = zero
    rsend[...] = jnp.zeros_like(rsend)
    for fetch in fetches[4:6]:
        fetch.wait()
    for c in range(comps):
        for b in range(halves):
            for j in range(KRY + 1):
                x_ref[j, c, b, 0:PAD, :] = jnp.zeros((PAD, BLK), F32)
                x_ref[j, c, b, PAD + height:, :] = jnp.zeros((PAD, BLK), F32)
            x_ref[0, c, b, PAD:PAD + height, :] = load_ref[c, :, b * BLK:(b + 1) * BLK]
            d_ref[c, b] = stiff_ref[:, b * BLK:(b + 1) * BLK]

    def split(r, _):
        for k in range(NNZ):
            piece = mort_ref[r, k] if k == 0 else -mort_ref[r, k]
            high = piece.astype(BF16)
            mhl_ref[r, 0:BLK, k * BLK:(k + 1) * BLK] = high
            mhl_ref[r, BLK:2 * BLK, k * BLK:(k + 1) * BLK] = (piece - high.astype(F32)).astype(BF16)
        return 0

    def set_up():
        pairs = rows * NNZ * 8
        wide = push_ref.shape[0]
        link_lane = lax.broadcasted_iota(jnp.int32, (1, wide), 1)
        tail = (link_lane - pairs) // 4
        entry = jnp.where(link_lane < pairs, link_lane // 8, jnp.where(tail < rows * NNZ, tail, -1))
        links = jnp.full((1, wide), -1, jnp.int32)
        for r in range(rows):
            scale_ref[r * 8:r * 8 + 8, :] = jnp.full((8, BLK), penalty * active_ref[0, 0, r].astype(F32))
            for k in range(NNZ):
                links = jnp.where(entry == r * NNZ + k, link(r, k), links)
        out_row = lax.broadcasted_iota(jnp.int32, (n_zone * CAP * 4, wide), 0)
        out_lane = lax.broadcasted_iota(jnp.int32, (n_zone * CAP * 4, wide), 1)
        hit = (out_row // 4 == links) & (lax.rem(out_row, 4) == lax.rem(out_lane, 4))
        spread_ref[...] = jnp.where(hit, 1.0, 0.0).astype(BF16)
        back_ref[...] = jnp.zeros_like(back_ref)
        push_ref[...] = jnp.zeros_like(push_ref)
        u_ref[...] = jnp.zeros_like(u_ref)
        lu_ref[...] = jnp.zeros_like(lu_ref)
        for b in range(halves):
            flag = jnp.transpose(jnp.broadcast_to(flags_ref[b:b + 1, :], (height, BLK)))
            hard_ref[b] = jnp.where(flag == 1, plastic_hardening, 1.0).astype(F32)
        fetches[6].wait()
        lax.fori_loop(0, rows, split, 0)

    pl.semaphore_wait(barrier, n_vol - 1 + n_zone - 1)
    for v in range(1, n_vol):
        pl.semaphore_signal(here, inc=1, device_id={"vol": at_vol(v)})

    def remote(src, dst, send, recv, target):
        return pltpu.make_async_remote_copy(
            src_ref=src, dst_ref=dst, send_sem=send, recv_sem=recv, device_id=target
        )

    def await_bytes(ref, sem):
        pltpu.make_async_copy(ref, ref, sem).wait()

    def slots_of(z):
        return pl.ds(z * CAP, CAP)

    def group_rows(g):
        return pl.ds(pl.multiple_of(PAD + g * 8, 8), 8)

    def tile_rows(g):
        return pl.ds(pl.multiple_of(g * 8, 8), 8)

    def sum_tiles(body, count):
        def group(g, sums):
            added = []
            for c in range(comps):
                for b in range(halves):
                    terms = body(c, b, group_rows(g), tile_rows(g))
                    added += [total + term for total, term in zip(sums[c * halves + b], terms)]
            return tuple(tuple(added[i:i + count]) for i in range(0, len(added), count))

        start = tuple(tuple(zero for _ in range(count)) for _ in range(comps * halves))
        sums = lax.fori_loop(0, groups, group, start, unroll=4)
        return [total_of([tile[i] for tile in sums]) for i in range(count)]

    def total_of(terms):
        while len(terms) > 1:
            terms = [sum(terms[i:i + 2][1:], terms[i]) for i in range(0, len(terms), 2)]
        return terms[0]

    def send_surface(it, tile, landing):
        for c in range(comps):
            for b in range(halves):
                surf_ref[pl.ds(b * 8 + c, SROWS, stride=8 * halves), :] = tile(c, b)
        for m in range(blocks):
            block_ref[m] = surf_ref[m * 8:m * 8 + 8, :]
        for step in (4, 3, 5, 2, 6, 1, 7, 0):
            z = at_zone(step)
            for k in range(CAP):
                block = block_ref[pack_tab[z * CAP + k]][0:4]
                if step:
                    fsend[it, step, k] = block
                else:
                    landing[zone * CAP + k] = block
            if step:
                remote(fsend.at[it, step], landing.at[slots_of(zone)], fs.at[it], fr.at[it], {"zone": z}).start()

    def send_field(j, it, landing):
        send_surface(it, lambda c, b: x_ref[j, c, b, PAD:PAD + SROWS, :], landing)

    def send_row(j, it, end):
        at = PAD + (height - 1 if end else 0)
        for c in range(comps):
            for b in range(halves):
                i = c * halves + b
                rsend[it, end, i:i + 1, :] = x_ref[j, c, b, at:at + 1, :]
        if end == 0:
            own_ref[j, 0] = rsend[it, 0]
        ship_row(it, end)

    def ship_row(it, end):
        target = at_vol(1 if end else n_vol - 1)
        remote(
            rsend.at[it, end], rrecv.at[it, 1 - end], rs.at[it, end], rr.at[it, 1 - end], {"vol": target}
        ).start()

    def strip_of(field, end, chosen, strip):
        b, column = (halves - 1, BLK - 1) if end else (0, 0)
        for c in range(comps):
            for g in chosen:
                tile = field[c, b, PAD + g * 8:PAD + g * 8 + 8, :]
                strip = jnp.where(
                    lane == c * groups + g, jnp.broadcast_to(tile[:, column:column + 1], (8, BLK)), strip
                )
        return strip

    def pack_strips(j, it, chosen, strips):
        for end in range(2):
            csend[it, end] = strip_of(x_ref.at[j], end, chosen, strips(end))

    def send_strips(j, it):
        pack_strips(j, it, range(1), lambda end: csend[it, end])
        own_ref[j, 1] = csend[it, 0]
        ship_strips(it)

    def ship_strips(it):
        remote(csend.at[it, 0], crecv.at[it, 1], cs.at[it], cr.at[it], {"zone": at_zone(n_zone - 1)}).start()
        remote(csend.at[it, 1], crecv.at[it, 0], cs.at[it], cr.at[it], {"zone": at_zone(1)}).start()

    def take_row(j, it, end):
        await_bytes(rrecv.at[it, end], rr.at[it, end])
        halo_ref[j, end] = jnp.where(vol == (n_vol - 1 if end else 0), 0.0, rrecv[it, end])

    def take_strips(j, it):
        await_bytes(crecv.at[it], cr.at[it])
        halo_ref[j, 2] = jnp.where(zone == 0, 0.0, crecv[it, 0])
        halo_ref[j, 3] = jnp.where(zone == n_zone - 1, 0.0, crecv[it, 1])

    def apply_row(field, offset, end, halo):
        at = offset + (height - 1 if end else 0)
        for c in range(comps):
            for b in range(halves):
                i = c * halves + b
                field[c, b, at:at + 1, :] = field[c, b, at:at + 1, :] - halo[i:i + 1]

    def apply_strips(field, offset, left, right, chosen):
        for halo, b, column in ((left, 0, 0), (right, halves - 1, BLK - 1)):
            for c in range(comps):
                for g in chosen:
                    i = c * groups + g
                    at = slice(offset + g * 8, offset + g * 8 + 8)
                    spread = jnp.broadcast_to(halo[:, i:i + 1], (8, BLK))
                    image = field[c, b, at, :]
                    field[c, b, at, :] = jnp.where(lane == column, image - spread, image)

    def inner(j, sums=False):
        def group(g, totals):
            totals = list(totals)
            for c in range(comps):
                tiles = [x_ref[j, c, b, group_rows(g), :] for b in range(halves)]
                to_right = [pltpu.roll(tile, 1, axis=1) for tile in tiles]
                to_left = [pltpu.roll(tile, BLK - 1, axis=1) for tile in tiles]
                for b in range(halves):
                    x = tiles[b]
                    before = to_right[b - 1] if b > 0 else zero
                    after = to_left[b + 1] if b < halves - 1 else zero
                    left = jnp.where(lane == 0, before, to_right[b])
                    right = jnp.where(lane == BLK - 1, after, to_left[b])
                    over = x_ref[j, c, b, pl.ds(PAD + g * 8 - 1, 8), :]
                    under = x_ref[j, c, b, pl.ds(PAD + g * 8 + 1, 8), :]
                    part = 4.0 * x - ((over + under) + (left + right))
                    l_ref[j, c, b, tile_rows(g), :] = part
                    if sums:
                        i = 2 * (c * halves + b)
                        totals[i] = totals[i] + x * x
                        totals[i + 1] = totals[i + 1] + x * (part + d_ref[c, b, tile_rows(g), :] * x)
            return tuple(totals)

        start = (zero,) * (2 * comps * halves if sums else 0)
        totals = lax.fori_loop(0, groups, group, start, unroll=4)
        return [total_of(list(totals[i::2])) for i in range(2)] if sums else None

    def image(j, c, b, at, padded):
        part = l_ref[j, c, b, at, :]
        return part + d_ref[c, b, at, :] * x_ref[j, c, b, padded, :] if j < KRY - 1 else part

    def first_rows(j):
        for c in range(comps):
            for b in range(halves):
                at = slice(PAD, PAD + SROWS)
                x_ref[j + 1, c, b, at, :] = image(j, c, b, slice(0, SROWS), at)
        field = x_ref.at[j + 1]
        apply_row(field, PAD, 0, halo_ref[j, 0])
        apply_strips(field, PAD, halo_ref[j, 2], halo_ref[j, 3], range(1))

    def other_rows(j):
        def group(g, _):
            for c in range(comps):
                for b in range(halves):
                    x_ref[j + 1, c, b, group_rows(g), :] = image(j, c, b, tile_rows(g), group_rows(g))
            return 0

        lax.fori_loop(1, groups, group, 0, unroll=5)
        field = x_ref.at[j + 1]
        apply_row(field, PAD, 1, halo_ref[j, 1])
        apply_strips(field, PAD, halo_ref[j, 2], halo_ref[j, 3], range(1, groups))

    upper = lax.broadcasted_iota(jnp.int32, (8, NNZ * BLK), 0) < 4
    contract_last = (((1,), (1,)), ((), ()))

    def split_rows(piece):
        high = piece.astype(BF16).astype(F32)
        rest = piece - high
        middle = rest.astype(BF16).astype(F32)
        return jnp.concatenate([high, middle, rest - middle, jnp.zeros_like(piece)], axis=0).astype(BF16)

    def join_rows(product):
        product = product[0:8] + product[8:16]
        return product + pltpu.roll(product, 4, axis=0)

    def fill_slots(j, n):
        it = n * KRY + j
        await_bytes(frecv[j].at[n, 0:(n_zone - 1) * CAP], fr.at[it])
        slot_ref[j] = frecv[j][n] + bsend[it - 1] if j else frecv[j][n]

    def find_gaps(j):
        for r in range(rows):
            picked = split_rows(jnp.concatenate([slot_ref[j, link(r, k)] for k in range(NNZ)], axis=1))
            gap = lax.dot_general(picked, mhl_ref[r], contract_last, preferred_element_type=F32)
            gap_ref[j, r * 8:r * 8 + 8, :] = join_rows(gap[:, 0:BLK] + gap[:, BLK:2 * BLK])

    def push_forces(j, n):
        it = n * KRY + j
        for r in range(rows):
            at = slice(r * 8, r * 8 + 8)
            multiplier = split_rows((scale_ref[at, :] * gap_ref[j, at, :])[0:4])
            multiplier = jnp.concatenate([multiplier, multiplier], axis=1)
            force = join_rows(jnp.dot(multiplier, mhl_ref[r], preferred_element_type=F32))
            high = force.astype(BF16).astype(F32)
            rest = force - high
            middle = rest.astype(BF16).astype(F32)
            two = jnp.where(upper, high, middle)
            low = (rest - middle)[0:4]
            for k in range(NNZ):
                entry = r * NNZ + k
                part = slice(k * BLK, (k + 1) * BLK)
                push_ref[entry * 8:entry * 8 + 8, :] = two[:, part]
                to = rows * NNZ * 8 + entry * 4
                push_ref[to:to + 4, :] = low[:, part]
        summed = jnp.dot(spread_ref[...], push_ref[...].astype(BF16), preferred_element_type=F32)
        bsend[it] = summed.reshape(n_zone * CAP, 4, BLK)
        for step in (4, 3, 5, 2, 6, 1, 7):
            z = at_zone(step)
            remote(
                bsend.at[it, slots_of(z)], brecv[j].at[n, slots_of(zone)], bs.at[it], br.at[it], {"zone": z}
            ).start()
        brecv[j][n, slots_of(zone)] = bsend[it, slots_of(zone)]

    def receive_forces(j, n):
        await_bytes(brecv[j].at[n, 0:(n_zone - 1) * CAP], br.at[n * KRY + j])
        for m in range(blocks):
            back_ref[m * 8:m * 8 + 4, :] = brecv[j][n, unpack_tab[m]]
        for c in range(comps):
            for b in range(halves):
                contact_ref[j, c, b] = back_ref[pl.ds(b * 8 + c, SROWS, stride=8 * halves), :]

    def energy(gaps):
        terms = []
        for r in range(rows):
            at = slice(r * 8, r * 8 + 8)
            gap = gaps(at)
            terms.append(scale_ref[at, :] * (gap * gap))
        return 0.5 * total_of(terms)

    def start_sums(it, gamma, delta, cross):
        parts = []
        for part in (gamma, delta, cross):
            part = part + pltpu.roll(part, 64, axis=1)
            parts.append(part + pltpu.roll(part, 32, axis=1))
        mixed = jnp.where(lane < 32, parts[0], jnp.where(lane < 64, parts[1], parts[2]))
        mixed = jnp.sum(mixed, axis=0, keepdims=True)
        me = vol * n_zone + zone
        ssend[it] = mixed
        srecv[it, me] = mixed
        for v, z in others:
            target = {"vol": at_vol(v), "zone": at_zone(z)}
            remote(ssend.at[it], srecv.at[it, me], ss.at[it], sr.at[it], target).start()

    def finish_sums(it):
        await_bytes(srecv.at[it, 0:devices - 1], sr.at[it])
        total = srecv[it]
        while total.shape[0] > 1:
            half = total.shape[0] // 2
            total = total[:half] + total[half:]
        total = total[0]
        place = lane[0:1]
        return [
            jnp.sum(jnp.where(place // 32 == i, total, 0.0), axis=1, keepdims=True) for i in range(3)
        ]

    def full(scalar):
        return jnp.broadcast_to(scalar, (8, BLK))

    def add_contact(j):
        for c in range(comps):
            for b in range(halves):
                at = slice(PAD, PAD + SROWS)
                x_ref[j + 1, c, b, at, :] = x_ref[j + 1, c, b, at, :] + contact_ref[j, c, b]

    def edges(mix):
        return 2.0 * (
            mix(lambda j: own_ref[j, 0]) * mix(lambda j: halo_ref[j, 0])
            + mix(lambda j: own_ref[j, 1]) * mix(lambda j: halo_ref[j, 2])
        )

    def newton(n, _):
        it = n * KRY

        gamma, delta = inner(0, sums=True)

        @pl.when(n == 0)
        def _():
            fill_slots(0, 0)
            find_gaps(0)
            push_forces(0, 0)
            take_row(0, 0, 0)
            take_strips(0, 0)


        @pl.when(n == 0)
        def _():
            pl.semaphore_wait(here, n_vol - 1)

        first_rows(0)
        send_field(1, it + 1, frecv[1].at[n])
        delta = delta + energy(lambda at: gap_ref[0, at, :]) - edges(lambda part: part(0))
        start_sums(it, gamma, delta, zero)

        @pl.when(n == 0)
        def _():
            take_row(0, 0, 1)

        @pl.when(n > 0)
        def _():
            take_row(KRY, KRY, 1)
            derive_halo(1)

        other_rows(0)
        send_row(1, it + 1, 1)
        pack_strips(1, it + 1, range(1, groups), lambda end: zero)
        receive_forces(0, n)
        add_contact(0)
        send_strips(1, it + 1)
        send_row(1, it + 1, 0)
        inner(1)
        fill_slots(1, n)
        find_gaps(1)
        push_forces(1, n)
        take_row(1, it + 1, 0)
        take_strips(1, it + 1)
        first_rows(1)
        send_field(2, it + 2, frecv[2].at[n])
        gamma0, pq0, _ = finish_sums(it)
        a0 = gamma0 / pq0
        w0 = full(a0)

        def dots1(c, b, padded, at):
            x1 = x_ref[1, c, b, padded, :]
            r = x_ref[0, c, b, padded, :] - w0 * x1
            r_ref[c, b, at, :] = r
            q = (l_ref[0, c, b, at, :] - w0 * l_ref[1, c, b, at, :]) + d_ref[c, b, at, :] * r
            return r * r, r * q, r * x1

        gamma, delta, cross = sum_tiles(dots1, 3)
        delta = delta + energy(lambda at: gap_ref[0, at, :] - w0 * gap_ref[1, at, :])
        delta = delta - edges(lambda part: part(0) - w0 * part(1))
        start_sums(it + 1, gamma, delta, cross)
        take_row(1, it + 1, 1)
        other_rows(1)
        send_row(2, it + 2, 1)
        pack_strips(2, it + 2, range(1, groups), lambda end: zero)
        receive_forces(1, n)
        add_contact(1)
        send_strips(2, it + 2)
        send_row(2, it + 2, 0)
        inner(2)
        fill_slots(2, n)
        find_gaps(2)
        push_forces(2, n)
        gamma1, delta, cross = finish_sums(it + 1)
        beta1 = gamma1 / gamma0
        pq1 = delta + beta1 * (2.0 * cross + beta1 * pq0)
        a1 = gamma1 / pq1
        take_row(2, it + 2, 0)
        take_strips(2, it + 2)
        more, w1 = full(1.0 + beta1), full(a1)

        def second(x0, x1, x2):
            return (x0 - w0 * x1) - w1 * (more * x1 - w0 * x2)

        def dots2(c, b, padded, at):
            image = more * x_ref[1, c, b, padded, :] - w0 * x_ref[2, c, b, padded, :]
            r = r_ref[c, b, at, :] - w1 * image
            q = second(l_ref[0, c, b, at, :], l_ref[1, c, b, at, :], l_ref[2, c, b, at, :])
            q = q + d_ref[c, b, at, :] * r
            return r * r, r * q, r * image

        gamma, delta, cross = sum_tiles(dots2, 3)
        delta = delta + energy(lambda at: second(gap_ref[0, at, :], gap_ref[1, at, :], gap_ref[2, at, :]))
        delta = delta - edges(lambda part: second(part(0), part(1), part(2)))
        start_sums(it + 2, gamma, delta, cross)

        @pl.when(n < NEWTON - 1)
        def _():
            first_rows(2)
            send_field(KRY, KRY, frecv[0].at[1])

        take_row(2, it + 2, 1)

        @pl.when(n < NEWTON - 1)
        def _():
            other_rows(2)
            send_row(KRY, KRY, 1)
            pack_strips(KRY, KRY, range(1, groups), lambda end: zero)

        receive_forces(2, n)

        @pl.when(n < NEWTON - 1)
        def _():
            add_contact(2)
            send_strips(KRY, KRY)
            send_row(KRY, KRY, 0)

        gamma2, delta, cross = finish_sums(it + 2)
        beta2 = gamma2 / gamma1
        pq2 = delta + beta2 * (2.0 * cross + beta2 * pq1)
        a2 = gamma2 / pq2
        turned = beta2 * (1.0 + beta1)
        k0 = full(a0 + a1 * (1.0 + beta1) + a2 * (1.0 + turned))
        k1 = full(-(a1 * a0 + a2 * (a0 + a1 * (1.0 + beta1) + beta2 * a0)))
        k2 = full(a2 * a1 * a0)

        coef_ref[0], coef_ref[1], coef_ref[2] = k0, k1, k2

        @pl.when(n < NEWTON - 1)
        def _():
            derive_slots()
            find_gaps(0)
            push_forces(0, 1)

        def mix(fields):
            return k0 * fields(0) + k1 * fields(1) + k2 * fields(2)

        for c in range(comps):
            for b in range(halves):
                lu_ref[c, b, 0:SROWS, :] = lu_ref[c, b, 0:SROWS, :] + mix(lambda j: contact_ref[j, c, b])
        over, under, left, right = [mix(lambda j: halo_ref[j, i]) for i in range(4)]
        apply_row(lu_ref, 0, 0, over)
        apply_strips(lu_ref, 0, left, right, range(1))

        def finish(g, _):
            at = tile_rows(g)
            for b in range(halves):
                half = slice(b * BLK, (b + 1) * BLK)
                stiff, hard = stiff_ref[at, half], hard_ref[b, at, :]
                for c in range(comps):
                    u = u_ref[c, at, half] + mix(lambda j: x_ref[j, c, b, group_rows(g), :])
                    image = lu_ref[c, b, at, :] + mix(lambda j: l_ref[j, c, b, at, :])
                    bent = jnp.tanh(u / yield_scale)
                    material = stiff * (hard * u + (1.0 - hard) * yield_scale * bent)
                    residual = image + material - load_ref[c, at, half]
                    u_ref[c, at, half] = u
                    res_ref[c, at, half] = residual
                    lu_ref[c, b, at, :] = image
                    x_ref[0, c, b, group_rows(g), :] = -residual
                    d_ref[c, b, at, :] = stiff * (hard + (1.0 - hard) * (1.0 - bent * bent))
            return 0

        finish(0, 0)
        apply_row(lu_ref, 0, 1, under)
        apply_strips(lu_ref, 0, left, right, range(1, groups))
        lax.fori_loop(1, groups, finish, 0, unroll=3)

        @pl.when(n < NEWTON - 1)
        def _():
            for c in range(comps):
                for b in range(halves):
                    i = c * halves + b
                    own_ref[0, 0, i:i + 1, :] = x_ref[0, c, b, PAD:PAD + 1, :]
            own_ref[0, 1] = strip_of(x_ref.at[0], 0, range(groups), zero)
            take_row(KRY, KRY, 0)
            take_strips(KRY, KRY)
            await_bytes(crecv.at[STEPS], cr.at[STEPS])
            for i in (0, 2, 3):
                derive_halo(i)

        return 0

    def next_residual(loads, stiff, hard, first, second, third, last):
        k0, k1, k2 = [coef_ref[j] for j in range(KRY)]
        if len(first.shape) == 3:
            k0, k1, k2 = k0[0:4][None], k1[0:4][None], k2[0:4][None]
        u = k0 * first + k1 * second + k2 * third
        moved = k0 * (second - stiff * first) + k1 * (third - stiff * second) + k2 * last
        material = stiff * (hard * u + (1.0 - hard) * yield_scale * jnp.tanh(u / yield_scale))
        return loads - (moved + material)

    def derive_slots():
        await_bytes(fixed.at[0:(n_zone - 1) * CAP], fr.at[STEPS])
        await_bytes(frecv[0].at[1, 0:(n_zone - 1) * CAP], fr.at[KRY])
        stiff = jnp.broadcast_to(fixed[:, 0:1, :], fixed.shape)
        hard = jnp.broadcast_to(fixed[:, 1:2, :], fixed.shape)
        fields = [slot_ref[j] for j in range(KRY)]
        slot_ref[0] = next_residual(fields[0], stiff, hard, *fields, frecv[0][1] + bsend[KRY - 1])

    def derive_halo(i):
        if i < 2:
            await_bytes(rrecv.at[STEPS, i], rr.at[STEPS, i])
            packed = rrecv[STEPS, i]
            stiff, hard = [
                jnp.where(
                    sub < comps * halves,
                    jnp.where(lax.rem(sub, halves) == 0, packed[e:e + 1], packed[e + 1:e + 2]), 0.0,
                )
                for e in (0, halves)
            ]
        else:
            packed = crecv[STEPS, i - 2]
            parts = [
                jnp.where(lane < groups, packed, 0.0),
                jnp.where(lane < groups, pltpu.roll(packed, BLK - groups, axis=1), 0.0),
            ]
            stiff, hard = [
                part + pltpu.roll(part, groups, axis=1) + pltpu.roll(part, 2 * groups, axis=1) for part in parts
            ]
        fields = [halo_ref[j, i] for j in range(KRY + 1)]
        halo_ref[0, i] = next_residual(fields[0], stiff, hard, *fields)

    def send_fixed():
        def tile(c, b):
            if c == 0:
                return stiff_ref[0:SROWS, b * BLK:(b + 1) * BLK]
            return hard_ref[b, 0:SROWS, :] if c == 1 else zero

        send_surface(STEPS, tile, fixed)
        for end, at in ((0, 0), (1, height - 1)):
            for b in range(halves):
                rsend[STEPS, end, b:b + 1, :] = stiff_ref[at:at + 1, b * BLK:(b + 1) * BLK]
                rsend[STEPS, end, halves + b:halves + b + 1, :] = hard_ref[b, at:at + 1, :]
            ship_row(STEPS, end)
        for end, b, column in ((0, 0, 0), (1, halves - 1, BLK - 1)):
            strip = zero
            for g in range(groups):
                at = slice(g * 8, g * 8 + 8)
                for e, tile8 in ((0, stiff_ref[at, b * BLK:(b + 1) * BLK]), (groups, hard_ref[b, at, :])):
                    strip = jnp.where(
                        lane == e + g, jnp.broadcast_to(tile8[:, column:column + 1], (8, BLK)), strip
                    )
            csend[STEPS, end] = strip
        ship_strips(STEPS)

    own_ref[0, 0] = zero
    send_row(0, 0, 1)
    send_field(0, 0, frecv[0].at[0])
    pack_strips(0, 0, range(1, groups), lambda end: zero)
    send_strips(0, 0)
    send_row(0, 0, 0)
    set_up()
    send_fixed()
    lax.fori_loop(0, NEWTON, newton, 0)

    def drain(it, _):
        await_bytes(fsend.at[it, 0:n_zone - 1], fs.at[it])
        for end in range(2):
            await_bytes(rsend.at[it, end], rs.at[it, end])
        await_bytes(csend.at[it], cs.at[it])
        return 0

    def drain_sums(it, _):
        await_bytes(bsend.at[it, 0:(n_zone - 1) * CAP], bs.at[it])
        await_bytes(srecv.at[it, 0:devices - 1], ss.at[it])
        return 0

    lax.fori_loop(0, STEPS + 1, drain, 0)
    lax.fori_loop(0, STEPS, drain_sums, 0)


def local(n_vol, n_zone, load, support_stiffness, plastic_flags, owner_map, pattern, active, mortar):
    comps, height, breadth = load.shape
    halves = breadth // BLK
    rows = active.shape[2]
    field = pltpu.VMEM((comps, halves, height, BLK), F32)
    slots = n_zone * CAP
    landing = pltpu.VMEM((NEWTON, slots, 4, BLK), F32)
    blocks = SROWS * halves
    devices = n_vol * n_zone
    wide = -(-rows * NNZ * 12 // BLK) * BLK
    dma = pltpu.SemaphoreType.DMA
    vmem = pl.BlockSpec(memory_space=pltpu.VMEM)
    hbm = pl.BlockSpec(memory_space=pltpu.HBM)
    flags = plastic_flags.T
    links = jnp.transpose(pattern, (0, 3, 1, 2))
    operands = (load, support_stiffness, flags, owner_map, links, active, mortar)
    return pl.pallas_call(
        functools.partial(kernel, n_vol, n_zone),
        out_shape=[jax.ShapeDtypeStruct(load.shape, F32)] * 2,
        in_specs=[hbm] * 7,
        out_specs=[vmem, vmem],
        scratch_shapes=[
            pltpu.VMEM(load.shape, F32),
            pltpu.VMEM(support_stiffness.shape, F32),
            pltpu.VMEM(flags.shape, jnp.int32),
            pltpu.SMEM(owner_map.shape, jnp.int32),
            pltpu.SMEM(links.shape, jnp.int32),
            pltpu.SMEM(active.shape, jnp.int32),
            pltpu.VMEM(mortar.shape[2:], F32),
            pltpu.VMEM((KRY + 1, comps, halves, height + 2 * PAD, BLK), F32),
            pltpu.VMEM((KRY, comps, halves, height, BLK), F32),
            field, field, field,
            pltpu.VMEM((halves, height, BLK), F32),
            pltpu.VMEM((KRY, comps, halves, SROWS, BLK), F32),
            pltpu.VMEM((KRY + 1, 4, 8, BLK), F32),
            pltpu.VMEM((KRY + 1, 2, 8, BLK), F32),
            pltpu.VMEM((KRY, slots, 4, BLK), F32),
            pltpu.VMEM((KRY, 8, BLK), F32),
            pltpu.VMEM((KRY, rows * 8, BLK), F32),
            pltpu.VMEM((rows * 8, BLK), F32),
            pltpu.VMEM((rows, 2 * BLK, NNZ * BLK), BF16),
            pltpu.VMEM((slots * 4, wide), BF16),
            pltpu.VMEM((wide, BLK), F32),
            pltpu.VMEM((blocks * 8, BLK), F32),
            pltpu.VMEM((blocks + 1, 8, BLK), F32),
            pltpu.VMEM((blocks * 8, BLK), F32),
            pltpu.SMEM((slots,), jnp.int32),
            pltpu.SMEM((blocks,), jnp.int32),
            pltpu.VMEM((STEPS + 1, n_zone, CAP, 4, BLK), F32),
            landing, landing, landing,
            pltpu.VMEM((slots, 4, BLK), F32),
            pltpu.VMEM((STEPS, slots, 4, BLK), F32),
            landing, landing, landing,
            pltpu.VMEM((STEPS + 1, 2, 8, BLK), F32),
            pltpu.VMEM((STEPS + 1, 2, 8, BLK), F32),
            pltpu.VMEM((STEPS + 1, 2, 8, BLK), F32),
            pltpu.VMEM((STEPS + 1, 2, 8, BLK), F32),
            pltpu.VMEM((STEPS, 1, BLK), F32),
            pltpu.VMEM((STEPS, devices, 1, BLK), F32),
            pltpu.SemaphoreType.REGULAR,
            dma((7,)),
        ] + [dma((STEPS + 1,))] * 4 + [dma((STEPS + 1, 2))] * 2 + [dma((STEPS + 1,))] * 4,
        compiler_params=pltpu.CompilerParams(
            collective_id=0, has_side_effects=True, vmem_limit_bytes=32 * 1024 * 1024
        ),
    )(*[pltpu.with_memory_space_constraint(a, pltpu.HBM) for a in operands])


def solution(mesh):
    in_specs = (
        P(None, "vol", "zone"),
        P("vol", "zone"),
        P("vol", "zone"),
        P("vol", "zone", None),
        P("vol", "zone", None, None),
        P("vol", "zone", None),
        P("vol", "zone", None, None, None, None),
    )
    out_specs = (P(None, "vol", "zone"), P(None, "vol", "zone"))
    body = functools.partial(local, mesh.shape["vol"], mesh.shape["zone"])
    return jax.shard_map(body, mesh=mesh, in_specs=in_specs, out_specs=out_specs, check_vma=False)
```

```python
import functools

import jax
import jax.numpy as jnp
from jax import lax
from jax.experimental import pallas as pl
from jax.experimental.pallas import tpu as pltpu
from jax.sharding import PartitionSpec as P

SROWS = 8
BLK = 128
NNZ = 3
CAP = 4
KRY = 3
NEWTON = 2
STEPS = KRY * NEWTON
PAD = 8

yield_scale = 0.5
penalty = 2.0
plastic_hardening = 0.2

F32 = jnp.float32
BF16 = jnp.bfloat16


def kernel(
    n_vol, n_zone,
    load_hbm, stiff_hbm, flags_hbm, owner_hbm, pattern_hbm, active_hbm, mortar_ref,
    u_ref, res_ref,
    load_ref, stiff_ref, flags_ref, owner_ref, pattern_ref, active_ref, mort_ref,
    x_ref, l_ref, r_ref, d_ref, lu_ref, hard_ref, contact_ref, halo_ref, own_ref, slot_ref, coef_ref, gap_ref, scale_ref,
    mhl_ref, spread_ref, push_ref,
    surf_ref, block_ref, back_ref,
    pack_tab, unpack_tab,
    fsend, frecv0, frecv1, frecv2, fixed, bsend, brecv0, brecv1, brecv2, rsend, rrecv, csend, crecv, ssend, srecv,
    here, in_sem, fs, fr, bs, br, rs, rr, cs, cr, ss, sr,
):
    frecv, brecv = (frecv0, frecv1, frecv2), (brecv0, brecv1, brecv2)
    comps, height = load_ref.shape[0], load_ref.shape[1]
    halves = load_ref.shape[2] // BLK
    groups = height // 8
    blocks = SROWS * halves
    rows = active_ref.shape[2]
    devices = n_vol * n_zone
    zone = lax.axis_index("zone")
    vol = lax.axis_index("vol")

    inputs = [
        (owner_hbm, owner_ref), (pattern_hbm, pattern_ref), (active_hbm, active_ref), (flags_hbm, flags_ref),
        (load_hbm, load_ref), (stiff_hbm, stiff_ref), (mortar_ref.at[0, 0], mort_ref),
    ]
    fetches = [pltpu.make_async_copy(src, dst, in_sem.at[i]) for i, (src, dst) in enumerate(inputs)]
    for fetch in fetches:
        fetch.start()

    def at_zone(step):
        return lax.rem(zone + step, n_zone) if step else zone

    def at_vol(step):
        return lax.rem(vol + step, n_vol) if step else vol

    side = 4

    def hops(offset):
        around = [offset[0] // side, offset[0] % side, (offset[1] + 1) // 2]
        return sum(min(a % side, side - a % side) for a in around)

    others = [(v, z) for v in range(n_vol) for z in range(n_zone) if (v, z) != (0, 0)]
    others.sort(key=lambda offset: -hops(offset))

    barrier = pltpu.get_barrier_semaphore()
    for v in (10, 9, 11, 6, 14, 8, 2, 5, 7, 13, 15, 4, 12, 1, 3):
        pl.semaphore_signal(barrier, inc=1, device_id={"vol": at_vol(v)})
    for z in (4, 3, 5, 2, 6, 1, 7):
        pl.semaphore_signal(barrier, inc=1, device_id={"zone": at_zone(z)})

    sub = lax.broadcasted_iota(jnp.int32, (8, BLK), 0)
    lane = lax.broadcasted_iota(jnp.int32, (8, BLK), 1)
    zero = jnp.zeros((8, BLK), F32)

    for fetch in fetches[:4]:
        fetch.wait()
    owners = [owner_ref[0, 0, m] for m in range(blocks)]
    weights = []
    for m in range(blocks):
        weight, rank = jnp.int32(1), jnp.int32(0)
        for e in range(m):
            same = owners[e] == owners[m]
            weight = jnp.where(same, weight * 32, weight)
            rank = rank + jnp.where(same, 1, 0)
        weights.append(weight)
        unpack_tab[m] = owners[m] * CAP + rank
    for z in range(n_zone):
        code = jnp.int32(0)
        for m in range(blocks):
            code = code + jnp.where(owners[m] == z, weights[m] * (blocks + m), 0)
        for k in range(CAP):
            field = lax.shift_right_logical(code, 5 * k) & 31
            pack_tab[z * CAP + k] = jnp.where(field >= blocks, field - blocks, blocks)

    def link(r, k):
        return pattern_ref[0, k, 0, r]

    surf_ref[...] = jnp.zeros_like(surf_ref)
    block_ref[blocks] = zero
    rsend[...] = jnp.zeros_like(rsend)
    for fetch in fetches[4:6]:
        fetch.wait()
    for c in range(comps):
        for b in range(halves):
            for j in range(KRY + 1):
                x_ref[j, c, b, 0:PAD, :] = jnp.zeros((PAD, BLK), F32)
                x_ref[j, c, b, PAD + height:, :] = jnp.zeros((PAD, BLK), F32)
            x_ref[0, c, b, PAD:PAD + height, :] = load_ref[c, :, b * BLK:(b + 1) * BLK]
            d_ref[c, b] = stiff_ref[:, b * BLK:(b + 1) * BLK]

    def split(r, _):
        for k in range(NNZ):
            piece = mort_ref[r, k] if k == 0 else -mort_ref[r, k]
            high = piece.astype(BF16)
            mhl_ref[r, 0:BLK, k * BLK:(k + 1) * BLK] = high
            mhl_ref[r, BLK:2 * BLK, k * BLK:(k + 1) * BLK] = (piece - high.astype(F32)).astype(BF16)
        return 0

    def set_up():
        pairs = rows * NNZ * 8
        wide = push_ref.shape[0]
        link_lane = lax.broadcasted_iota(jnp.int32, (1, wide), 1)
        tail = (link_lane - pairs) // 4
        entry = jnp.where(link_lane < pairs, link_lane // 8, jnp.where(tail < rows * NNZ, tail, -1))
        links = jnp.full((1, wide), -1, jnp.int32)
        for r in range(rows):
            scale_ref[r * 8:r * 8 + 8, :] = jnp.full((8, BLK), penalty * active_ref[0, 0, r].astype(F32))
            for k in range(NNZ):
                links = jnp.where(entry == r * NNZ + k, link(r, k), links)
        out_row = lax.broadcasted_iota(jnp.int32, (n_zone * CAP * 4, wide), 0)
        out_lane = lax.broadcasted_iota(jnp.int32, (n_zone * CAP * 4, wide), 1)
        hit = (out_row // 4 == links) & (lax.rem(out_row, 4) == lax.rem(out_lane, 4))
        spread_ref[...] = jnp.where(hit, 1.0, 0.0).astype(BF16)
        back_ref[...] = jnp.zeros_like(back_ref)
        push_ref[...] = jnp.zeros_like(push_ref)
        u_ref[...] = jnp.zeros_like(u_ref)
        lu_ref[...] = jnp.zeros_like(lu_ref)
        for b in range(halves):
            flag = jnp.transpose(jnp.broadcast_to(flags_ref[b:b + 1, :], (height, BLK)))
            hard_ref[b] = jnp.where(flag == 1, plastic_hardening, 1.0).astype(F32)
        fetches[6].wait()
        lax.fori_loop(0, rows, split, 0)

    pl.semaphore_wait(barrier, n_vol - 1 + n_zone - 1)
    for v in range(1, n_vol):
        pl.semaphore_signal(here, inc=1, device_id={"vol": at_vol(v)})

    def remote(src, dst, send, recv, target):
        return pltpu.make_async_remote_copy(
            src_ref=src, dst_ref=dst, send_sem=send, recv_sem=recv, device_id=target
        )

    def await_bytes(ref, sem):
        pltpu.make_async_copy(ref, ref, sem).wait()

    def slots_of(z):
        return pl.ds(z * CAP, CAP)

    def group_rows(g):
        return pl.ds(pl.multiple_of(PAD + g * 8, 8), 8)

    def tile_rows(g):
        return pl.ds(pl.multiple_of(g * 8, 8), 8)

    def sum_tiles(body, count):
        def group(g, sums):
            added = []
            for c in range(comps):
                for b in range(halves):
                    terms = body(c, b, group_rows(g), tile_rows(g))
                    added += [total + term for total, term in zip(sums[c * halves + b], terms)]
            return tuple(tuple(added[i:i + count]) for i in range(0, len(added), count))

        start = tuple(tuple(zero for _ in range(count)) for _ in range(comps * halves))
        sums = lax.fori_loop(0, groups, group, start, unroll=4)
        return [total_of([tile[i] for tile in sums]) for i in range(count)]

    def total_of(terms):
        while len(terms) > 1:
            terms = [sum(terms[i:i + 2][1:], terms[i]) for i in range(0, len(terms), 2)]
        return terms[0]

    def send_surface(it, tile, landing):
        for c in range(comps):
            for b in range(halves):
                surf_ref[pl.ds(b * 8 + c, SROWS, stride=8 * halves), :] = tile(c, b)
        for m in range(blocks):
            block_ref[m] = surf_ref[m * 8:m * 8 + 8, :]
        for step in (4, 3, 5, 2, 6, 1, 7, 0):
            z = at_zone(step)
            for k in range(CAP):
                block = block_ref[pack_tab[z * CAP + k]][0:4]
                if step:
                    fsend[it, step, k] = block
                else:
                    landing[zone * CAP + k] = block
            if step:
                remote(fsend.at[it, step], landing.at[slots_of(zone)], fs.at[it], fr.at[it], {"zone": z}).start()

    def send_field(j, it, landing):
        send_surface(it, lambda c, b: x_ref[j, c, b, PAD:PAD + SROWS, :], landing)

    def send_row(j, it, end):
        at = PAD + (height - 1 if end else 0)
        for c in range(comps):
            for b in range(halves):
                i = c * halves + b
                rsend[it, end, i:i + 1, :] = x_ref[j, c, b, at:at + 1, :]
        if end == 0:
            own_ref[j, 0] = rsend[it, 0]
        ship_row(it, end)

    def ship_row(it, end):
        target = at_vol(1 if end else n_vol - 1)
        remote(
            rsend.at[it, end], rrecv.at[it, 1 - end], rs.at[it, end], rr.at[it, 1 - end], {"vol": target}
        ).start()

    def strip_of(field, end, chosen, strip):
        b, column = (halves - 1, BLK - 1) if end else (0, 0)
        for c in range(comps):
            for g in chosen:
                tile = field[c, b, PAD + g * 8:PAD + g * 8 + 8, :]
                strip = jnp.where(
                    lane == c * groups + g, jnp.broadcast_to(tile[:, column:column + 1], (8, BLK)), strip
                )
        return strip

    def pack_strips(j, it, chosen, strips):
        for end in range(2):
            csend[it, end] = strip_of(x_ref.at[j], end, chosen, strips(end))

    def send_strips(j, it):
        pack_strips(j, it, range(1), lambda end: csend[it, end])
        own_ref[j, 1] = csend[it, 0]
        ship_strips(it)

    def ship_strips(it):
        remote(csend.at[it, 0], crecv.at[it, 1], cs.at[it], cr.at[it], {"zone": at_zone(n_zone - 1)}).start()
        remote(csend.at[it, 1], crecv.at[it, 0], cs.at[it], cr.at[it], {"zone": at_zone(1)}).start()

    def take_row(j, it, end):
        await_bytes(rrecv.at[it, end], rr.at[it, end])
        halo_ref[j, end] = jnp.where(vol == (n_vol - 1 if end else 0), 0.0, rrecv[it, end])

    def take_strips(j, it):
        await_bytes(crecv.at[it], cr.at[it])
        halo_ref[j, 2] = jnp.where(zone == 0, 0.0, crecv[it, 0])
        halo_ref[j, 3] = jnp.where(zone == n_zone - 1, 0.0, crecv[it, 1])

    def apply_row(field, offset, end, halo):
        at = offset + (height - 1 if end else 0)
        for c in range(comps):
            for b in range(halves):
                i = c * halves + b
                field[c, b, at:at + 1, :] = field[c, b, at:at + 1, :] - halo[i:i + 1]

    def apply_strips(field, offset, left, right, chosen):
        for halo, b, column in ((left, 0, 0), (right, halves - 1, BLK - 1)):
            for c in range(comps):
                for g in chosen:
                    i = c * groups + g
                    at = slice(offset + g * 8, offset + g * 8 + 8)
                    spread = jnp.broadcast_to(halo[:, i:i + 1], (8, BLK))
                    image = field[c, b, at, :]
                    field[c, b, at, :] = jnp.where(lane == column, image - spread, image)

    def inner(j, sums=False):
        def group(g, totals):
            totals = list(totals)
            for c in range(comps):
                tiles = [x_ref[j, c, b, group_rows(g), :] for b in range(halves)]
                to_right = [pltpu.roll(tile, 1, axis=1) for tile in tiles]
                to_left = [pltpu.roll(tile, BLK - 1, axis=1) for tile in tiles]
                for b in range(halves):
                    x = tiles[b]
                    before = to_right[b - 1] if b > 0 else zero
                    after = to_left[b + 1] if b < halves - 1 else zero
                    left = jnp.where(lane == 0, before, to_right[b])
                    right = jnp.where(lane == BLK - 1, after, to_left[b])
                    over = x_ref[j, c, b, pl.ds(PAD + g * 8 - 1, 8), :]
                    under = x_ref[j, c, b, pl.ds(PAD + g * 8 + 1, 8), :]
                    part = 4.0 * x - ((over + under) + (left + right))
                    l_ref[j, c, b, tile_rows(g), :] = part
                    if sums:
                        i = 2 * (c * halves + b)
                        totals[i] = totals[i] + x * x
                        totals[i + 1] = totals[i + 1] + x * (part + d_ref[c, b, tile_rows(g), :] * x)
            return tuple(totals)

        start = (zero,) * (2 * comps * halves if sums else 0)
        totals = lax.fori_loop(0, groups, group, start, unroll=4)
        return [total_of(list(totals[i::2])) for i in range(2)] if sums else None

    def image(j, c, b, at, padded):
        part = l_ref[j, c, b, at, :]
        return part + d_ref[c, b, at, :] * x_ref[j, c, b, padded, :] if j < KRY - 1 else part

    def first_rows(j):
        for c in range(comps):
            for b in range(halves):
                at = slice(PAD, PAD + SROWS)
                x_ref[j + 1, c, b, at, :] = image(j, c, b, slice(0, SROWS), at)
        field = x_ref.at[j + 1]
        apply_row(field, PAD, 0, halo_ref[j, 0])
        apply_strips(field, PAD, halo_ref[j, 2], halo_ref[j, 3], range(1))

    def other_rows(j):
        def group(g, _):
            for c in range(comps):
                for b in range(halves):
                    x_ref[j + 1, c, b, group_rows(g), :] = image(j, c, b, tile_rows(g), group_rows(g))
            return 0

        lax.fori_loop(1, groups, group, 0, unroll=5)
        field = x_ref.at[j + 1]
        apply_row(field, PAD, 1, halo_ref[j, 1])
        apply_strips(field, PAD, halo_ref[j, 2], halo_ref[j, 3], range(1, groups))

    upper = lax.broadcasted_iota(jnp.int32, (8, NNZ * BLK), 0) < 4
    contract_last = (((1,), (1,)), ((), ()))

    def split_rows(piece):
        high = piece.astype(BF16).astype(F32)
        rest = piece - high
        middle = rest.astype(BF16).astype(F32)
        return jnp.concatenate([high, middle, rest - middle, jnp.zeros_like(piece)], axis=0).astype(BF16)

    def join_rows(product):
        product = product[0:8] + product[8:16]
        return product + pltpu.roll(product, 4, axis=0)

    def fill_slots(j, n):
        it = n * KRY + j
        await_bytes(frecv[j].at[n, 0:(n_zone - 1) * CAP], fr.at[it])
        slot_ref[j] = frecv[j][n] + bsend[it - 1] if j else frecv[j][n]

    def find_gaps(j):
        for r in range(rows):
            picked = split_rows(jnp.concatenate([slot_ref[j, link(r, k)] for k in range(NNZ)], axis=1))
            gap = lax.dot_general(picked, mhl_ref[r], contract_last, preferred_element_type=F32)
            gap_ref[j, r * 8:r * 8 + 8, :] = join_rows(gap[:, 0:BLK] + gap[:, BLK:2 * BLK])

    def push_forces(j, n):
        it = n * KRY + j
        for r in range(rows):
            at = slice(r * 8, r * 8 + 8)
            multiplier = split_rows((scale_ref[at, :] * gap_ref[j, at, :])[0:4])
            multiplier = jnp.concatenate([multiplier, multiplier], axis=1)
            force = join_rows(jnp.dot(multiplier, mhl_ref[r], preferred_element_type=F32))
            high = force.astype(BF16).astype(F32)
            rest = force - high
            middle = rest.astype(BF16).astype(F32)
            two = jnp.where(upper, high, middle)
            low = (rest - middle)[0:4]
            for k in range(NNZ):
                entry = r * NNZ + k
                part = slice(k * BLK, (k + 1) * BLK)
                push_ref[entry * 8:entry * 8 + 8, :] = two[:, part]
                to = rows * NNZ * 8 + entry * 4
                push_ref[to:to + 4, :] = low[:, part]
        summed = jnp.dot(spread_ref[...], push_ref[...].astype(BF16), preferred_element_type=F32)
        bsend[it] = summed.reshape(n_zone * CAP, 4, BLK)
        for step in (4, 3, 5, 2, 6, 1, 7):
            z = at_zone(step)
            remote(
                bsend.at[it, slots_of(z)], brecv[j].at[n, slots_of(zone)], bs.at[it], br.at[it], {"zone": z}
            ).start()
        brecv[j][n, slots_of(zone)] = bsend[it, slots_of(zone)]

    def receive_forces(j, n):
        await_bytes(brecv[j].at[n, 0:(n_zone - 1) * CAP], br.at[n * KRY + j])
        for m in range(blocks):
            back_ref[m * 8:m * 8 + 4, :] = brecv[j][n, unpack_tab[m]]
        for c in range(comps):
            for b in range(halves):
                contact_ref[j, c, b] = back_ref[pl.ds(b * 8 + c, SROWS, stride=8 * halves), :]

    def energy(gaps):
        terms = []
        for r in range(rows):
            at = slice(r * 8, r * 8 + 8)
            gap = gaps(at)
            terms.append(scale_ref[at, :] * (gap * gap))
        return 0.5 * total_of(terms)

    def start_sums(it, gamma, delta, cross):
        parts = []
        for part in (gamma, delta, cross):
            part = part + pltpu.roll(part, 64, axis=1)
            parts.append(part + pltpu.roll(part, 32, axis=1))
        mixed = jnp.where(lane < 32, parts[0], jnp.where(lane < 64, parts[1], parts[2]))
        mixed = jnp.sum(mixed, axis=0, keepdims=True)
        me = vol * n_zone + zone
        ssend[it] = mixed
        srecv[it, me] = mixed
        for v, z in others:
            target = {"vol": at_vol(v), "zone": at_zone(z)}
            remote(ssend.at[it], srecv.at[it, me], ss.at[it], sr.at[it], target).start()

    def finish_sums(it):
        await_bytes(srecv.at[it, 0:devices - 1], sr.at[it])
        total = srecv[it]
        while total.shape[0] > 1:
            half = total.shape[0] // 2
            total = total[:half] + total[half:]
        total = total[0]
        place = lane[0:1]
        return [
            jnp.sum(jnp.where(place // 32 == i, total, 0.0), axis=1, keepdims=True) for i in range(3)
        ]

    def full(scalar):
        return jnp.broadcast_to(scalar, (8, BLK))

    def add_contact(j):
        for c in range(comps):
            for b in range(halves):
                at = slice(PAD, PAD + SROWS)
                x_ref[j + 1, c, b, at, :] = x_ref[j + 1, c, b, at, :] + contact_ref[j, c, b]

    def edges(mix):
        return 2.0 * (
            mix(lambda j: own_ref[j, 0]) * mix(lambda j: halo_ref[j, 0])
            + mix(lambda j: own_ref[j, 1]) * mix(lambda j: halo_ref[j, 2])
        )

    def newton(n, _):
        it = n * KRY

        gamma, delta = inner(0, sums=True)

        @pl.when(n == 0)
        def _():
            fill_slots(0, 0)
            find_gaps(0)
            push_forces(0, 0)
            take_row(0, 0, 0)
            take_strips(0, 0)


        @pl.when(n == 0)
        def _():
            pl.semaphore_wait(here, n_vol - 1)

        first_rows(0)
        send_field(1, it + 1, frecv[1].at[n])
        delta = delta + energy(lambda at: gap_ref[0, at, :]) - edges(lambda part: part(0))
        start_sums(it, gamma, delta, zero)

        @pl.when(n == 0)
        def _():
            take_row(0, 0, 1)

        @pl.when(n > 0)
        def _():
            take_row(KRY, KRY, 1)
            derive_halo(1)

        other_rows(0)
        send_row(1, it + 1, 1)
        pack_strips(1, it + 1, range(1, groups), lambda end: zero)
        receive_forces(0, n)
        add_contact(0)
        send_strips(1, it + 1)
        send_row(1, it + 1, 0)
        inner(1)
        fill_slots(1, n)
        find_gaps(1)
        push_forces(1, n)
        take_row(1, it + 1, 0)
        take_strips(1, it + 1)
        first_rows(1)
        send_field(2, it + 2, frecv[2].at[n])
        gamma0, pq0, _ = finish_sums(it)
        a0 = gamma0 / pq0
        w0 = full(a0)

        def dots1(c, b, padded, at):
            x1 = x_ref[1, c, b, padded, :]
            r = x_ref[0, c, b, padded, :] - w0 * x1
            r_ref[c, b, at, :] = r
            q = (l_ref[0, c, b, at, :] - w0 * l_ref[1, c, b, at, :]) + d_ref[c, b, at, :] * r
            return r * r, r * q, r * x1

        gamma, delta, cross = sum_tiles(dots1, 3)
        delta = delta + energy(lambda at: gap_ref[0, at, :] - w0 * gap_ref[1, at, :])
        delta = delta - edges(lambda part: part(0) - w0 * part(1))
        start_sums(it + 1, gamma, delta, cross)
        take_row(1, it + 1, 1)
        other_rows(1)
        send_row(2, it + 2, 1)
        pack_strips(2, it + 2, range(1, groups), lambda end: zero)
        receive_forces(1, n)
        add_contact(1)
        send_strips(2, it + 2)
        send_row(2, it + 2, 0)
        inner(2)
        fill_slots(2, n)
        find_gaps(2)

        @pl.when(n < NEWTON - 1)
        def _():
            push_forces(2, 0)

        gamma1, delta, cross = finish_sums(it + 1)
        beta1 = gamma1 / gamma0
        pq1 = delta + beta1 * (2.0 * cross + beta1 * pq0)
        a1 = gamma1 / pq1
        take_row(2, it + 2, 0)
        take_strips(2, it + 2)
        more, w1 = full(1.0 + beta1), full(a1)

        def second(x0, x1, x2):
            return (x0 - w0 * x1) - w1 * (more * x1 - w0 * x2)

        def dots2(c, b, padded, at):
            image = more * x_ref[1, c, b, padded, :] - w0 * x_ref[2, c, b, padded, :]
            r = r_ref[c, b, at, :] - w1 * image
            q = second(l_ref[0, c, b, at, :], l_ref[1, c, b, at, :], l_ref[2, c, b, at, :])
            q = q + d_ref[c, b, at, :] * r
            return r * r, r * q, r * image

        gamma, delta, cross = sum_tiles(dots2, 3)
        delta = delta + energy(lambda at: second(gap_ref[0, at, :], gap_ref[1, at, :], gap_ref[2, at, :]))
        delta = delta - edges(lambda part: second(part(0), part(1), part(2)))
        start_sums(it + 2, gamma, delta, cross)

        @pl.when(n == NEWTON - 1)
        def _():
            push_forces(2, NEWTON - 1)

        @pl.when(n < NEWTON - 1)
        def _():
            first_rows(2)
            send_field(KRY, KRY, frecv[0].at[1])

        take_row(2, it + 2, 1)

        @pl.when(n < NEWTON - 1)
        def _():
            other_rows(2)
            send_row(KRY, KRY, 1)
            pack_strips(KRY, KRY, range(1, groups), lambda end: zero)

        receive_forces(2, n)

        @pl.when(n < NEWTON - 1)
        def _():
            add_contact(2)
            send_strips(KRY, KRY)
            send_row(KRY, KRY, 0)

        gamma2, delta, cross = finish_sums(it + 2)
        beta2 = gamma2 / gamma1
        pq2 = delta + beta2 * (2.0 * cross + beta2 * pq1)
        a2 = gamma2 / pq2
        turned = beta2 * (1.0 + beta1)
        k0 = full(a0 + a1 * (1.0 + beta1) + a2 * (1.0 + turned))
        k1 = full(-(a1 * a0 + a2 * (a0 + a1 * (1.0 + beta1) + beta2 * a0)))
        k2 = full(a2 * a1 * a0)

        coef_ref[0], coef_ref[1], coef_ref[2] = k0, k1, k2

        @pl.when(n < NEWTON - 1)
        def _():
            derive_slots()
            find_gaps(0)
            push_forces(0, 1)

        def mix(fields):
            return k0 * fields(0) + k1 * fields(1) + k2 * fields(2)

        for c in range(comps):
            for b in range(halves):
                lu_ref[c, b, 0:SROWS, :] = lu_ref[c, b, 0:SROWS, :] + mix(lambda j: contact_ref[j, c, b])
        over, under, left, right = [mix(lambda j: halo_ref[j, i]) for i in range(4)]
        apply_row(lu_ref, 0, 0, over)
        apply_strips(lu_ref, 0, left, right, range(1))

        def finish(g, _):
            at = tile_rows(g)
            for b in range(halves):
                half = slice(b * BLK, (b + 1) * BLK)
                stiff, hard = stiff_ref[at, half], hard_ref[b, at, :]
                for c in range(comps):
                    u = u_ref[c, at, half] + mix(lambda j: x_ref[j, c, b, group_rows(g), :])
                    image = lu_ref[c, b, at, :] + mix(lambda j: l_ref[j, c, b, at, :])
                    bent = jnp.tanh(u / yield_scale)
                    material = stiff * (hard * u + (1.0 - hard) * yield_scale * bent)
                    residual = image + material - load_ref[c, at, half]
                    u_ref[c, at, half] = u
                    res_ref[c, at, half] = residual
                    lu_ref[c, b, at, :] = image
                    x_ref[0, c, b, group_rows(g), :] = -residual
                    d_ref[c, b, at, :] = stiff * (hard + (1.0 - hard) * (1.0 - bent * bent))
            return 0

        finish(0, 0)
        apply_row(lu_ref, 0, 1, under)
        apply_strips(lu_ref, 0, left, right, range(1, groups))
        lax.fori_loop(1, groups, finish, 0, unroll=3)

        @pl.when(n < NEWTON - 1)
        def _():
            for c in range(comps):
                for b in range(halves):
                    i = c * halves + b
                    own_ref[0, 0, i:i + 1, :] = x_ref[0, c, b, PAD:PAD + 1, :]
            own_ref[0, 1] = strip_of(x_ref.at[0], 0, range(groups), zero)
            take_row(KRY, KRY, 0)
            take_strips(KRY, KRY)
            await_bytes(crecv.at[STEPS], cr.at[STEPS])
            for i in (0, 2, 3):
                derive_halo(i)

        return 0

    def next_residual(loads, stiff, hard, first, second, third, last):
        k0, k1, k2 = [coef_ref[j] for j in range(KRY)]
        if len(first.shape) == 3:
            k0, k1, k2 = k0[0:4][None], k1[0:4][None], k2[0:4][None]
        u = k0 * first + k1 * second + k2 * third
        moved = k0 * (second - stiff * first) + k1 * (third - stiff * second) + k2 * last
        material = stiff * (hard * u + (1.0 - hard) * yield_scale * jnp.tanh(u / yield_scale))
        return loads - (moved + material)

    def derive_slots():
        await_bytes(fixed.at[0:(n_zone - 1) * CAP], fr.at[STEPS])
        await_bytes(frecv[0].at[1, 0:(n_zone - 1) * CAP], fr.at[KRY])
        stiff = jnp.broadcast_to(fixed[:, 0:1, :], fixed.shape)
        hard = jnp.broadcast_to(fixed[:, 1:2, :], fixed.shape)
        fields = [slot_ref[j] for j in range(KRY)]
        slot_ref[0] = next_residual(fields[0], stiff, hard, *fields, frecv[0][1] + bsend[KRY - 1])

    def derive_halo(i):
        if i < 2:
            await_bytes(rrecv.at[STEPS, i], rr.at[STEPS, i])
            packed = rrecv[STEPS, i]
            stiff, hard = [
                jnp.where(
                    sub < comps * halves,
                    jnp.where(lax.rem(sub, halves) == 0, packed[e:e + 1], packed[e + 1:e + 2]), 0.0,
                )
                for e in (0, halves)
            ]
        else:
            packed = crecv[STEPS, i - 2]
            parts = [
                jnp.where(lane < groups, packed, 0.0),
                jnp.where(lane < groups, pltpu.roll(packed, BLK - groups, axis=1), 0.0),
            ]
            stiff, hard = [
                part + pltpu.roll(part, groups, axis=1) + pltpu.roll(part, 2 * groups, axis=1) for part in parts
            ]
        fields = [halo_ref[j, i] for j in range(KRY + 1)]
        halo_ref[0, i] = next_residual(fields[0], stiff, hard, *fields)

    def send_fixed():
        def tile(c, b):
            if c == 0:
                return stiff_ref[0:SROWS, b * BLK:(b + 1) * BLK]
            return hard_ref[b, 0:SROWS, :] if c == 1 else zero

        send_surface(STEPS, tile, fixed)
        for end, at in ((0, 0), (1, height - 1)):
            for b in range(halves):
                rsend[STEPS, end, b:b + 1, :] = stiff_ref[at:at + 1, b * BLK:(b + 1) * BLK]
                rsend[STEPS, end, halves + b:halves + b + 1, :] = hard_ref[b, at:at + 1, :]
            ship_row(STEPS, end)
        for end, b, column in ((0, 0, 0), (1, halves - 1, BLK - 1)):
            strip = zero
            for g in range(groups):
                at = slice(g * 8, g * 8 + 8)
                for e, tile8 in ((0, stiff_ref[at, b * BLK:(b + 1) * BLK]), (groups, hard_ref[b, at, :])):
                    strip = jnp.where(
                        lane == e + g, jnp.broadcast_to(tile8[:, column:column + 1], (8, BLK)), strip
                    )
            csend[STEPS, end] = strip
        ship_strips(STEPS)

    own_ref[0, 0] = zero
    send_row(0, 0, 1)
    send_field(0, 0, frecv[0].at[0])
    pack_strips(0, 0, range(1, groups), lambda end: zero)
    send_strips(0, 0)
    send_row(0, 0, 0)
    set_up()
    send_fixed()
    lax.fori_loop(0, NEWTON, newton, 0)

    def drain(it, _):
        await_bytes(fsend.at[it, 0:n_zone - 1], fs.at[it])
        for end in range(2):
            await_bytes(rsend.at[it, end], rs.at[it, end])
        await_bytes(csend.at[it], cs.at[it])
        return 0

    def drain_sums(it, _):
        await_bytes(bsend.at[it, 0:(n_zone - 1) * CAP], bs.at[it])
        await_bytes(srecv.at[it, 0:devices - 1], ss.at[it])
        return 0

    lax.fori_loop(0, STEPS + 1, drain, 0)
    lax.fori_loop(0, STEPS, drain_sums, 0)


def local(n_vol, n_zone, load, support_stiffness, plastic_flags, owner_map, pattern, active, mortar):
    comps, height, breadth = load.shape
    halves = breadth // BLK
    rows = active.shape[2]
    field = pltpu.VMEM((comps, halves, height, BLK), F32)
    slots = n_zone * CAP
    landing = pltpu.VMEM((NEWTON, slots, 4, BLK), F32)
    blocks = SROWS * halves
    devices = n_vol * n_zone
    wide = -(-rows * NNZ * 12 // BLK) * BLK
    dma = pltpu.SemaphoreType.DMA
    vmem = pl.BlockSpec(memory_space=pltpu.VMEM)
    hbm = pl.BlockSpec(memory_space=pltpu.HBM)
    flags = plastic_flags.T
    links = jnp.transpose(pattern, (0, 3, 1, 2))
    operands = (load, support_stiffness, flags, owner_map, links, active, mortar)
    return pl.pallas_call(
        functools.partial(kernel, n_vol, n_zone),
        out_shape=[jax.ShapeDtypeStruct(load.shape, F32)] * 2,
        in_specs=[hbm] * 7,
        out_specs=[vmem, vmem],
        scratch_shapes=[
            pltpu.VMEM(load.shape, F32),
            pltpu.VMEM(support_stiffness.shape, F32),
            pltpu.VMEM(flags.shape, jnp.int32),
            pltpu.SMEM(owner_map.shape, jnp.int32),
            pltpu.SMEM(links.shape, jnp.int32),
            pltpu.SMEM(active.shape, jnp.int32),
            pltpu.VMEM(mortar.shape[2:], F32),
            pltpu.VMEM((KRY + 1, comps, halves, height + 2 * PAD, BLK), F32),
            pltpu.VMEM((KRY, comps, halves, height, BLK), F32),
            field, field, field,
            pltpu.VMEM((halves, height, BLK), F32),
            pltpu.VMEM((KRY, comps, halves, SROWS, BLK), F32),
            pltpu.VMEM((KRY + 1, 4, 8, BLK), F32),
            pltpu.VMEM((KRY + 1, 2, 8, BLK), F32),
            pltpu.VMEM((KRY, slots, 4, BLK), F32),
            pltpu.VMEM((KRY, 8, BLK), F32),
            pltpu.VMEM((KRY, rows * 8, BLK), F32),
            pltpu.VMEM((rows * 8, BLK), F32),
            pltpu.VMEM((rows, 2 * BLK, NNZ * BLK), BF16),
            pltpu.VMEM((slots * 4, wide), BF16),
            pltpu.VMEM((wide, BLK), F32),
            pltpu.VMEM((blocks * 8, BLK), F32),
            pltpu.VMEM((blocks + 1, 8, BLK), F32),
            pltpu.VMEM((blocks * 8, BLK), F32),
            pltpu.SMEM((slots,), jnp.int32),
            pltpu.SMEM((blocks,), jnp.int32),
            pltpu.VMEM((STEPS + 1, n_zone, CAP, 4, BLK), F32),
            landing, landing, landing,
            pltpu.VMEM((slots, 4, BLK), F32),
            pltpu.VMEM((STEPS, slots, 4, BLK), F32),
            landing, landing, landing,
            pltpu.VMEM((STEPS + 1, 2, 8, BLK), F32),
            pltpu.VMEM((STEPS + 1, 2, 8, BLK), F32),
            pltpu.VMEM((STEPS + 1, 2, 8, BLK), F32),
            pltpu.VMEM((STEPS + 1, 2, 8, BLK), F32),
            pltpu.VMEM((STEPS, 1, BLK), F32),
            pltpu.VMEM((STEPS, devices, 1, BLK), F32),
            pltpu.SemaphoreType.REGULAR,
            dma((7,)),
        ] + [dma((STEPS + 1,))] * 4 + [dma((STEPS + 1, 2))] * 2 + [dma((STEPS + 1,))] * 4,
        compiler_params=pltpu.CompilerParams(
            collective_id=0, has_side_effects=True, vmem_limit_bytes=32 * 1024 * 1024
        ),
    )(*[pltpu.with_memory_space_constraint(a, pltpu.HBM) for a in operands])


def solution(mesh):
    in_specs = (
        P(None, "vol", "zone"),
        P("vol", "zone"),
        P("vol", "zone"),
        P("vol", "zone", None),
        P("vol", "zone", None, None),
        P("vol", "zone", None),
        P("vol", "zone", None, None, None, None),
    )
    out_specs = (P(None, "vol", "zone"), P(None, "vol", "zone"))
    body = functools.partial(local, mesh.shape["vol"], mesh.shape["zone"])
    return jax.shard_map(body, mesh=mesh, in_specs=in_specs, out_specs=out_specs, check_vma=False)
```
